32 devices in a mesh: seq: 32 (over z, y, x, core).
Axes of the slice: x: 2, y: 2, z: 4, core: 2. Of those that a mesh axis runs over, the one named last changes fastest.
Arguments:
- tokens: bfloat16 [4096, 1024], P('seq'), may hold values from -6 to 6
- scene_lengths: int32 [8], replicated, may hold values from 1 to 1024, 4096 in all
- cotangent: bfloat16 [4096, 1024], P('seq'), may hold values from -6 to 6
- attend_weight: float32 [1024, 3072], P('seq'), may hold values from -0.09375 to 0.09375
- output_weight: float32 [1024, 1024], P('seq'), may hold values from -2 to 2
- expand_weight: float32 [1024, 4096], P('seq'), may hold values from -0.1875 to 0.1875
- reduce_weight: float32 [4096, 1024], P('seq'), may hold values from -0.09375 to 0.09375
- vector_params: float32 [9, 1024], P(None, 'seq'), may hold values from -1.2 to 7.2, as said below
- attend_momentum: float32 [1024, 3072], P('seq'), may hold values from -0.0048828125 to 0.0048828125
- output_momentum: float32 [1024, 1024], P('seq'), may hold values from -0.0048828125 to 0.0048828125
- expand_momentum: float32 [1024, 4096], P('seq'), may hold values from -0.0048828125 to 0.0048828125
- reduce_momentum: float32 [4096, 1024], P('seq'), may hold values from -0.0048828125 to 0.0048828125
- vector_momentum: float32 [9, 1024], P(None, 'seq'), may hold values from -0.0048828125 to 0.0048828125
- attend_average: float32 [1024, 3072], P('seq'), may hold values from -0.09375 to 0.09375
- output_average: float32 [1024, 1024], P('seq'), may hold values from -2 to 2
- expand_average: float32 [1024, 4096], P('seq'), may hold values from -0.1875 to 0.1875
- reduce_average: float32 [4096, 1024], P('seq'), may hold values from -0.09375 to 0.09375
- vector_average: float32 [9, 1024], P(None, 'seq'), may hold values from 0.1 to 1.9
Outputs:
- block_output: bfloat16 [4096, 1024], P('seq')
- input_gradient: bfloat16 [4096, 1024], P('seq')
- gradient_norm: float32 [], replicated
- attend_velocity: float32 [1024, 3072], P('seq')
- attend_updated: float32 [1024, 3072], P('seq')
- attend_smoothed: float32 [1024, 3072], P('seq')
- output_velocity: float32 [1024, 1024], P('seq')
- output_updated: float32 [1024, 1024], P('seq')
- output_smoothed: float32 [1024, 1024], P('seq')
- expand_velocity: float32 [1024, 4096], P('seq')
- expand_updated: float32 [1024, 4096], P('seq')
- expand_smoothed: float32 [1024, 4096], P('seq')
- reduce_velocity: float32 [4096, 1024], P('seq')
- reduce_updated: float32 [4096, 1024], P('seq')
- reduce_smoothed: float32 [4096, 1024], P('seq')
- vector_velocity: float32 [9, 1024], P(None, 'seq')
- vector_updated: float32 [9, 1024], P(None, 'seq')
- vector_smoothed: float32 [9, 1024], P(None, 'seq')
The draws below stay inside these ranges and needn't reach their ends.
Inputs may be any that keep to these rules, and one draw needn't show every extreme that they name: `scene_lengths`: the lengths sum to 4096; no scene holds more than 1024 tokens. `vector_params`: rows 0 and 2 are positive.
All inputs are finite; a program needn't handle non-finite values.
Results may differ from the reference program's by a relative error of at most 0.015.
The reference program's roundings to bfloat16 on the way count: a program that leaves them out, or rounds other values in their place, can miss the bound.
Values may be sent and summed in bfloat16 or wider, within the bound.
No kernel may reach another device: no remote copies, remote signals or barrier semaphores. Data moves between devices by JAX's collectives and lax.ppermute only.
A program may use at most 256 MiB of HBM per device.

```python
import math
import jax
import jax.numpy as jnp
import numpy as np
from jax import lax

D = 1024
FF = 4096
HEADS = 16
TOK_DEV = 128
SPAN = 8
SCENES = 8
STEP = 10
VEC_ROWS = 9
TOKENS = 4096
N_SEQ = 32


def draw_vector_params(key, part):
    key = jax.random.fold_in(key, 7)
    keys_split = jax.random.split(key, 2)
    places = jnp.arange(D, dtype=jnp.float32) / (D - 1)
    bias_rows = 5 + FF // D - 2
    top_gain = 3.0
    biases = jnp.clip(0.3 * jax.random.normal(keys_split[1], (bias_rows, D), jnp.float32), -1.2, 1.2)
    rough = jnp.exp(jax.random.uniform(keys_split[0], (2, D), jnp.float32, -0.35, 0.35))
    gains = (1.0 + (top_gain - 1.0) * places)[None, :] * rough
    return jnp.concatenate([gains[0:1], biases[0:1], gains[1:2], biases[1:]], axis=0)


def shard_levels(rng, extent, cuts, least, largest):
    def one(position, blocks):
        heights = jax.random.uniform(jax.random.fold_in(jax.random.fold_in(rng, 6), position), (blocks,), jnp.float32, least / len(cuts), largest / len(cuts))
        return jnp.repeat(jnp.exp(heights), extent[position] // blocks).reshape((-1,) + (1,) * (len(extent) - position - 1))

    level = one(*cuts[0])
    for cut in cuts[1:]:
        level = level * one(*cut)
    return level


def split_up(count, total, limit, slope):
    loads = [(1 << 20) // math.isqrt(rank ** slope) + 1 for rank in range(2, count + 1)]
    surplus, counts = total - limit - (count - 1), [1] * (count - 1)
    while surplus > 0:
        candidates = [i for i in range(count - 1) if counts[i] < limit]
        pool, budget = sum([loads[i] for i in candidates]), surplus
        for i in candidates:
            extra = min(limit - counts[i], max(1, budget * loads[i] // pool), surplus)
            counts[i] = counts[i] + extra
            surplus = surplus - extra
    return np.array([limit] + counts)


def uneven_parts(own_key, number_of, total, reach, skew):
    if number_of == 2:
        one = jax.random.randint(own_key, (), max(1, total - reach), min(reach, total - 1) + 1)
        return jnp.stack([one, total - one])
    tallies = jnp.asarray(split_up(number_of, total, reach, skew), jnp.int32)
    couples = (number_of - 1) // 2
    source_of, sink = tallies[1:1 + 2 * couples:2], tallies[2:2 + 2 * couples:2]
    room = jnp.minimum(source_of - 1, reach - sink)
    passed = jax.random.randint(jax.random.fold_in(own_key, 1), (couples,), 0, 1 << 20) % (room + 1)
    tallies = tallies.at[1:1 + 2 * couples:2].set(source_of - passed).at[2:2 + 2 * couples:2].set(sink + passed)
    return tallies[jax.random.permutation(jax.random.fold_in(own_key, 2), number_of)]


def scatter_about(own_key, extent, deviation, limit, pieces=(), kind=jnp.bfloat16):
    entries = deviation * jax.random.normal(own_key, extent, jnp.float32)
    if pieces:
        entries = entries * shard_levels(own_key, extent, pieces, -0.22, 0.18)
    return jnp.clip(entries, -limit, limit).astype(kind)


def setup_inputs(seed: int = 0) -> dict:
    splits = jax.random.split(jax.random.key(seed), 19)
    return {
        "tokens": scatter_about(splits[0], (TOKENS, D), 1.0, 6.0, ((0, 32),)),
        "scene_lengths": uneven_parts(splits[1], SCENES, TOKENS, SPAN * TOK_DEV, 1).astype(jnp.int32),
        "cotangent": scatter_about(splits[2], (TOKENS, D), 1.0, 6.0, ((0, 32),)),
        "attend_weight": scatter_about(splits[3], (D, 3 * D), (4 * D) ** -0.5, 0.09375, ((0, 32),), jnp.float32),
        "output_weight": scatter_about(splits[4], (D, D), (max(4, D // 128)) ** -0.5, 2.0, ((0, 32),), jnp.float32),
        "expand_weight": scatter_about(splits[5], (D, FF), D ** -0.5, 0.1875, ((0, 32),), jnp.float32),
        "reduce_weight": scatter_about(splits[6], (FF, D), FF ** -0.5, 0.09375, ((0, 32),), jnp.float32),
        "vector_params": draw_vector_params(jax.random.fold_in(splits[18], 71), 0),
        "attend_momentum": scatter_about(splits[8], (D, 3 * D), (1.1 / (4 * D * D + 2 * D * FF + VEC_ROWS * D) ** 0.5), 0.0048828125, ((0, 32),), jnp.float32),
        "output_momentum": scatter_about(splits[9], (D, D), (1.1 / (4 * D * D + 2 * D * FF + VEC_ROWS * D) ** 0.5), 0.0048828125, ((0, 32),), jnp.float32),
        "expand_momentum": scatter_about(splits[10], (D, FF), (1.1 / (4 * D * D + 2 * D * FF + VEC_ROWS * D) ** 0.5), 0.0048828125, ((0, 32),), jnp.float32),
        "reduce_momentum": scatter_about(splits[11], (FF, D), (1.1 / (4 * D * D + 2 * D * FF + VEC_ROWS * D) ** 0.5), 0.0048828125, ((0, 32),), jnp.float32),
        "vector_momentum": scatter_about(splits[12], (VEC_ROWS, D), (1.1 / (4 * D * D + 2 * D * FF + VEC_ROWS * D) ** 0.5), 0.0048828125, ((1, 32),), jnp.float32),
        "attend_average": scatter_about(splits[13], (D, 3 * D), (4 * D) ** -0.5, 0.09375, ((0, 32),), jnp.float32),
        "output_average": scatter_about(splits[14], (D, D), (max(4, D // 128)) ** -0.5, 2.0, ((0, 32),), jnp.float32),
        "expand_average": scatter_about(splits[15], (D, FF), D ** -0.5, 0.1875, ((0, 32),), jnp.float32),
        "reduce_average": scatter_about(splits[16], (FF, D), FF ** -0.5, 0.09375, ((0, 32),), jnp.float32),
        "vector_average": jnp.clip(1.0 + 0.18 * jax.random.normal(splits[17], (VEC_ROWS, D), jnp.float32), 0.1, 1.9),
    }


@jax.custom_vjp
def low(v):
    return lax.optimization_barrier(v.astype(jnp.bfloat16)).astype(jnp.float32)

@jax.custom_vjp
def low_back(v):
    return v

def low_keep(v):
    return (low(v), None)

def low_pass(kept, grad):
    return (grad,)

def back_keep(v):
    return (v, None)

def back_low(kept, grad):
    return (low(grad),)
low.defvjp(low_keep, low_pass)
low_back.defvjp(back_keep, back_low)
PRECISE = lax.Precision.HIGHEST
EPSILON = 1e-05
MOMENTUM = 0.9
LEARNING_RATES = (60.0, 480.0, 60.0, 60.0, 600.0)
WEIGHT_DECAY = 0.0001
CLIP_NORM = 1.0
MASK_FLOOR = -1e+30

def layer_norm(values, scales, shifts):
    centre = values - lax.optimization_barrier(jnp.mean(values, axis=-1, keepdims=True))
    spread = lax.optimization_barrier(jnp.mean(centre * centre, axis=-1, keepdims=True))
    return centre * lax.rsqrt(spread + EPSILON) * scales + shifts

def scene_labels(lengths, count):
    finish = jnp.cumsum(lengths).astype(jnp.int32)
    places = jnp.arange(count, dtype=jnp.int32)
    return lax.optimization_barrier(jnp.sum((places[:, None] >= finish[None, :]).astype(jnp.int32), axis=1))

def attention(joined, labels):
    count, triple = joined.shape
    columns = triple // 3
    head_size = columns // HEADS
    window = (2 * SPAN + 1) * TOK_DEV
    margin = SPAN * TOK_DEV
    queries_all = joined[:, :columns]
    padded = jnp.pad(joined[:, columns:], ((margin, margin), (0, 0)))
    padded_labels = jnp.pad(labels, (margin, margin), constant_values=-1).astype(jnp.int32)

    def one_block(block_index):
        first_row = (block_index * TOK_DEV).astype(jnp.int32)
        queries = lax.dynamic_slice_in_dim(queries_all, first_row, TOK_DEV, 0).reshape(TOK_DEV, HEADS, head_size)
        pair_rows = lax.dynamic_slice_in_dim(padded, first_row, window, 0)
        keyset = pair_rows[:, :columns].reshape(window, HEADS, head_size)
        valueset = pair_rows[:, columns:].reshape(window, HEADS, head_size)
        query_labels = lax.dynamic_slice_in_dim(labels, first_row, TOK_DEV, 0)
        key_labels = lax.dynamic_slice_in_dim(padded_labels, first_row, window, 0)
        allowed = query_labels[:, None] == key_labels[None, :]
        scores = jnp.einsum('qhd,khd->hqk', queries, keyset, precision=PRECISE) * head_size ** (-0.5)
        scores = low_back(scores)
        masked = jnp.where(allowed[None], scores, MASK_FLOOR)
        row_peak = lax.optimization_barrier(jnp.max(masked, axis=-1, keepdims=True))
        raised = jnp.exp(masked - row_peak)
        shares = raised / lax.optimization_barrier(jnp.sum(raised, axis=-1, keepdims=True))
        mixed = jnp.einsum('hqk,khd->qhd', low(shares), valueset, precision=PRECISE)
        return mixed.reshape(TOK_DEV, columns)
    mixed_all = lax.map(jax.checkpoint(one_block), jnp.arange(N_SEQ, dtype=jnp.int32))
    return mixed_all.reshape(count, columns)

def reference(tokens, scene_lengths, cotangent, attend_weight, output_weight, expand_weight, reduce_weight, vector_params, attend_momentum, output_momentum, expand_momentum, reduce_momentum, vector_momentum, attend_average, output_average, expand_average, reduce_average, vector_average):
    rows_all = tokens.astype(jnp.float32)
    labels = scene_labels(scene_lengths.astype(jnp.int32), N_SEQ * TOK_DEV)

    def forward(rows_in, attend, output, expand, shrink, vectors):
        attend, output, expand, shrink, vectors = (low(attend), low(output), low(expand), low(shrink), low(vectors))
        first = layer_norm(rows_in, vectors[0], vectors[1])
        joined = low_back(low(jnp.dot(low(first), attend, precision=PRECISE)))
        mixed_heads = low_back(low(attention(joined, labels)))
        second = rows_in + low_back(jnp.dot(mixed_heads, output, precision=PRECISE))
        normed = layer_norm(second, vectors[2], vectors[3])
        upper_part = low_back(jnp.dot(low(normed), expand, precision=PRECISE) + vectors[5:].reshape(-1))
        active = jax.nn.gelu(upper_part, approximate=False)
        return second + low_back(jnp.dot(low(active), shrink, precision=PRECISE) + vectors[4])
    result, backward = jax.vjp(forward, rows_all, attend_weight, output_weight, expand_weight, reduce_weight, vector_params)
    gradients = backward(cotangent.astype(jnp.float32))
    block_output = result.astype(jnp.bfloat16)
    input_gradient = gradients[0].astype(jnp.bfloat16)
    square_total = jnp.zeros((), jnp.float32)
    for gradient_now in gradients[1:]:
        square_total = square_total + jnp.sum(gradient_now * gradient_now)
    gradient_norm = jnp.sqrt(square_total)
    factor = jnp.minimum(1.0, CLIP_NORM / (gradient_norm + 1e-06))
    smooth_rate = min(0.999, (1.0 + STEP) / (10.0 + STEP))

    def update(weight_now, moment_now, average_now, gradient_now, rate_now):
        clipped = factor * gradient_now + WEIGHT_DECAY * weight_now
        velocity = MOMENTUM * moment_now + clipped
        updated = weight_now - rate_now * (clipped + MOMENTUM * velocity)
        smoothed = smooth_rate * average_now + (1.0 - smooth_rate) * updated
        return (velocity, updated, smoothed)
    attend_new = update(attend_weight, attend_momentum, attend_average, gradients[1], LEARNING_RATES[0])
    output_new = update(output_weight, output_momentum, output_average, gradients[2], LEARNING_RATES[1])
    expand_new = update(expand_weight, expand_momentum, expand_average, gradients[3], LEARNING_RATES[2])
    reduce_new = update(reduce_weight, reduce_momentum, reduce_average, gradients[4], LEARNING_RATES[3])
    vector_new = update(vector_params, vector_momentum, vector_average, gradients[5], LEARNING_RATES[4])
    return (block_output, input_gradient, gradient_norm, attend_new[0], attend_new[1], attend_new[2], output_new[0], output_new[1], output_new[2], expand_new[0], expand_new[1], expand_new[2], reduce_new[0], reduce_new[1], reduce_new[2], vector_new[0], vector_new[1], vector_new[2])
```

```python
import functools

import jax
import jax.numpy as jnp
from jax import lax
from jax.experimental import pallas as pl
from jax.experimental.pallas import tpu as pltpu
from jax.sharding import PartitionSpec as P

HEADS = 16
STEP = 10
EPSILON = 1e-05
MOMENTUM = 0.9
LEARNING_RATES = (60.0, 480.0, 60.0, 60.0, 600.0)
WEIGHT_DECAY = 0.0001
CLIP_NORM = 1.0
MASK_FLOOR = -1e30
PLANE = 8
QUERY_TILE = 256
KEY_TILE = 256
F32 = jnp.float32
LOW = jnp.bfloat16


def swap(block, bit):
    n = lax.axis_size("seq")
    return lax.ppermute(block, "seq", [(i, i ^ bit) for i in range(n)])


def move(block, distance):
    n = lax.axis_size("seq")
    return lax.ppermute(
        block, "seq", [(i, i + distance) for i in range(n) if 0 <= i + distance < n]
    )


def plane_groups():
    n = lax.axis_size("seq")
    return [[g * PLANE + j for j in range(PLANE)] for g in range(n // PLANE)]


def cross_groups():
    n = lax.axis_size("seq")
    return [[g * PLANE + j for g in range(n // PLANE)] for j in range(PLANE)]


def exchange(blocks, groups=None):
    return lax.all_to_all(blocks, "seq", 0, 0, axis_index_groups=groups)


def spread(block):
    half = block.shape[0] // 2
    across = swap(block, 2)
    along = swap(block, 4)
    corner = jnp.concatenate([swap(across[:half], 4), swap(along[half:], 2)], axis=0)
    mine = jnp.stack([block, across, along, corner])
    return jnp.stack([mine, swap(mine, 1)])


def collect(parts):
    half = parts.shape[2] // 2
    pair = parts[0] + swap(parts[1].astype(LOW), 1).astype(F32)
    corner = pair[3].astype(LOW)
    by_across = swap(corner[:half], 2).astype(F32)
    by_along = swap(corner[half:], 4).astype(F32)
    across = jnp.concatenate([pair[1][:half], pair[1][half:] + by_along], axis=0).astype(LOW)
    along = jnp.concatenate([pair[2][:half] + by_across, pair[2][half:]], axis=0).astype(LOW)
    return pair[0] + swap(across, 2).astype(F32) + swap(along, 4).astype(F32)


def norm_parts(values):
    centre = values - jnp.mean(values, axis=-1, keepdims=True)
    spread_of = jnp.mean(centre * centre, axis=-1, keepdims=True)
    inverse = lax.rsqrt(spread_of + EPSILON)
    return centre * inverse, inverse


def norm_back(unit, inverse, gain, incoming):
    scaled = incoming * gain
    return inverse * (
        scaled
        - jnp.mean(scaled, axis=-1, keepdims=True)
        - unit * jnp.mean(scaled * unit, axis=-1, keepdims=True)
    )


def dot(a, b, dims=((1,), (0,))):
    return lax.dot_general(a, b, (dims, ((), ())), preferred_element_type=F32)


def project_kernel(order_ref, tokens_ref, gain_ref, shift_ref, weight_ref, first_ref, joined_ref):
    unit, _ = norm_parts(tokens_ref[0].astype(F32))
    first = (unit * gain_ref[...] + shift_ref[...]).astype(LOW)
    first_ref[0] = first
    joined_ref[0] = dot(first, weight_ref[...]).astype(LOW)


def project(place, tokens, gain, shift, weight):
    blocks, number, columns = tokens.shape
    wide = weight.shape[1]
    return pl.pallas_call(
        project_kernel,
        grid_spec=pltpu.PrefetchScalarGridSpec(
            num_scalar_prefetch=1,
            grid=(blocks,),
            in_specs=[
                pl.BlockSpec((1, number, columns), lambda i, s: (i, 0, 0)),
                pl.BlockSpec((1, columns), lambda i, s: (0, 0)),
                pl.BlockSpec((1, columns), lambda i, s: (0, 0)),
                pl.BlockSpec((columns, wide), lambda i, s: (0, 0)),
            ],
            out_specs=[
                pl.BlockSpec((1, number, columns), lambda i, s: (s[i], 0, 0)),
                pl.BlockSpec((1, number, wide), lambda i, s: (s[i], 0, 0)),
            ],
        ),
        out_shape=[
            jax.ShapeDtypeStruct((blocks, number, columns), LOW),
            jax.ShapeDtypeStruct((blocks, number, wide), LOW),
        ],
        cost_estimate=pl.CostEstimate(
            flops=2 * blocks * number * columns * wide, bytes_accessed=2 * tokens.size * 3, transcendentals=0
        ),
        compiler_params=pltpu.CompilerParams(vmem_limit_bytes=40 << 20),
    )(place, tokens, gain, shift, weight)


def head_mask(shape, head):
    return lax.broadcasted_iota(jnp.int32, shape, len(shape) - 1) // 64 == head


def attend_kernel(
    range_ref, query_ref, before_ref, own_ref, after_ref, span_ref, mixed_ref, log_ref, keys, values
):
    step = pl.program_id(0)
    tokens = own_ref.shape[0]
    wide = query_ref.shape[1]

    @pl.when(step == 0)
    def _():
        for place, ref in enumerate((before_ref, own_ref, after_ref)):
            keys[pl.ds(place * tokens, tokens), :] = ref[:, :wide]
            values[:, pl.ds(place * tokens, tokens)] = ref[:, wide:].T

    queries = query_ref[...] * jnp.asarray(0.125, LOW)
    begin = span_ref[0:1, :]
    end = span_ref[1:2, :]
    here = query_ref.shape[0]
    split = [jnp.where(head_mask(queries.shape, h), queries, jnp.zeros_like(queries)) for h in range(2)]

    def body(index, carry):
        start = pl.multiple_of(index * KEY_TILE, KEY_TILE)
        block = keys[pl.ds(start, KEY_TILE), :]
        place = start + lax.broadcasted_iota(jnp.int32, (KEY_TILE, here), 0)
        allowed = (place >= begin) & (place < end)
        out = []
        for h in range(2):
            peak, total, mixed = carry[h]
            scores = jnp.where(allowed, dot(block, split[h], ((1,), (1,))), MASK_FLOOR)
            raised_peak = jnp.maximum(peak, jnp.max(scores, axis=0, keepdims=True))
            raised = jnp.exp(scores - raised_peak)
            fade = jnp.exp(peak - raised_peak)
            total = total * fade + jnp.sum(raised, axis=0, keepdims=True)
            turned = values[64 * h : 64 * h + 64, pl.ds(start, KEY_TILE)]
            mixed = mixed * fade + dot(turned, raised.astype(LOW))
            out.append((raised_peak, total, mixed))
        return tuple(out)

    init = tuple(
        (jnp.full((1, here), MASK_FLOOR, F32), jnp.zeros((1, here), F32), jnp.zeros((64, here), F32))
        for _ in range(2)
    )
    done = lax.fori_loop(range_ref[0, step], range_ref[1, step], body, init)
    mixed_ref[...] = jnp.concatenate([m / t for _, t, m in done], axis=0).T
    log_ref[...] = jnp.concatenate([k + jnp.log(t) for k, t, _ in done], axis=0)


def attend_back_kernel(
    range_ref,
    query_ref,
    before_ref,
    own_ref,
    after_ref,
    span_ref,
    mixed_ref,
    log_ref,
    grad_ref,
    query_grad_ref,
    before_grad_ref,
    own_grad_ref,
    after_grad_ref,
    keys,
    values,
    turned_keys,
    key_grad,
    value_grad,
):
    step = pl.program_id(0)
    tokens = own_ref.shape[0]
    wide = query_ref.shape[1]

    @pl.when(step == 0)
    def _():
        for place, ref in enumerate((before_ref, own_ref, after_ref)):
            keys[pl.ds(place * tokens, tokens), :] = ref[:, :wide]
            values[pl.ds(place * tokens, tokens), :] = ref[:, wide:]
            turned_keys[:, pl.ds(place * tokens, tokens)] = ref[:, :wide].T
        key_grad[...] = jnp.zeros_like(key_grad)
        value_grad[...] = jnp.zeros_like(value_grad)

    queries = query_ref[...] * jnp.asarray(0.125, LOW)
    grads = grad_ref[...]
    here = queries.shape[0]
    zero = jnp.zeros_like(queries)
    split = [jnp.where(head_mask(queries.shape, h), queries, zero) for h in range(2)]
    split_grads = [jnp.where(head_mask(queries.shape, h), grads, zero) for h in range(2)]
    product = (grads.astype(F32) * mixed_ref[...]).T
    centred = [jnp.sum(product[64 * h : 64 * h + 64], axis=0, keepdims=True) for h in range(2)]
    begin = span_ref[0:1, :]
    end = span_ref[1:2, :]

    def body(index, carry):
        start = pl.multiple_of(index * KEY_TILE, KEY_TILE)
        rows = pl.ds(start, KEY_TILE)
        place = start + lax.broadcasted_iota(jnp.int32, (KEY_TILE, here), 0)
        allowed = (place >= begin) & (place < end)
        out, key_part, value_part = [], 0, 0
        for h in range(2):
            scores = dot(keys[rows, :], split[h], ((1,), (1,)))
            shares = jnp.exp(jnp.where(allowed, scores - log_ref[h : h + 1, :], MASK_FLOOR))
            value_part += dot(shares.astype(LOW), split_grads[h])
            share_grad = dot(values[rows, :], split_grads[h], ((1,), (1,)))
            score_grad = (shares * (share_grad - centred[h])).astype(LOW)
            key_part += dot(score_grad, split[h])
            out.append(carry[h] + dot(turned_keys[64 * h : 64 * h + 64, rows], score_grad))
        key_grad[rows, :] += key_part
        value_grad[rows, :] += value_part
        return tuple(out)

    init = tuple(jnp.zeros((64, here), F32) for _ in range(2))
    done = lax.fori_loop(range_ref[0, step], range_ref[1, step], body, init)
    query_grad_ref[...] = (jnp.concatenate(done, axis=0).T * 0.125).astype(LOW)

    @pl.when(step == pl.num_programs(0) - 1)
    def _():
        for place, ref in enumerate((before_grad_ref, own_grad_ref, after_grad_ref)):
            ref[:, :wide] = key_grad[pl.ds(place * tokens, tokens), :].astype(ref.dtype)
            ref[:, wide:] = value_grad[pl.ds(place * tokens, tokens), :].astype(ref.dtype)


def attention(ranges, queries, before, own, after, spans):
    tokens, wide = queries.shape
    whole = lambda shape: pl.BlockSpec(shape, lambda i, s: (0, 0))
    tile = pl.BlockSpec((QUERY_TILE, wide), lambda i, s: (i, 0))
    row = pl.BlockSpec((2, QUERY_TILE), lambda i, s: (0, i))
    return pl.pallas_call(
        attend_kernel,
        grid_spec=pltpu.PrefetchScalarGridSpec(
            num_scalar_prefetch=1,
            grid=(tokens // QUERY_TILE,),
            in_specs=[tile] + [whole((tokens, 2 * wide))] * 3 + [row],
            out_specs=[tile, row],
            scratch_shapes=[
                pltpu.VMEM((3 * tokens, wide), LOW),
                pltpu.VMEM((wide, 3 * tokens), LOW),
            ],
        ),
        out_shape=[
            jax.ShapeDtypeStruct((tokens, wide), F32),
            jax.ShapeDtypeStruct((2, tokens), F32),
        ],
        cost_estimate=pl.CostEstimate(
            flops=4 * tokens * tokens * wide * 2, bytes_accessed=16 * tokens * wide, transcendentals=2 * tokens * tokens
        ),
        compiler_params=pltpu.CompilerParams(vmem_limit_bytes=40 << 20),
    )(ranges, queries, before, own, after, spans)


def attention_back(ranges, queries, before, own, after, spans, mixed, logs, grads):
    tokens, wide = queries.shape
    whole = lambda shape: pl.BlockSpec(shape, lambda i, s: (0, 0))
    tile = pl.BlockSpec((QUERY_TILE, wide), lambda i, s: (i, 0))
    row = pl.BlockSpec((2, QUERY_TILE), lambda i, s: (0, i))
    return pl.pallas_call(
        attend_back_kernel,
        grid_spec=pltpu.PrefetchScalarGridSpec(
            num_scalar_prefetch=1,
            grid=(tokens // QUERY_TILE,),
            in_specs=[tile] + [whole((tokens, 2 * wide))] * 3 + [row, tile, row, tile],
            out_specs=[tile] + [whole((tokens, 2 * wide))] * 3,
            scratch_shapes=[
                pltpu.VMEM((3 * tokens, wide), LOW),
                pltpu.VMEM((3 * tokens, wide), LOW),
                pltpu.VMEM((wide, 3 * tokens), LOW),
                pltpu.VMEM((3 * tokens, wide), F32),
                pltpu.VMEM((3 * tokens, wide), F32),
            ],
        ),
        out_shape=[
            jax.ShapeDtypeStruct((tokens, wide), LOW),
            jax.ShapeDtypeStruct((tokens, 2 * wide), LOW),
            jax.ShapeDtypeStruct((tokens, 2 * wide), F32),
            jax.ShapeDtypeStruct((tokens, 2 * wide), LOW),
        ],
        cost_estimate=pl.CostEstimate(
            flops=10 * tokens * tokens * wide * 2, bytes_accessed=32 * tokens * wide, transcendentals=2 * tokens * tokens
        ),
        compiler_params=pltpu.CompilerParams(vmem_limit_bytes=48 << 20),
    )(ranges, queries, before, own, after, spans, mixed, logs, grads)


def on_device(
    tokens,
    scene_lengths,
    cotangent,
    attend_weight,
    output_weight,
    expand_weight,
    reduce_weight,
    vector_params,
    attend_momentum,
    output_momentum,
    expand_momentum,
    reduce_momentum,
    vector_momentum,
    attend_average,
    output_average,
    expand_average,
    reduce_average,
    vector_average,
):
    n = lax.axis_size("seq")
    planes = n // PLANE
    device = lax.axis_index("seq")
    plane, spot = device // PLANE, device % PLANE
    number, columns = tokens.shape
    shared = number * PLANE
    rows = columns // n
    hidden = reduce_weight.shape[0]
    wide = columns // PLANE

    vectors = exchange(jnp.broadcast_to(vector_params.astype(LOW)[None], (n,) + vector_params.shape))
    vectors = jnp.moveaxis(vectors, 0, 1).reshape(-1, columns).astype(F32)
    bias_up = lax.dynamic_index_in_dim(
        vectors[5:].reshape(planes, PLANE, hidden), spot, axis=1, keepdims=False
    ).reshape(1, planes * hidden)

    attend = (
        attend_weight.astype(LOW).reshape(rows, 3, PLANE, wide).transpose(2, 0, 1, 3).reshape(PLANE, rows, 3 * wide)
    )
    attend = exchange(jnp.broadcast_to(attend[None], (planes,) + attend.shape).reshape(n, rows, 3 * wide))
    attend = attend.reshape(columns, 3 * wide)
    expand = (
        expand_weight.astype(LOW)
        .reshape(rows, planes, PLANE, hidden)
        .transpose(2, 0, 1, 3)
        .reshape(PLANE, rows, planes * hidden)
    )
    expand = exchange(jnp.broadcast_to(expand[None], (planes,) + expand.shape).reshape(n, rows, -1))
    expand = expand.reshape(columns, planes * hidden)
    shrink = exchange(
        jnp.broadcast_to(reduce_weight.astype(LOW)[None], (planes,) + reduce_weight.shape), cross_groups()
    ).reshape(planes * hidden, columns)
    output = exchange(
        jnp.broadcast_to(output_weight.astype(LOW)[None], (planes,) + output_weight.shape), cross_groups()
    )
    output = exchange(jnp.broadcast_to(output[None], (PLANE,) + output.shape), plane_groups())
    output = output.transpose(1, 0, 2, 3).reshape(columns, columns)

    order = spot ^ jnp.array([2 * m + k for k in range(2) for m in range(4)], jnp.int32)
    gathered = spread(tokens).reshape(PLANE, number, columns)
    first_low, joined = project(order, gathered, vectors[0:1], vectors[1:2], attend)
    first_low = first_low.reshape(shared, columns)
    joined = joined.reshape(shared, 3 * wide)
    queries, pairs = joined[:, :wide], joined[:, wide:]
    before, after = move(pairs, PLANE), move(pairs, -PLANE)

    finish = jnp.cumsum(scene_lengths)
    begin = finish - scene_lengths
    base = (plane - 1) * shared
    position = plane * shared + jnp.arange(shared, dtype=jnp.int32)
    past = begin[None, :] <= position[:, None]
    span_begin = jnp.max(jnp.where(past, begin[None, :], 0), axis=1) - base
    span_end = jnp.min(jnp.where(finish[None, :] > position[:, None], finish[None, :], 1 << 30), axis=1) - base
    spans = jnp.stack([span_begin, span_end])
    ranges = jnp.stack(
        [span_begin[::QUERY_TILE] // KEY_TILE, (span_end[QUERY_TILE - 1 :: QUERY_TILE] + KEY_TILE - 1) // KEY_TILE]
    )
    mixed_exact, logs = attention(ranges, queries, before, pairs, after, spans)
    mixed_mine = mixed_exact.astype(LOW)
    mixed = exchange(mixed_mine.reshape(PLANE, number, wide), plane_groups())
    mixed = mixed.transpose(1, 0, 2).reshape(number, columns)

    second = tokens.astype(F32) + dot(mixed, output)
    unit_two, inverse_two = norm_parts(second)
    normed = (unit_two * vectors[2:3] + vectors[3:4]).astype(LOW)
    normed_all = spread(normed).reshape(shared, columns)
    cotangent_all = spread(cotangent).reshape(shared, columns)

    upper = dot(normed_all, expand) + bias_up
    active, active_back = jax.vjp(lambda v: jax.nn.gelu(v, approximate=False), upper)
    active_low = active.astype(LOW)
    upper_grad = active_back(dot(cotangent_all, shrink, ((1,), (1,))))[0].astype(LOW)
    normed_grad = collect(dot(upper_grad, expand, ((1,), (1,))).reshape(2, 4, number, columns))
    block_output = collect(dot(active_low, shrink).reshape(2, 4, number, columns))
    block_output = (second + block_output + vectors[4:5]).astype(LOW)

    second_grad = cotangent.astype(F32) + norm_back(unit_two, inverse_two, vectors[2:3], normed_grad)
    branch_grad = second_grad.astype(LOW)
    mixed_grad = dot(branch_grad, output, ((1,), (1,))).astype(LOW)
    mixed_grad = exchange(mixed_grad.reshape(number, PLANE, wide).transpose(1, 0, 2), plane_groups())
    mixed_grad = mixed_grad.reshape(shared, wide)

    query_grad, before_grad, own_grad, after_grad = attention_back(
        ranges, queries, before, pairs, after, spans, mixed_exact, logs, mixed_grad
    )
    pair_grad = own_grad + move(before_grad, -PLANE).astype(F32) + move(after_grad, PLANE).astype(F32)
    joined_grad = jnp.concatenate([query_grad, pair_grad.astype(LOW)], axis=1)

    attend_grad = dot(first_low, joined_grad, ((0,), (0,))).astype(LOW)
    attend_grad = exchange(attend_grad.reshape(n, rows, 3 * wide)).astype(F32)
    attend_grad = attend_grad.reshape(planes, PLANE, rows, 3, wide).sum(0).transpose(1, 2, 0, 3).reshape(rows, -1)

    expand_grad = dot(normed_all, upper_grad, ((0,), (0,))).astype(LOW)
    expand_grad = exchange(expand_grad.reshape(n, rows, planes * hidden)).astype(F32)
    expand_grad = (
        expand_grad.reshape(planes, PLANE, rows, planes, hidden).sum(0).transpose(1, 2, 0, 3).reshape(rows, -1)
    )
    shrink_grad = dot(active_low, cotangent_all, ((0,), (0,))).astype(LOW)
    shrink_grad = exchange(shrink_grad.reshape(planes, hidden, columns), cross_groups()).astype(F32).sum(0)
    branch_all = exchange(jnp.broadcast_to(branch_grad[None], (PLANE,) + branch_grad.shape), plane_groups())
    output_grad = dot(mixed_mine, branch_all.reshape(shared, columns), ((0,), (0,))).astype(LOW)
    output_grad = exchange(output_grad.reshape(planes, rows, columns), cross_groups()).astype(F32).sum(0)
    output_grad = lax.ppermute(
        output_grad,
        "seq",
        [(g * PLANE + j, j * planes + g) for g in range(planes) for j in range(PLANE)],
    )

    first_grad = collect(
        jnp.take(dot(joined_grad, attend, ((1,), (1,))).reshape(PLANE, number, columns), order, axis=0).reshape(
            2, 4, number, columns
        )
    )
    unit_one, inverse_one = norm_parts(tokens.astype(F32))
    input_gradient = (second_grad + norm_back(unit_one, inverse_one, vectors[0:1], first_grad)).astype(LOW)

    up_sum = jnp.sum(upper_grad.astype(F32), axis=0).reshape(planes, 1, hidden)
    up_sum = lax.dynamic_update_slice_in_dim(jnp.zeros((planes, PLANE, hidden), F32), up_sum, spot, axis=1)
    vector_grad = jnp.concatenate(
        [
            jnp.stack(
                [
                    jnp.sum(first_grad * unit_one, axis=0),
                    jnp.sum(first_grad, axis=0),
                    jnp.sum(normed_grad * unit_two, axis=0),
                    jnp.sum(normed_grad, axis=0),
                    jnp.sum(cotangent.astype(F32), axis=0),
                ]
            ),
            up_sum.reshape(-1, columns),
        ],
        axis=0,
    )
    vector_grad = exchange(jnp.moveaxis(vector_grad.reshape(-1, n, rows), 1, 0)).sum(0)

    groups = (
        (attend_weight, attend_momentum, attend_average, attend_grad),
        (output_weight, output_momentum, output_average, output_grad),
        (expand_weight, expand_momentum, expand_average, expand_grad),
        (reduce_weight, reduce_momentum, reduce_average, shrink_grad),
        (vector_params, vector_momentum, vector_average, vector_grad),
    )
    local_square = sum(jnp.sum(g[3] * g[3]) for g in groups)
    norm_square = jnp.sum(exchange(jnp.full((n, 1, 128), local_square, F32))[:, 0, 0])
    gradient_norm = jnp.sqrt(norm_square)
    factor = jnp.minimum(1.0, CLIP_NORM / (gradient_norm + 1e-06))
    smooth_rate = min(0.999, (1.0 + STEP) / (10.0 + STEP))
    updates = []
    for rate, (weight, moment, average, gradient) in zip(LEARNING_RATES, groups):
        clipped = factor * gradient + WEIGHT_DECAY * weight
        velocity = MOMENTUM * moment + clipped
        updated = weight - rate * (clipped + MOMENTUM * velocity)
        smoothed = smooth_rate * average + (1.0 - smooth_rate) * updated
        updates += [velocity, updated, smoothed]
    return (block_output, input_gradient, gradient_norm, *updates)


def solution(mesh):
    split, turned = P("seq", None), P(None, "seq")
    return jax.shard_map(
        on_device,
        mesh=mesh,
        in_specs=(split, P()) + (split,) * 5 + (turned,) + ((split,) * 4 + (turned,)) * 2,
        out_specs=(split, split, P()) + (split,) * 12 + (turned,) * 3,
        check_vma=False,
    )
```

```python
import functools

import jax
import jax.numpy as jnp
from jax import lax
from jax.experimental import pallas as pl
from jax.experimental.pallas import tpu as pltpu
from jax.sharding import PartitionSpec as P

HEADS = 16
STEP = 10
EPSILON = 1e-05
MOMENTUM = 0.9
LEARNING_RATES = (60.0, 480.0, 60.0, 60.0, 600.0)
WEIGHT_DECAY = 0.0001
CLIP_NORM = 1.0
MASK_FLOOR = -1e30
PLANE = 8
EXTRA = 8
LANES = 128
QUERY_TILE = 256
KEY_TILE = 256
F32 = jnp.float32
LOW = jnp.bfloat16
WHOLE = pl.BlockSpec()
SMEM = pl.BlockSpec(memory_space=pltpu.SMEM)


def like(shape, dtype):
    return jax.ShapeDtypeStruct(shape, dtype)


def kernel_call(body, outs, *args, scalars=(), scratch=(), flops=0, limit=60):
    moved = sum(a.size * a.dtype.itemsize for a in list(args) + list(outs))
    return pl.pallas_call(
        body,
        in_specs=[SMEM] * len(scalars) + [WHOLE] * len(args),
        out_specs=[WHOLE] * len(outs),
        out_shape=list(outs),
        scratch_shapes=list(scratch),
        cost_estimate=pl.CostEstimate(flops=flops, bytes_accessed=moved, transcendentals=0),
        compiler_params=pltpu.CompilerParams(vmem_limit_bytes=limit << 20),
    )(*scalars, *args)


def after(value, *others):
    return lax.optimization_barrier((value, *others))[0]


def tie(*values):
    return lax.optimization_barrier(values)


def swap(block, bit):
    n = lax.axis_size("seq")
    return lax.ppermute(block, "seq", [(i, i ^ bit) for i in range(n)])


def move(block, distance):
    n = lax.axis_size("seq")
    return lax.ppermute(
        block, "seq", [(i, i + distance) for i in range(n) if 0 <= i + distance < n]
    )


def turn(block, planes_on):
    n = lax.axis_size("seq")
    return lax.ppermute(block, "seq", [(i, (i + planes_on * PLANE) % n) for i in range(n)])


def plane_groups():
    n = lax.axis_size("seq")
    return [[g * PLANE + j for j in range(PLANE)] for g in range(n // PLANE)]


def cross_groups():
    n = lax.axis_size("seq")
    return [[g * PLANE + j for g in range(n // PLANE)] for j in range(PLANE)]


def exchange(blocks, groups=None):
    return lax.all_to_all(blocks, "seq", 0, 0, axis_index_groups=groups)


def spread_sides(block):
    return swap(block, 2), swap(block, 4)


def spread_corner(across, along):
    half = across.shape[0] // 2
    return swap(across[:half], 4), swap(along[half:], 2)


def spread_far(block, sides, corner):
    far = swap(jnp.stack([block, *sides]), 1)
    return [block, *sides, *corner, far, *[swap(c, 1) for c in corner]]


def spread(block):
    sides = spread_sides(block)
    return spread_far(block, sides, spread_corner(*sides))


SPREAD = 8


def join(refs, out):
    number = refs[0].shape[0]
    place = 0
    for ref in refs:
        if len(ref.shape) == 3:
            for m in range(ref.shape[0]):
                out[pl.ds(place, number), :] = ref[m]
                place += number
        else:
            out[pl.ds(place, ref.shape[0]), :] = ref[...]
            place += ref.shape[0]


def collect(near, far, far_corner):
    half = near.shape[1] // 2
    came_corner = swap(far_corner, 1)
    came = swap(far, 1)
    corner = (near[3] + came_corner.astype(F32)).astype(LOW)
    by_across = swap(corner[:half], 2).astype(F32)
    by_along = swap(corner[half:], 4).astype(F32)
    across = near[1] + came[1].astype(F32)
    along = near[2] + came[2].astype(F32)
    across = jnp.concatenate([across[:half], across[half:] + by_along], axis=0).astype(LOW)
    along = jnp.concatenate([along[:half] + by_across, along[half:]], axis=0).astype(LOW)
    return near[0] + came[0].astype(F32), swap(across, 2), swap(along, 4)


def put_block(outs, k, m, value):
    if k == 0:
        outs[0][m] = value
    elif m < 3:
        outs[1][m] = value.astype(LOW)
    else:
        outs[2][...] = value.astype(LOW)


def total(terms):
    return terms[0] + terms[1].astype(F32) + terms[2].astype(F32)


def norm_parts(values):
    centre = values - jnp.mean(values, axis=-1, keepdims=True)
    spread_of = jnp.mean(centre * centre, axis=-1, keepdims=True)
    inverse = lax.rsqrt(spread_of + EPSILON)
    return centre * inverse, inverse


def norm_back(unit, inverse, gain, incoming):
    scaled = incoming * gain
    return inverse * (
        scaled
        - jnp.mean(scaled, axis=-1, keepdims=True)
        - unit * jnp.mean(scaled * unit, axis=-1, keepdims=True)
    )


def dot(a, b, dims=((1,), (0,))):
    return lax.dot_general(a, b, (dims, ((), ())), preferred_element_type=F32)


NT = ((1,), (1,))
TN = ((0,), (0,))


def block_rows(place, number):
    return pl.ds(pl.multiple_of(place * number, number), number)


def gather_planes(plane, refs, out):
    planes = len(refs)
    rows = refs[0].shape[0]
    for s, ref in enumerate(refs):
        out[block_rows(lax.rem(plane - s + planes, planes), rows), :] = ref[...]


def project_kernel(spot_ref, *refs):
    token_refs, refs = refs[:SPREAD], refs[SPREAD:]
    sent_ref, lots_ref, unit_ref, first_ref, pair_ref, weight_ref, vector_ref, held = refs
    spot = spot_ref[0]
    number, columns = token_refs[0].shape
    devices = sent_ref.shape[0]
    rows = columns // devices
    for d in range(devices):
        weight_ref[pl.ds(d * rows, rows), :] = sent_ref[d, :rows, :]
    for g in range(lots_ref.shape[0]):
        lanes = slice(g * LANES, (g + 1) * LANES)
        vector_ref[:EXTRA, lanes] = lots_ref[g, :, :LANES]
        vector_ref[EXTRA:, lanes] = lots_ref[g, :, LANES : 2 * LANES]
    join(token_refs, held)
    gain, shift = vector_ref[0:1, :], vector_ref[1:2, :]
    for r in range(PLANE):
        here = pl.ds(r * number, number)
        unit, _ = norm_parts(held[here, :].astype(F32))
        first = (unit * gain + shift).astype(LOW)
        unit_ref[here, :] = unit.astype(LOW)
        held[here, :] = first
        first_ref[block_rows(spot ^ relative(r), number), :] = first
    pairs = dot(held[...], weight_ref[...]).astype(LOW)
    for r in range(PLANE):
        pair_ref[block_rows(spot ^ relative(r), number), :] = pairs[r * number : (r + 1) * number]


def relative(r):
    return 2 * (r % 4) + r // 4


def head_mask(shape, head):
    return lax.broadcasted_iota(jnp.int32, shape, len(shape) - 1) // 64 == head


def attend_kernel(
    range_ref, query_ref, before_ref, own_ref, after_ref, span_ref, mixed_ref, low_ref, log_ref, keys, values
):
    step = pl.program_id(0)
    tokens = own_ref.shape[0]
    wide = query_ref.shape[1]

    @pl.when(step == 0)
    def _():
        for place, ref in enumerate((before_ref, own_ref, after_ref)):
            keys[pl.ds(place * tokens, tokens), :] = ref[:, :wide]
            values[:, pl.ds(place * tokens, tokens)] = ref[:, wide:].T

    queries = query_ref[...] * jnp.asarray(0.125, LOW)
    begin = span_ref[0:1, :]
    end = span_ref[1:2, :]
    here = query_ref.shape[0]
    split = [jnp.where(head_mask(queries.shape, h), queries, jnp.zeros_like(queries)) for h in range(2)]

    def body(index, carry):
        start = pl.multiple_of(index * KEY_TILE, KEY_TILE)
        block = keys[pl.ds(start, KEY_TILE), :]
        place = start + lax.broadcasted_iota(jnp.int32, (KEY_TILE, here), 0)
        allowed = (place >= begin) & (place < end)
        out = []
        for h in range(2):
            peak, whole, mixed = carry[h]
            scores = jnp.where(allowed, dot(block, split[h], NT), MASK_FLOOR)
            raised_peak = jnp.maximum(peak, jnp.max(scores, axis=0, keepdims=True))
            raised = jnp.exp(scores - raised_peak)
            fade = jnp.exp(peak - raised_peak)
            whole = whole * fade + jnp.sum(raised, axis=0, keepdims=True)
            turned = values[64 * h : 64 * h + 64, pl.ds(start, KEY_TILE)]
            mixed = mixed * fade + dot(turned, raised.astype(LOW))
            out.append((raised_peak, whole, mixed))
        return tuple(out)

    init = tuple(
        (jnp.full((1, here), MASK_FLOOR, F32), jnp.zeros((1, here), F32), jnp.zeros((64, here), F32))
        for _ in range(2)
    )
    done = lax.fori_loop(range_ref[0, step], range_ref[1, step], body, init)
    mixed = jnp.concatenate([m / t for _, t, m in done], axis=0).T
    mixed_ref[...] = mixed
    low_ref[...] = mixed.astype(LOW)
    log_ref[...] = jnp.concatenate([k + jnp.log(t) for k, t, _ in done], axis=0)


def attend_back_kernel(
    range_ref,
    query_ref,
    before_ref,
    own_ref,
    after_ref,
    span_ref,
    mixed_ref,
    log_ref,
    grad_ref,
    query_grad_ref,
    before_grad_ref,
    own_grad_ref,
    after_grad_ref,
    keys,
    values,
    turned_keys,
    key_grad,
    value_grad,
):
    step = pl.program_id(0)
    tokens = own_ref.shape[0]
    wide = query_ref.shape[1]

    @pl.when(step == 0)
    def _():
        for place, ref in enumerate((before_ref, own_ref, after_ref)):
            keys[pl.ds(place * tokens, tokens), :] = ref[:, :wide]
            values[pl.ds(place * tokens, tokens), :] = ref[:, wide:]
            turned_keys[:, pl.ds(place * tokens, tokens)] = ref[:, :wide].T
        key_grad[...] = jnp.zeros_like(key_grad)
        value_grad[...] = jnp.zeros_like(value_grad)

    queries = query_ref[...] * jnp.asarray(0.125, LOW)
    grads = grad_ref[...]
    here = queries.shape[0]
    zero = jnp.zeros_like(queries)
    split = [jnp.where(head_mask(queries.shape, h), queries, zero) for h in range(2)]
    split_grads = [jnp.where(head_mask(queries.shape, h), grads, zero) for h in range(2)]
    product = (grads.astype(F32) * mixed_ref[...]).T
    centred = [jnp.sum(product[64 * h : 64 * h + 64], axis=0, keepdims=True) for h in range(2)]
    begin = span_ref[0:1, :]
    end = span_ref[1:2, :]

    def body(index, carry):
        start = pl.multiple_of(index * KEY_TILE, KEY_TILE)
        rows = pl.ds(start, KEY_TILE)
        place = start + lax.broadcasted_iota(jnp.int32, (KEY_TILE, here), 0)
        allowed = (place >= begin) & (place < end)
        out, key_part, value_part = [], 0, 0
        for h in range(2):
            scores = dot(keys[rows, :], split[h], NT)
            shares = jnp.exp(jnp.where(allowed, scores - log_ref[h : h + 1, :], MASK_FLOOR))
            value_part += dot(shares.astype(LOW), split_grads[h])
            share_grad = dot(values[rows, :], split_grads[h], NT)
            score_grad = (shares * (share_grad - centred[h])).astype(LOW)
            key_part += dot(score_grad, split[h])
            out.append(carry[h] + dot(turned_keys[64 * h : 64 * h + 64, rows], score_grad))
        key_grad[rows, :] += key_part
        value_grad[rows, :] += value_part
        return tuple(out)

    init = tuple(jnp.zeros((64, here), F32) for _ in range(2))
    done = lax.fori_loop(range_ref[0, step], range_ref[1, step], body, init)
    query_grad_ref[...] = (jnp.concatenate(done, axis=0).T * 0.125).astype(LOW)

    @pl.when(step == pl.num_programs(0) - 1)
    def _():
        for place, ref in enumerate((before_grad_ref, own_grad_ref, after_grad_ref)):
            ref[:, :wide] = key_grad[pl.ds(place * tokens, tokens), :].astype(ref.dtype)
            ref[:, wide:] = value_grad[pl.ds(place * tokens, tokens), :].astype(ref.dtype)


def attention(ranges, queries, before, own, behind, spans):
    tokens, wide = queries.shape
    whole = lambda shape: pl.BlockSpec(shape, lambda i, s: (0, 0))
    tile = pl.BlockSpec((QUERY_TILE, wide), lambda i, s: (i, 0))
    row = pl.BlockSpec((2, QUERY_TILE), lambda i, s: (0, i))
    return pl.pallas_call(
        attend_kernel,
        grid_spec=pltpu.PrefetchScalarGridSpec(
            num_scalar_prefetch=1,
            grid=(tokens // QUERY_TILE,),
            in_specs=[tile] + [whole((tokens, 2 * wide))] * 3 + [row],
            out_specs=[tile, tile, row],
            scratch_shapes=[
                pltpu.VMEM((3 * tokens, wide), LOW),
                pltpu.VMEM((wide, 3 * tokens), LOW),
            ],
        ),
        out_shape=[like((tokens, wide), F32), like((tokens, wide), LOW), like((2, tokens), F32)],
        cost_estimate=pl.CostEstimate(
            flops=40 * tokens * tokens * wide, bytes_accessed=16 * tokens * wide, transcendentals=2 * tokens * tokens
        ),
        compiler_params=pltpu.CompilerParams(vmem_limit_bytes=60 << 20),
    )(ranges, queries, before, own, behind, spans)


def attention_back(ranges, queries, before, own, behind, spans, mixed, logs, grads):
    tokens, wide = queries.shape
    whole = lambda shape: pl.BlockSpec(shape, lambda i, s: (0, 0))
    tile = pl.BlockSpec((QUERY_TILE, wide), lambda i, s: (i, 0))
    row = pl.BlockSpec((2, QUERY_TILE), lambda i, s: (0, i))
    return pl.pallas_call(
        attend_back_kernel,
        grid_spec=pltpu.PrefetchScalarGridSpec(
            num_scalar_prefetch=1,
            grid=(tokens // QUERY_TILE,),
            in_specs=[tile] + [whole((tokens, 2 * wide))] * 3 + [row, tile, row, tile],
            out_specs=[tile] + [whole((tokens, 2 * wide))] * 3,
            scratch_shapes=[
                pltpu.VMEM((3 * tokens, wide), LOW),
                pltpu.VMEM((3 * tokens, wide), LOW),
                pltpu.VMEM((wide, 3 * tokens), LOW),
                pltpu.VMEM((3 * tokens, wide), F32),
                pltpu.VMEM((3 * tokens, wide), F32),
            ],
        ),
        out_shape=[
            like((tokens, wide), LOW),
            like((tokens, 2 * wide), LOW),
            like((tokens, 2 * wide), F32),
            like((tokens, 2 * wide), LOW),
        ],
        cost_estimate=pl.CostEstimate(
            flops=60 * tokens * tokens * wide, bytes_accessed=32 * tokens * wide, transcendentals=2 * tokens * tokens
        ),
        compiler_params=pltpu.CompilerParams(vmem_limit_bytes=60 << 20),
    )(ranges, queries, before, own, behind, spans, mixed, logs, grads)


def place_output(planes, place_ref, refs, held, out):
    if len(refs) == 1:
        out[...] = refs[0][...]
        return
    join(refs, held)
    rows = out.shape[0] // (PLANE * planes)
    for r in range(PLANE):
        for s in range(planes):
            device = lax.rem(place_ref[1] - s + planes, planes) * PLANE + (place_ref[0] ^ relative(r))
            out[block_rows(device, rows), :] = held[pl.ds((r * planes + s) * rows, rows), :]


def ordered_output(spot, plane, refs, planes):
    rows = refs[0].shape[0] // planes
    if rows % 16 == 0:
        return refs
    whole = jnp.concatenate([r.reshape(-1, r.shape[-1]) for r in refs], axis=0)
    whole = whole.reshape(PLANE, planes, rows, -1)
    device = jnp.arange(PLANE * planes)
    turns = (plane - device // PLANE) % planes
    bits = device % PLANE ^ spot
    return [whole[bits // 2 + 4 * (bits % 2), turns].reshape(PLANE * planes * rows, -1)]


def mix_out_kernel(planes, place_ref, mixed_ref, tokens_ref, vector_ref, *refs):
    output_refs, (second_ref, normed_ref, held, output) = refs[:-4], refs[-4:]
    place_output(planes, place_ref, output_refs, held, output)
    mixed = jnp.concatenate([mixed_ref[j] for j in range(PLANE)], axis=1)
    second = tokens_ref[...].astype(F32) + dot(mixed, output[...])
    second_ref[...] = second
    unit, _ = norm_parts(second)
    normed_ref[...] = (unit * vector_ref[2:3, :] + vector_ref[3:4, :]).astype(LOW)


def feed_kernel(planes, place_ref, *refs):
    normed_refs, refs = refs[:SPREAD], refs[SPREAD:]
    cot_refs, refs = refs[:SPREAD], refs[SPREAD:]
    shrink_refs, refs = refs[:planes], refs[planes:]
    expand_refs, refs = refs[:2], refs[2:]
    bias_ref, near_out, far_out, corner_out, active_ref, grad_ref, bias_out, expand, shrink, x, c = refs
    part = expand.shape[1] // 2
    expand[:, :part] = expand_refs[0][...]
    expand[:, part:] = expand_refs[1][...]
    gather_planes(place_ref[1], shrink_refs, shrink)
    join(normed_refs, x)
    join(cot_refs, c)
    number = near_out.shape[1]
    sums = jnp.zeros(bias_ref.shape, F32)
    for k, m in ((1, 2), (1, 0), (0, 2), (0, 0)):
        rows = pl.ds((4 * k + m) * number, 2 * number)
        upper = dot(x[rows, :], expand[...]) + bias_ref[...]
        share = 0.5 + 0.5 * lax.erf(upper * 0.7071067811865476)
        density = 0.3989422804014327 * jnp.exp(-0.5 * upper * upper)
        active_ref[rows, :] = (upper * share).astype(LOW)
        grad = (dot(c[rows, :], shrink[...], NT) * (share + upper * density)).astype(LOW)
        grad_ref[rows, :] = grad
        sums += jnp.sum(grad.astype(F32), axis=0, keepdims=True)
        down = dot(grad, expand[...], NT)
        put_block((near_out, far_out, corner_out), k, m, down[:number])
        put_block((near_out, far_out, corner_out), k, m + 1, down[number:])
    bias_out[...] = sums


def lower_kernel(planes, place_ref, active_ref, *refs):
    shrink_refs, (near_out, far_out, corner_out, shrink) = refs[:planes], refs[planes:]
    gather_planes(place_ref[1], shrink_refs, shrink)
    number = near_out.shape[1]
    for k, m in ((1, 2), (1, 0), (0, 2), (0, 0)):
        lower = dot(active_ref[pl.ds((4 * k + m) * number, 2 * number), :], shrink[...])
        put_block((near_out, far_out, corner_out), k, m, lower[:number])
        put_block((near_out, far_out, corner_out), k, m + 1, lower[number:])


def plane_blocks(plane, whole, outs):
    planes = len(outs)
    tall = whole.shape[0] // planes
    for s, out in enumerate(outs):
        out[...] = whole[block_rows(lax.rem(plane + s, planes), tall), :].astype(out.dtype)


def shrink_grad_kernel(place_ref, active_ref, *refs):
    cot_refs, outs, (whole, cotangents) = refs[:SPREAD], refs[SPREAD:-2], refs[-2:]
    join(cot_refs, cotangents)
    whole[...] = dot(active_ref[...], cotangents[...], TN)
    plane_blocks(place_ref[1], whole, outs)


def expand_grad_kernel(grad_ref, *refs):
    normed_refs, (out_ref, other_ref, normed) = refs[:SPREAD], refs[SPREAD:]
    join(normed_refs, normed)
    half = grad_ref.shape[1] // 2
    out_ref[...] = dot(normed[...], grad_ref[:, :half], TN).astype(LOW)
    other_ref[...] = dot(normed[...], grad_ref[:, half:], TN).astype(LOW)


def norm_two_back_kernel(
    planes, place_ref, one_ref, two_ref, three_ref, second_ref, cotangent_ref, vector_ref, *refs
):
    output_refs, (second_grad_ref, branch_ref, mixed_ref, sums_ref, held, output) = refs[:-6], refs[-6:]
    place_output(planes, place_ref, output_refs, held, output)
    incoming = one_ref[...] + two_ref[...].astype(F32) + three_ref[...].astype(F32)
    unit, inverse = norm_parts(second_ref[...])
    cotangent = cotangent_ref[...].astype(F32)
    second_grad = cotangent + norm_back(unit, inverse, vector_ref[2:3, :], incoming)
    second_grad_ref[...] = second_grad
    branch = second_grad.astype(LOW)
    branch_ref[...] = branch
    mixed = dot(branch, output[...], NT).astype(LOW)
    wide = mixed_ref.shape[2]
    for j in range(PLANE):
        mixed_ref[j] = mixed[:, wide * j : wide * j + wide]
    sums_ref[...] = jnp.concatenate(
        [
            jnp.sum(incoming * unit, axis=0, keepdims=True),
            jnp.sum(incoming, axis=0, keepdims=True),
            jnp.sum(cotangent, axis=0, keepdims=True),
        ],
        axis=0,
    )


def output_grad_kernel(place_ref, mixed_ref, *refs):
    branch_refs, outs, (whole, left, right) = refs[:SPREAD], refs[SPREAD:-3], refs[-3:]
    join(branch_refs, right)
    number = branch_refs[0].shape[0]
    for r in range(PLANE):
        left[pl.ds(r * number, number), :] = mixed_ref[block_rows(place_ref[0] ^ relative(r), number), :]
    whole[...] = dot(left[...], right[...], TN)
    if len(outs) == 1:
        outs[0][...] = whole[...].astype(LOW)
    else:
        plane_blocks(place_ref[1], whole, outs)


def first_back_kernel(
    place_ref, own_ref, from_after_ref, from_before_ref, query_ref, first_ref, unit_ref,
    pair_weight_ref, query_weight_ref, grad_ref, near_ref, far_ref, corner_ref, sums_ref, joined, weight,
):
    spot = place_ref[0]
    number, columns = near_ref.shape[1:]
    wide = query_ref.shape[1]
    pairs = (own_ref[...] + from_after_ref[...].astype(F32) + from_before_ref[...].astype(F32)).astype(LOW)
    joined[:, :wide] = query_ref[...]
    joined[:, wide:] = pairs
    weight[:, :wide] = query_weight_ref[...]
    weight[:, wide:] = pair_weight_ref[...]
    grad_ref[...] = dot(first_ref[...], joined[...], TN).astype(LOW)
    gain = jnp.zeros((1, columns), F32)
    shift = jnp.zeros((1, columns), F32)
    for k, m in ((1, 2), (1, 0), (0, 2), (0, 0)):
        part = jnp.concatenate(
            [joined[block_rows(spot ^ (2 * (m + i) + k), number), :] for i in range(2)], axis=0
        )
        down = dot(part, weight[...], NT)
        unit = unit_ref[pl.ds((4 * k + m) * number, 2 * number), :].astype(F32)
        gain += jnp.sum(down * unit, axis=0, keepdims=True)
        shift += jnp.sum(down, axis=0, keepdims=True)
        put_block((near_ref, far_ref, corner_ref), k, m, down[:number])
        put_block((near_ref, far_ref, corner_ref), k, m + 1, down[number:])
    sums_ref[...] = jnp.concatenate([gain, shift], axis=0)


def first_norm_back_kernel(one_ref, two_ref, three_ref, tokens_ref, second_grad_ref, vector_ref, out_ref):
    incoming = one_ref[...] + two_ref[...].astype(F32) + three_ref[...].astype(F32)
    unit, inverse = norm_parts(tokens_ref[...].astype(F32))
    out_ref[...] = (second_grad_ref[...] + norm_back(unit, inverse, vector_ref[0:1, :], incoming)).astype(LOW)


def sum_kernel(wide, *refs):
    part_refs, (grad_ref, square_ref) = refs[:-2], refs[-2:]
    rows = grad_ref.shape[0]
    square = jnp.zeros((rows, wide), F32)
    start = 0
    for ref in part_refs:
        for c in range(ref.shape[2] // wide):
            for j in range(PLANE):
                sources = range(j, ref.shape[0], PLANE)
                whole = sum(ref[d, :rows, c * wide : (c + 1) * wide].astype(F32) for d in sources)
                grad_ref[:, start : start + wide] = whole
                square += whole * whole
                start += wide
    square_ref[...] = jnp.sum(square, keepdims=True)


def sum_parts(wide, rows, *parts):
    if wide % LANES == 0:
        columns = PLANE * sum(p.shape[2] for p in parts)
        return kernel_call(
            functools.partial(sum_kernel, wide), [like((rows, columns), F32), like((1, 1), F32)], *parts
        )
    whole = jnp.concatenate([p[:, :rows] for p in parts], axis=2).astype(F32)
    whole = whole.reshape(-1, PLANE, rows, whole.shape[2] // wide, wide).sum(0)
    whole = whole.transpose(1, 2, 0, 3).reshape(rows, -1)
    return whole, jnp.sum(whole * whole).reshape(1, 1)


def update_kernel(factor_ref, *refs):
    factor = factor_ref[0]
    smooth_rate = min(0.999, (1.0 + STEP) / (10.0 + STEP))
    count = len(LEARNING_RATES)
    states, grads, outs = refs[: 3 * count], refs[3 * count : 4 * count], refs[4 * count :]
    for place, rate in enumerate(LEARNING_RATES):
        weight, moment, average = (ref[...] for ref in states[3 * place : 3 * place + 3])
        clipped = factor * grads[place][...] + WEIGHT_DECAY * weight
        velocity = MOMENTUM * moment + clipped
        updated = weight - rate * (clipped + MOMENTUM * velocity)
        outs[3 * place][...] = velocity
        outs[3 * place + 1][...] = updated
        outs[3 * place + 2][...] = smooth_rate * average + (1.0 - smooth_rate) * updated


def on_device(
    tokens,
    scene_lengths,
    cotangent,
    attend_weight,
    output_weight,
    expand_weight,
    reduce_weight,
    vector_params,
    attend_momentum,
    output_momentum,
    expand_momentum,
    reduce_momentum,
    vector_momentum,
    attend_average,
    output_average,
    expand_average,
    reduce_average,
    vector_average,
):
    n = lax.axis_size("seq")
    planes = n // PLANE
    device = lax.axis_index("seq")
    plane, spot = device // PLANE, device % PLANE
    place = jnp.stack([spot, plane]).astype(jnp.int32)
    number, columns = tokens.shape
    shared = number * PLANE
    rows = columns // n
    hidden = reduce_weight.shape[0]
    wide = columns // PLANE
    lots = columns // LANES
    in_lot = LANES // rows
    inner = planes * hidden
    near_like, far_like = like((4, number, columns), F32), like((3, number, columns), LOW)
    block_like, block_exact = like((number, columns), LOW), like((number, columns), F32)
    shared_scratch = pltpu.VMEM((shared, columns), LOW)
    square_scratch = pltpu.VMEM((columns, columns), LOW)

    sides = spread_sides(tokens)
    attend_low = attend_weight.astype(LOW).reshape(rows, 3, PLANE, wide)
    pair_weight = attend_low[:, 1:].transpose(2, 0, 1, 3).reshape(PLANE, rows, 2 * wide)
    vector_part = lax.dynamic_update_slice(
        jnp.zeros((2 * EXTRA, LANES), LOW), vector_params.astype(LOW), (0, rows * (device % in_lot))
    )
    vector_part = jnp.concatenate([vector_part[:EXTRA], vector_part[EXTRA:]], axis=1)
    pair_weight = jnp.concatenate(
        [
            jnp.broadcast_to(pair_weight[None], (planes,) + pair_weight.shape).reshape(n, rows, 2 * wide),
            jnp.broadcast_to(vector_part[None], (n,) + vector_part.shape),
        ],
        axis=1,
    )
    pair_weight = exchange(pair_weight)
    lot_vectors = pair_weight[:, rows:].reshape(lots, in_lot, EXTRA, 2 * wide).astype(F32).sum(1)
    corner = spread_corner(*sides)
    output = after(output_weight, *sides).astype(LOW)
    output = jnp.concatenate([output] + [turn(output, s) for s in range(1, planes)], axis=0)
    gathered = spread_far(tokens, sides, corner)
    query_weight = attend_low[:, 0].transpose(1, 0, 2)
    query_weight = jnp.broadcast_to(query_weight[None], (planes,) + query_weight.shape).reshape(n, rows, wide)
    expand = (
        expand_weight.astype(LOW)
        .reshape(rows, planes, PLANE, hidden)
        .transpose(2, 0, 1, 3)
        .reshape(PLANE, rows, inner)
    )
    expand = jnp.broadcast_to(expand[None], (planes,) + expand.shape).reshape(n, rows, inner)
    expand = [expand[:, :, : inner // 2], expand[:, :, inner // 2 :]]
    shrink = reduce_weight.astype(LOW)
    gathered, output, query_weight, expand, shrink = tie(gathered, output, query_weight, expand, shrink)

    units, first_low, pairs, pair_weight, vectors = kernel_call(
        project_kernel,
        [
            like((shared, columns), LOW),
            like((shared, columns), LOW),
            like((shared, 2 * wide), LOW),
            like((columns, 2 * wide), LOW),
            like((2 * EXTRA, columns), F32),
        ],
        *gathered,
        pair_weight,
        lot_vectors,
        scalars=(place,),
        scratch=[shared_scratch],
        flops=4 * shared * columns * wide,
    )
    bias_up = lax.dynamic_index_in_dim(
        vectors[5 : vector_params.shape[0]].reshape(planes, PLANE, hidden), spot, axis=1, keepdims=False
    ).reshape(1, inner)

    before, behind = move(pairs, PLANE), move(pairs, -PLANE)
    query_weight = exchange(after(query_weight, pairs)).reshape(columns, wide)
    queries = dot(first_low, query_weight).astype(LOW)
    expand[0] = exchange(after(expand[0], query_weight)).reshape(columns, inner // 2)
    output_sides = spread_sides(after(output, pairs))
    queries, output_sides = tie(queries, output_sides)

    finish = jnp.cumsum(scene_lengths)
    begin = finish - scene_lengths
    base = (plane - 1) * shared
    position = plane * shared + jnp.arange(shared, dtype=jnp.int32)
    past = begin[None, :] <= position[:, None]
    span_begin = jnp.max(jnp.where(past, begin[None, :], 0), axis=1) - base
    span_end = jnp.min(jnp.where(finish[None, :] > position[:, None], finish[None, :], 1 << 30), axis=1) - base
    spans = jnp.stack([span_begin, span_end])
    ranges = jnp.stack(
        [span_begin[::QUERY_TILE] // KEY_TILE, (span_end[QUERY_TILE - 1 :: QUERY_TILE] + KEY_TILE - 1) // KEY_TILE]
    )
    output_corner = spread_corner(*output_sides)
    cot_sides = spread_sides(after(cotangent, queries))
    mixed_exact, mixed_low, logs = attention(ranges, queries, before, pairs, behind, spans)
    mixed_low, output_corner, cot_sides, expand[0] = tie(mixed_low, output_corner, cot_sides, expand[0])

    mixed = exchange(mixed_low.reshape(PLANE, number, wide), plane_groups())
    output = spread_far(output, output_sides, output_corner)
    cot_corner = spread_corner(*cot_sides)
    shrink = after(shrink, mixed_low)
    shrink_turns = [turn(shrink, s) for s in range(1, planes)]
    output = ordered_output(spot, plane, output, planes)
    second, normed = kernel_call(
        functools.partial(mix_out_kernel, planes),
        [block_exact, block_like],
        mixed,
        tokens,
        vectors,
        *output,
        scalars=(place,),
        scratch=[square_scratch, square_scratch],
        flops=2 * number * columns * columns,
    )

    expand[1] = exchange(after(expand[1], mixed)).reshape(columns, inner // 2)
    sides = spread_sides(normed)
    sides, shrink_turns[::2], cot_corner = tie(sides, shrink_turns[::2], cot_corner)
    cotangents = spread_far(cotangent, cot_sides, cot_corner)
    corner = spread_corner(*sides)
    corner, shrink_turns = tie(corner, shrink_turns)
    shrink = [shrink] + shrink_turns
    normed_all = spread_far(normed, sides, corner)

    inner_low = like((shared, inner), LOW)
    grad_near, grad_far, grad_corner, active, upper_grad, up_sums = kernel_call(
        functools.partial(feed_kernel, planes),
        [near_like, far_like, block_like, inner_low, inner_low, like((1, inner), F32)],
        *normed_all,
        *cotangents,
        *shrink,
        *expand,
        bias_up,
        scalars=(place,),
        scratch=[pltpu.VMEM((columns, inner), LOW), pltpu.VMEM((inner, columns), LOW), shared_scratch, shared_scratch],
        flops=6 * shared * columns * inner,
    )

    normed_grad = collect(grad_near, grad_far, grad_corner)
    shrink_grad = kernel_call(
        shrink_grad_kernel,
        [like((hidden, columns), LOW)] * planes,
        active,
        *cotangents,
        scalars=(place,),
        scratch=[pltpu.VMEM((inner, columns), F32), shared_scratch],
        flops=2 * shared * columns * inner,
    )
    shrink_turns = [turn(shrink_grad[s], s) for s in range(1, planes)]
    normed_grad, shrink_turns[:1] = tie(normed_grad, shrink_turns[:1])
    second_grad, branch_grad, mixed_grad, two_sums = kernel_call(
        functools.partial(norm_two_back_kernel, planes),
        [block_exact, block_like, like((PLANE, number, wide), LOW), like((3, columns), F32)],
        *normed_grad,
        second,
        cotangent,
        vectors,
        *output,
        scalars=(place,),
        scratch=[square_scratch, square_scratch],
        flops=2 * number * columns * columns,
    )

    mixed_grad = exchange(mixed_grad, plane_groups()).reshape(shared, wide)
    expand_grad = kernel_call(
        expand_grad_kernel,
        [like((columns, inner // 2), LOW)] * 2,
        after(upper_grad, branch_grad),
        *normed_all,
        scratch=[shared_scratch],
        flops=2 * shared * columns * inner,
    )
    branch_sides = spread_sides(branch_grad)
    mixed_grad, expand_grad, branch_sides, shrink_turns = tie(mixed_grad, expand_grad, branch_sides, shrink_turns)
    shrink_grad = sum(g.astype(F32) for g in [shrink_grad[0], *shrink_turns])

    expand_part = [exchange(expand_grad[0].reshape(n, rows, inner // 2))]
    branch_corner = spread_corner(*branch_sides)
    query_grad, before_grad, own_grad, behind_grad = attention_back(
        ranges, queries, before, pairs, behind, spans, mixed_exact, logs, mixed_grad
    )
    before_grad, behind_grad, branch_corner, expand_part = tie(before_grad, behind_grad, branch_corner, expand_part)

    from_after, from_before = move(before_grad, -PLANE), move(behind_grad, PLANE)
    expand_part = expand_part + [exchange(after(expand_grad[1], before_grad).reshape(n, rows, inner // 2))]
    branch_all = spread_far(branch_grad, branch_sides, branch_corner)
    lower = kernel_call(
        functools.partial(lower_kernel, planes),
        [near_like, far_like, block_like],
        after(active, before_grad),
        *shrink,
        scalars=(place,),
        scratch=[pltpu.VMEM((inner, columns), LOW)],
        flops=2 * shared * columns * inner,
    )
    output_grad = kernel_call(
        output_grad_kernel,
        [like((rows, columns), LOW)] * planes if rows % 16 == 0 else [like((wide, columns), LOW)],
        mixed_low,
        *branch_all,
        scalars=(place,),
        scratch=[pltpu.VMEM((wide, columns), F32), pltpu.VMEM((shared, wide), LOW), shared_scratch],
        flops=2 * shared * columns * wide,
    )
    from_after, from_before, output_grad, lower, expand_part = tie(
        from_after, from_before, output_grad, lower, expand_part
    )

    attend_grad, first_near, first_far, first_corner, one_sums = kernel_call(
        first_back_kernel,
        [like((columns, 3 * wide), LOW), near_like, far_like, block_like, like((2, columns), F32)],
        own_grad,
        from_after,
        from_before,
        query_grad,
        first_low,
        units,
        pair_weight,
        query_weight,
        scalars=(place,),
        scratch=[pltpu.VMEM((shared, 3 * wide), LOW), pltpu.VMEM((columns, 3 * wide), LOW)],
        flops=2 * shared * columns * 6 * wide,
    )
    up_sums = lax.dynamic_update_slice_in_dim(
        jnp.zeros((planes, PLANE, hidden), F32), up_sums.reshape(planes, 1, hidden), spot, axis=1
    )
    vector_part = jnp.concatenate([two_sums, up_sums.reshape(-1, columns)], axis=0)
    vector_part = jnp.concatenate([one_sums, vector_part], axis=0).astype(LOW).reshape(-1, lots, LANES)
    vector_part = jnp.moveaxis(vector_part, 1, 0)
    more = vector_part.shape[1] - EXTRA
    vector_part = jnp.concatenate(
        [
            vector_part[:, :EXTRA],
            jnp.pad(vector_part[:, EXTRA:], ((0, 0), (0, EXTRA - more), (0, 3 * wide - 2 * LANES))),
        ],
        axis=2,
    )
    vector_part = jnp.repeat(vector_part, in_lot, axis=0)
    attend_part = jnp.concatenate([attend_grad.reshape(n, rows, 3 * wide), vector_part], axis=1)
    attend_part, output_grad, first_near, first_far, first_corner, lower, expand_part = tie(
        attend_part, output_grad, first_near, first_far, first_corner, lower, expand_part
    )
    attend_part = exchange(attend_part)
    expand_grad, expand_square = sum_parts(hidden, rows, *expand_part)
    vector_grad = attend_part[:, rows:].astype(F32).sum(0)
    vector_grad = jnp.concatenate([vector_grad[:, :LANES], vector_grad[:more, LANES : 2 * LANES]], axis=0)
    vector_grad = lax.dynamic_slice_in_dim(vector_grad, rows * (device % in_lot), rows, axis=1)
    attend_grad, attend_square = sum_parts(wide, rows, attend_part)

    if len(output_grad) == 1:
        output_grad = jnp.take(
            output_grad[0].reshape(planes, rows, columns), (plane + jnp.arange(planes)) % planes, axis=0, mode="clip"
        )
    output_grad = sum(
        [output_grad[0].astype(F32)] + [turn(output_grad[s], s).astype(F32) for s in range(1, planes)]
    )
    output_grad = lax.ppermute(
        output_grad, "seq", [(g * PLANE + j, j * planes + g) for g in range(planes) for j in range(PLANE)]
    )
    first_grad = collect(first_near, first_far, first_corner)
    (input_gradient,) = kernel_call(
        first_norm_back_kernel, [block_like], *first_grad, tokens, second_grad, vectors
    )
    block_output = collect(*lower)
    block_output = (second + total(block_output) + vectors[4:5]).astype(LOW)

    squares = [jnp.sum(g * g) for g in (output_grad, shrink_grad, vector_grad)]
    local_square = sum(squares) + expand_square[0, 0] + attend_square[0, 0]
    norm_square = jnp.sum(exchange(jnp.full((n, 1, LANES), local_square, F32))[:, 0, 0])
    gradient_norm = jnp.sqrt(norm_square)
    factor = jnp.minimum(1.0, CLIP_NORM / (gradient_norm + 1e-06))
    states = (
        (attend_weight, attend_momentum, attend_average),
        (output_weight, output_momentum, output_average),
        (expand_weight, expand_momentum, expand_average),
        (reduce_weight, reduce_momentum, reduce_average),
        (vector_params, vector_momentum, vector_average),
    )
    updates = kernel_call(
        update_kernel,
        [like(g[0].shape, F32) for g in states for _ in range(3)],
        *[a for g in states for a in g],
        attend_grad,
        output_grad,
        expand_grad,
        shrink_grad,
        vector_grad,
        scalars=(factor.reshape(1),),
    )
    return (block_output, input_gradient, gradient_norm, *updates)


def solution(mesh):
    split, turned = P("seq", None), P(None, "seq")
    return jax.shard_map(
        on_device,
        mesh=mesh,
        in_specs=(split, P()) + (split,) * 5 + (turned,) + ((split,) * 4 + (turned,)) * 2,
        out_specs=(split, split, P()) + (split,) * 12 + (turned,) * 3,
        check_vma=False,
    )
```

```python
import functools

import jax
import jax.numpy as jnp
from jax import lax
from jax.experimental import pallas as pl
from jax.experimental.pallas import tpu as pltpu
from jax.sharding import PartitionSpec as P

HEADS = 16
STEP = 10
EPSILON = 1e-05
MOMENTUM = 0.9
LEARNING_RATES = (60.0, 480.0, 60.0, 60.0, 600.0)
WEIGHT_DECAY = 0.0001
CLIP_NORM = 1.0
MASK_FLOOR = -1e30
PLANE = 8
EXTRA = 8
LANES = 128
QUERY_TILE = 512
KEY_TILE = 640
F32 = jnp.float32
LOW = jnp.bfloat16
WHOLE = pl.BlockSpec()
SMEM = pl.BlockSpec(memory_space=pltpu.SMEM)


def like(shape, dtype):
    return jax.ShapeDtypeStruct(shape, dtype)


def kernel_call(body, outs, *args, scalars=(), scratch=(), flops=0, limit=60):
    moved = sum(a.size * a.dtype.itemsize for a in list(args) + list(outs))
    return pl.pallas_call(
        body,
        in_specs=[SMEM] * len(scalars) + [WHOLE] * len(args),
        out_specs=[WHOLE] * len(outs),
        out_shape=list(outs),
        scratch_shapes=list(scratch),
        cost_estimate=pl.CostEstimate(flops=flops, bytes_accessed=moved, transcendentals=0),
        compiler_params=pltpu.CompilerParams(vmem_limit_bytes=limit << 20),
    )(*scalars, *args)


def after(value, *others):
    return lax.optimization_barrier((value, *others))[0]


def tie(*values):
    return lax.optimization_barrier(values)


def swap(block, bit):
    n = lax.axis_size("seq")
    return lax.ppermute(block, "seq", [(i, i ^ bit) for i in range(n)])


def move(block, distance):
    n = lax.axis_size("seq")
    return lax.ppermute(
        block, "seq", [(i, i + distance) for i in range(n) if 0 <= i + distance < n]
    )


def turn(block, planes_on):
    n = lax.axis_size("seq")
    return lax.ppermute(block, "seq", [(i, (i + planes_on * PLANE) % n) for i in range(n)])


def plane_groups():
    n = lax.axis_size("seq")
    return [[g * PLANE + j for j in range(PLANE)] for g in range(n // PLANE)]


def cross_groups():
    n = lax.axis_size("seq")
    return [[g * PLANE + j for g in range(n // PLANE)] for j in range(PLANE)]


def exchange(blocks, groups=None):
    return lax.all_to_all(blocks, "seq", 0, 0, axis_index_groups=groups)


def spread_sides(block):
    return swap(block, 2), swap(block, 4)


def spread_corner(across, along):
    half = across.shape[0] // 2
    return swap(across[:half], 4), swap(along[half:], 2)


def grow(block, bit):
    return jnp.concatenate([block, swap(block, bit)], axis=0)


def spread_far(block, sides, corner):
    far = swap(jnp.stack([block, *sides]), 1)
    return [block, *sides, *corner, far, *[swap(c, 1) for c in corner]]


def spread(block):
    sides = spread_sides(block)
    return spread_far(block, sides, spread_corner(*sides))


SPREAD = 8


def join(refs, out):
    number = refs[0].shape[0]
    place = 0
    for ref in refs:
        if len(ref.shape) == 3:
            for m in range(ref.shape[0]):
                out[pl.ds(place, number), :] = ref[m]
                place += number
        else:
            out[pl.ds(place, ref.shape[0]), :] = ref[...]
            place += ref.shape[0]


def collect(near, far, far_corner):
    return collect_came(near, swap(far_corner, 1), swap(far, 1))


def collect_came(near, came_corner, came):
    half = near.shape[1] // 2
    corner = (near[3] + came_corner.astype(F32)).astype(LOW)
    by_across = swap(corner[:half], 2).astype(F32)
    by_along = swap(corner[half:], 4).astype(F32)
    across = near[1] + came[1].astype(F32)
    along = near[2] + came[2].astype(F32)
    across = jnp.concatenate([across[:half], across[half:] + by_along], axis=0).astype(LOW)
    along = jnp.concatenate([along[:half] + by_across, along[half:]], axis=0).astype(LOW)
    return near[0] + came[0].astype(F32), swap(across, 2), swap(along, 4)


def put_block(outs, k, m, value):
    if k == 0:
        outs[0][m] = value
    elif m < 3:
        outs[1][m] = value.astype(LOW)
    else:
        outs[2][...] = value.astype(LOW)


def total(terms):
    return terms[0] + terms[1].astype(F32) + terms[2].astype(F32)


def norm_parts(values):
    centre = values - jnp.mean(values, axis=-1, keepdims=True)
    spread_of = jnp.mean(centre * centre, axis=-1, keepdims=True)
    inverse = lax.rsqrt(spread_of + EPSILON)
    return centre * inverse, inverse


def norm_back(unit, inverse, gain, incoming):
    scaled = incoming * gain
    return inverse * (
        scaled
        - jnp.mean(scaled, axis=-1, keepdims=True)
        - unit * jnp.mean(scaled * unit, axis=-1, keepdims=True)
    )


def dot(a, b, dims=((1,), (0,))):
    return lax.dot_general(a, b, (dims, ((), ())), preferred_element_type=F32)


NT = ((1,), (1,))
TN = ((0,), (0,))


def block_rows(place, number):
    return pl.ds(pl.multiple_of(place * number, number), number)


def gather_planes(plane, refs, out):
    planes = len(refs)
    rows = refs[0].shape[0]
    for s, ref in enumerate(refs):
        out[block_rows(lax.rem(plane - s + planes, planes), rows), :] = ref[...]


def project_kernel(spot_ref, *refs):
    token_refs, refs = refs[:SPREAD], refs[SPREAD:]
    sent_ref, lots_ref, unit_ref, first_ref, query_ref, pair_ref, weight_ref, vector_ref, held = refs
    spot = spot_ref[0]
    number, columns = token_refs[0].shape
    devices = sent_ref.shape[0]
    rows = columns // devices
    for d in range(devices):
        weight_ref[pl.ds(d * rows, rows), :] = sent_ref[d, :rows, :]
    for g in range(lots_ref.shape[0]):
        lanes = slice(g * LANES, (g + 1) * LANES)
        vector_ref[:EXTRA, lanes] = lots_ref[g, :, :LANES]
        vector_ref[EXTRA:, lanes] = lots_ref[g, :, LANES : 2 * LANES]
    join(token_refs, held)
    gain, shift = vector_ref[0:1, :], vector_ref[1:2, :]
    for r in range(PLANE):
        here = pl.ds(r * number, number)
        unit, _ = norm_parts(held[here, :].astype(F32))
        first = (unit * gain + shift).astype(LOW)
        unit_ref[here, :] = unit.astype(LOW)
        held[here, :] = first
        first_ref[block_rows(spot ^ relative(r), number), :] = first
    joined = dot(held[...], weight_ref[...]).astype(LOW)
    wide = query_ref.shape[1]
    for r in range(PLANE):
        here = slice(r * number, (r + 1) * number)
        query_ref[block_rows(spot ^ relative(r), number), :] = joined[here, :wide]
        pair_ref[block_rows(spot ^ relative(r), number), :] = joined[here, wide:]


def relative(r):
    return 2 * (r % 4) + r // 4


def head_part(array, head):
    lanes = lax.broadcasted_iota(jnp.int32, array.shape, len(array.shape) - 1)
    return jnp.where(lanes // 64 == head, array, jnp.zeros_like(array))


def scene_marks(bound_ref, first, count, inside, outside):
    place = first + lax.broadcasted_iota(jnp.int32, (count, LANES), 0)
    here = (place >= bound_ref[0:1, :]) & (place < bound_ref[1:2, :])
    return jnp.where(here, inside, outside).astype(LOW)


def marked_queries(bound_ref, query_ref, first):
    queries = query_ref[...] * jnp.asarray(0.125, LOW)
    marks = scene_marks(bound_ref, first, queries.shape[0], MASK_FLOOR, 0.0)
    return [jnp.concatenate([head_part(queries, h), marks], axis=1) for h in range(2)]


def marked_keys(bound_ref, refs, keys):
    tokens = refs[0].shape[0]
    for place, ref in enumerate(refs):
        keys[pl.ds(place * tokens, tokens), :LANES] = ref[:, :LANES]
        keys[pl.ds(place * tokens, tokens), LANES:] = scene_marks(bound_ref, place * tokens, tokens, 0.0, 1.0)
    keys[3 * tokens :, :LANES] = jnp.zeros((keys.shape[0] - 3 * tokens, LANES), LOW)
    keys[3 * tokens :, LANES:] = jnp.ones((keys.shape[0] - 3 * tokens, LANES), LOW)


def attend_kernel(
    range_ref, query_ref, before_ref, own_ref, after_ref, bound_ref, mixed_ref, low_ref, log_ref, keys, values
):
    step = pl.program_id(0)
    tokens = own_ref.shape[0]
    here = query_ref.shape[0]

    @pl.when(step == 0)
    def _():
        refs = (before_ref, own_ref, after_ref)
        marked_keys(bound_ref, refs, keys)
        for place, ref in enumerate(refs):
            values[:, pl.ds(place * tokens, tokens)] = ref[:, LANES:].T
        values[:, 3 * tokens :] = jnp.zeros((LANES, values.shape[1] - 3 * tokens), LOW)

    queries = marked_queries(bound_ref, query_ref, tokens + step * here)
    origin = range_ref[0, step] * LANES

    def body(index, carry):
        start = pl.multiple_of(origin + index * KEY_TILE, LANES)
        block = keys[pl.ds(start, KEY_TILE), :]
        out = []
        for h in range(2):
            peak, whole, mixed = carry[h]
            scores = dot(block, queries[h], NT)
            raised_peak = jnp.maximum(peak, jnp.max(scores, axis=0, keepdims=True))
            raised = jnp.exp(scores - raised_peak)
            fade = jnp.exp(peak - raised_peak)
            whole = whole * fade + jnp.sum(raised, axis=0, keepdims=True)
            turned = values[64 * h : 64 * h + 64, pl.ds(start, KEY_TILE)]
            mixed = mixed * fade + dot(turned, raised.astype(LOW))
            out.append((raised_peak, whole, mixed))
        return tuple(out)

    init = tuple(
        (jnp.full((1, here), MASK_FLOOR, F32), jnp.zeros((1, here), F32), jnp.zeros((64, here), F32))
        for _ in range(2)
    )
    done = lax.fori_loop(0, range_ref[1, step], body, init)
    mixed = jnp.concatenate([m / t for _, t, m in done], axis=0).T
    mixed_ref[...] = mixed
    low_ref[...] = mixed.astype(LOW)
    log_ref[...] = jnp.concatenate([k + jnp.log(t) for k, t, _ in done], axis=0)


def attend_back_kernel(
    range_ref,
    query_ref,
    before_ref,
    own_ref,
    after_ref,
    bound_ref,
    mixed_ref,
    log_ref,
    grad_ref,
    query_grad_ref,
    before_grad_ref,
    own_grad_ref,
    after_grad_ref,
    keys,
    values,
    turned_keys,
    key_grad,
    value_grad,
):
    step = pl.program_id(0)
    tokens = own_ref.shape[0]
    here = query_ref.shape[0]

    @pl.when(step == 0)
    def _():
        refs = (before_ref, own_ref, after_ref)
        marked_keys(bound_ref, refs, keys)
        for place, ref in enumerate(refs):
            values[pl.ds(place * tokens, tokens), :] = ref[:, LANES:]
            turned_keys[:, pl.ds(place * tokens, tokens)] = ref[:, :LANES].T
        values[3 * tokens :, :] = jnp.zeros((values.shape[0] - 3 * tokens, LANES), LOW)
        turned_keys[:, 3 * tokens :] = jnp.zeros((LANES, values.shape[0] - 3 * tokens), LOW)
        key_grad[...] = jnp.zeros_like(key_grad)
        value_grad[...] = jnp.zeros_like(value_grad)

    queries = marked_queries(bound_ref, query_ref, tokens + step * here)
    grads = grad_ref[...]
    split_grads = [head_part(grads, h) for h in range(2)]
    product = (grads.astype(F32) * mixed_ref[...]).T
    centred = [jnp.sum(product[64 * h : 64 * h + 64], axis=0, keepdims=True) for h in range(2)]
    origin = range_ref[0, step] * LANES

    def body(index, carry):
        start = pl.multiple_of(origin + index * KEY_TILE, LANES)
        rows = pl.ds(start, KEY_TILE)
        out, key_part, value_part = [], 0, 0
        for h in range(2):
            shares = jnp.exp(dot(keys[rows, :], queries[h], NT) - log_ref[h : h + 1, :])
            value_part += dot(shares.astype(LOW), split_grads[h])
            share_grad = dot(values[rows, :], split_grads[h], NT)
            score_grad = (shares * (share_grad - centred[h])).astype(LOW)
            key_part += dot(score_grad, queries[h][:, :LANES])
            out.append(carry[h] + dot(turned_keys[64 * h : 64 * h + 64, rows], score_grad))
        key_grad[rows, :] += key_part
        value_grad[rows, :] += value_part
        return tuple(out)

    init = tuple(jnp.zeros((64, here), F32) for _ in range(2))
    done = lax.fori_loop(0, range_ref[1, step], body, init)
    query_grad_ref[...] = (jnp.concatenate(done, axis=0).T * 0.125).astype(LOW)

    @pl.when(step == pl.num_programs(0) - 1)
    def _():
        for place, ref in enumerate((before_grad_ref, own_grad_ref, after_grad_ref)):
            ref[:, :LANES] = key_grad[pl.ds(place * tokens, tokens), :].astype(ref.dtype)
            ref[:, LANES:] = value_grad[pl.ds(place * tokens, tokens), :].astype(ref.dtype)


def key_ranges(spans, query_tile, key_tile):
    first = spans[0, ::query_tile] // LANES
    return jnp.stack([first, (spans[1, query_tile - 1 :: query_tile] - first * LANES + key_tile - 1) // key_tile])


def attention(spans, bounds, queries, before, own, behind):
    tokens, wide = queries.shape
    whole = lambda shape: pl.BlockSpec(shape, lambda i, s: (0, 0))
    tile = pl.BlockSpec((QUERY_TILE, wide), lambda i, s: (i, 0))
    row = pl.BlockSpec((2, QUERY_TILE), lambda i, s: (0, i))
    window = 3 * tokens + KEY_TILE
    return pl.pallas_call(
        attend_kernel,
        grid_spec=pltpu.PrefetchScalarGridSpec(
            num_scalar_prefetch=1,
            grid=(tokens // QUERY_TILE,),
            in_specs=[tile] + [whole((tokens, 2 * wide))] * 3 + [whole(bounds.shape)],
            out_specs=[tile, tile, row],
            scratch_shapes=[pltpu.VMEM((window, 2 * wide), LOW), pltpu.VMEM((wide, window), LOW)],
        ),
        out_shape=[like((tokens, wide), F32), like((tokens, wide), LOW), like((2, tokens), F32)],
        cost_estimate=pl.CostEstimate(
            flops=40 * tokens * tokens * wide, bytes_accessed=16 * tokens * wide, transcendentals=2 * tokens * tokens
        ),
        compiler_params=pltpu.CompilerParams(vmem_limit_bytes=60 << 20),
    )(key_ranges(spans, QUERY_TILE, KEY_TILE), queries, before, own, behind, bounds)


def attention_back(spans, bounds, queries, before, own, behind, mixed, logs, grads):
    tokens, wide = queries.shape
    whole = lambda shape: pl.BlockSpec(shape, lambda i, s: (0, 0))
    tile = pl.BlockSpec((QUERY_TILE, wide), lambda i, s: (i, 0))
    row = pl.BlockSpec((2, QUERY_TILE), lambda i, s: (0, i))
    window = 3 * tokens + KEY_TILE
    return pl.pallas_call(
        attend_back_kernel,
        grid_spec=pltpu.PrefetchScalarGridSpec(
            num_scalar_prefetch=1,
            grid=(tokens // QUERY_TILE,),
            in_specs=[tile] + [whole((tokens, 2 * wide))] * 3 + [whole(bounds.shape), tile, row, tile],
            out_specs=[tile] + [whole((tokens, 2 * wide))] * 3,
            scratch_shapes=[
                pltpu.VMEM((window, 2 * wide), LOW),
                pltpu.VMEM((window, wide), LOW),
                pltpu.VMEM((wide, window), LOW),
                pltpu.VMEM((window, wide), F32),
                pltpu.VMEM((window, wide), F32),
            ],
        ),
        out_shape=[
            like((tokens, wide), LOW),
            like((tokens, 2 * wide), LOW),
            like((tokens, 2 * wide), F32),
            like((tokens, 2 * wide), LOW),
        ],
        cost_estimate=pl.CostEstimate(
            flops=60 * tokens * tokens * wide, bytes_accessed=32 * tokens * wide, transcendentals=2 * tokens * tokens
        ),
        compiler_params=pltpu.CompilerParams(vmem_limit_bytes=60 << 20),
    )(key_ranges(spans, QUERY_TILE, KEY_TILE), queries, before, own, behind, bounds, mixed, logs, grads)


def output_steps(planes):
    return [PLANE << i for i in range(planes.bit_length() - 1)] + [4, 2, 1]


def step_bits(index, steps):
    return sum(bit for i, bit in enumerate(steps) if index >> i & 1)


def place_output(planes, place_ref, refs, out):
    if len(refs) == 1:
        out[...] = refs[0][...]
        return
    devices = PLANE * planes
    rows = out.shape[0] // devices
    steps = output_steps(planes)
    device = place_ref[1] * PLANE + place_ref[0]
    for k, ref in enumerate(refs):
        for i in range(devices // 2):
            bits = step_bits(k * devices // 2 + i, steps)
            out[block_rows(device ^ bits, rows), :] = ref[pl.ds(i * rows, rows), :]


def ordered_output(device, planes, refs):
    devices = PLANE * planes
    rows = 2 * refs[0].shape[0] // devices
    if rows % 16 == 0:
        return refs
    whole = jnp.concatenate(refs, axis=0).reshape(devices, rows, -1)
    steps = output_steps(planes)
    bits = jnp.array([step_bits(i, steps) for i in range(devices)], jnp.int32)
    return [jnp.zeros_like(whole).at[device ^ bits].set(whole).reshape(devices * rows, -1)]


def mix_out_kernel(planes, place_ref, mixed_ref, tokens_ref, vector_ref, *refs):
    output_refs, (second_ref, normed_ref, output) = refs[:-3], refs[-3:]
    place_output(planes, place_ref, output_refs, output)
    mixed = jnp.concatenate([mixed_ref[j] for j in range(PLANE)], axis=1)
    second = tokens_ref[...].astype(F32) + dot(mixed, output[...])
    second_ref[...] = second
    unit, _ = norm_parts(second)
    normed_ref[...] = (unit * vector_ref[2:3, :] + vector_ref[3:4, :]).astype(LOW)


def feed_kernel(planes, place_ref, *refs):
    normed_refs, refs = refs[:SPREAD], refs[SPREAD:]
    cot_refs, refs = refs[:2], refs[2:]
    shrink_refs, refs = refs[:planes], refs[planes:]
    expand_refs, refs = refs[:2], refs[2:]
    bias_ref, near_out, far_out, corner_out, active_ref, grad_ref, bias_out, expand, shrink, x, c = refs
    part = expand.shape[1] // 2
    expand[:, :part] = expand_refs[0][...]
    expand[:, part:] = expand_refs[1][...]
    gather_planes(place_ref[1], shrink_refs, shrink)
    join(normed_refs, x)
    join(cot_refs, c)
    number = near_out.shape[1]
    sums = jnp.zeros(bias_ref.shape, F32)
    for k, m in ((1, 2), (1, 0), (0, 2), (0, 0)):
        rows = pl.ds((4 * k + m) * number, 2 * number)
        upper = dot(x[rows, :], expand[...]) + bias_ref[...]
        share = 0.5 + 0.5 * lax.erf(upper * 0.7071067811865476)
        density = 0.3989422804014327 * jnp.exp(-0.5 * upper * upper)
        active_ref[rows, :] = (upper * share).astype(LOW)
        grad = (dot(c[rows, :], shrink[...], NT) * (share + upper * density)).astype(LOW)
        grad_ref[rows, :] = grad
        sums += jnp.sum(grad.astype(F32), axis=0, keepdims=True)
        down = dot(grad, expand[...], NT)
        put_block((near_out, far_out, corner_out), k, m, down[:number])
        put_block((near_out, far_out, corner_out), k, m + 1, down[number:])
    bias_out[...] = sums


def plane_blocks(plane, whole, outs):
    planes = len(outs)
    tall = whole.shape[0] // planes
    for s, out in enumerate(outs):
        out[...] = whole[block_rows(lax.rem(plane + s, planes), tall), :].astype(out.dtype)


def shrink_grad_kernel(place_ref, active_ref, *refs):
    cot_refs, outs, (whole, cotangents) = refs[:2], refs[2:-2], refs[-2:]
    join(cot_refs, cotangents)
    whole[...] = dot(active_ref[...], cotangents[...], TN)
    plane_blocks(place_ref[1], whole, outs)


def expand_grad_kernel(grad_ref, *refs):
    normed_refs, (out_ref, normed) = refs[:SPREAD], refs[SPREAD:]
    join(normed_refs, normed)
    out_ref[...] = dot(normed[...], grad_ref[...], TN).astype(LOW)


def norm_two_back_kernel(
    planes, place_ref, one_ref, two_ref, three_ref, second_ref, cotangent_ref, vector_ref, *refs
):
    output_refs, (second_grad_ref, branch_ref, mixed_ref, sums_ref, output) = refs[:-5], refs[-5:]
    place_output(planes, place_ref, output_refs, output)
    incoming = one_ref[...] + two_ref[...].astype(F32) + three_ref[...].astype(F32)
    unit, inverse = norm_parts(second_ref[...])
    cotangent = cotangent_ref[...].astype(F32)
    second_grad = cotangent + norm_back(unit, inverse, vector_ref[2:3, :], incoming)
    second_grad_ref[...] = second_grad
    branch = second_grad.astype(LOW)
    branch_ref[...] = branch
    mixed = dot(branch, output[...], NT).astype(LOW)
    wide = mixed_ref.shape[2]
    for j in range(PLANE):
        mixed_ref[j] = mixed[:, wide * j : wide * j + wide]
    sums_ref[...] = jnp.concatenate(
        [
            jnp.sum(incoming * unit, axis=0, keepdims=True),
            jnp.sum(incoming, axis=0, keepdims=True),
            jnp.sum(cotangent, axis=0, keepdims=True),
        ],
        axis=0,
    )


def output_grad_kernel(place_ref, mixed_ref, *refs):
    branch_refs, outs, (whole, left, right) = refs[:2], refs[2:-3], refs[-3:]
    join(branch_refs, right)
    number = right.shape[0] // PLANE
    for r in range(PLANE):
        left[pl.ds(r * number, number), :] = mixed_ref[block_rows(place_ref[0] ^ relative(r), number), :]
    whole[...] = dot(left[...], right[...], TN)
    if len(outs) == 1:
        outs[0][...] = whole[...].astype(LOW)
    else:
        plane_blocks(place_ref[1], whole, outs)


def first_back_kernel(
    planes, place_ref, own_ref, from_after_ref, from_before_ref, query_ref, first_ref, unit_ref,
    weight, two_sums_ref, up_sums_ref, active_ref, *refs
):
    shrink_refs, (grad_ref, near_ref, far_ref, corner_ref, sums_ref, joined, vectors, shrink) = refs[:planes], refs[planes:]
    gather_planes(place_ref[1], shrink_refs, shrink)
    spot = place_ref[0]
    number, columns = near_ref.shape[1] // 2, near_ref.shape[2]
    wide = query_ref.shape[1]
    pairs = (own_ref[...] + from_after_ref[...].astype(F32) + from_before_ref[...].astype(F32)).astype(LOW)
    joined[:, :wide] = query_ref[...]
    joined[:, wide:] = pairs
    grad = dot(first_ref[...], joined[...], TN).astype(LOW)
    gain = jnp.zeros((1, columns), F32)
    shift = jnp.zeros((1, columns), F32)
    for k, m in ((1, 2), (1, 0), (0, 2), (0, 0)):
        part = jnp.concatenate(
            [joined[block_rows(spot ^ (2 * (m + i) + k), number), :] for i in range(2)], axis=0
        )
        down = dot(part, weight[...], NT)
        unit = unit_ref[pl.ds((4 * k + m) * number, 2 * number), :].astype(F32)
        gain += jnp.sum(down * unit, axis=0, keepdims=True)
        shift += jnp.sum(down, axis=0, keepdims=True)
        lower = dot(active_ref[pl.ds((4 * k + m) * number, 2 * number), :], shrink[...])
        outs = (near_ref, far_ref, corner_ref)
        put_block(outs, k, m, jnp.concatenate([down[:number], lower[:number]], axis=0))
        put_block(outs, k, m + 1, jnp.concatenate([down[number:], lower[number:]], axis=0))
    sums_ref[...] = jnp.concatenate([gain, shift], axis=0)
    if len(grad_ref.shape) == 2:
        grad_ref[...] = grad
        return
    devices, tall, _ = grad_ref.shape
    rows = tall - EXTRA
    vectors[...] = jnp.zeros_like(vectors)
    vectors[0:2, :] = sums_ref[...]
    vectors[2:5, :] = two_sums_ref[...]
    for g in range(up_sums_ref.shape[1] // LANES):
        lanes = pl.ds(pl.multiple_of(spot * LANES, LANES), LANES)
        vectors[5 + g : 6 + g, lanes] = up_sums_ref[:, g * LANES : (g + 1) * LANES]
    grad_ref[:, rows:, :] = jnp.zeros((devices, EXTRA, grad_ref.shape[2]), LOW)
    for d in range(devices):
        lot = slice(d * rows // LANES * LANES, (d * rows // LANES + 1) * LANES)
        grad_ref[d, :rows, :] = grad[d * rows : (d + 1) * rows]
        grad_ref[d, rows:, :LANES] = vectors[:EXTRA, lot].astype(LOW)
        grad_ref[d, rows:, LANES : 2 * LANES] = vectors[EXTRA:, lot].astype(LOW)


def first_norm_back_kernel(one_ref, two_ref, three_ref, tokens_ref, second_grad_ref, vector_ref, out_ref):
    incoming = one_ref[...] + two_ref[...].astype(F32) + three_ref[...].astype(F32)
    unit, inverse = norm_parts(tokens_ref[...].astype(F32))
    out_ref[...] = (second_grad_ref[...] + norm_back(unit, inverse, vector_ref[0:1, :], incoming)).astype(LOW)


def sum_kernel(wide, with_vectors, square_ref, *refs):
    part_ref, grad_ref, total_ref = refs[:3]
    devices = part_ref.shape[0]
    rows = grad_ref.shape[0]
    square = jnp.zeros((rows, wide), F32)
    start = 0
    for c in range(part_ref.shape[2] // wide):
        for j in range(PLANE):
            sources = range(j, devices, PLANE)
            whole = sum(part_ref[d, :rows, c * wide : (c + 1) * wide].astype(F32) for d in sources)
            grad_ref[:, start : start + wide] = whole
            square += whole * whole
            start += wide
    found = jnp.sum(square, keepdims=True) + square_ref[0]
    if with_vectors:
        vectors = sum(part_ref[d, rows:, : 2 * LANES].astype(F32) for d in range(devices))
        refs[3][:EXTRA, :] = vectors[:, :LANES]
        refs[3][EXTRA:, :] = vectors[:, LANES:]
        lanes = lax.broadcasted_iota(jnp.int32, (2 * EXTRA, LANES), 1)
        mine = lanes // rows == square_ref[1].astype(jnp.int32)
        found += jnp.sum(jnp.where(mine, refs[3][...] * refs[3][...], 0.0), keepdims=True)
    total_ref[...] = jnp.broadcast_to(found.reshape((1,) * len(total_ref.shape)), total_ref.shape)


def sum_parts(wide, rows, part, square, lot=None):
    n, _, columns = part.shape
    vectors = lot is not None
    if wide % LANES == 0 and rows % 16 == 0:
        outs = [like((rows, PLANE * columns), F32), like((n, 1, LANES) if vectors else (1, 1), F32)]
        found = kernel_call(
            functools.partial(sum_kernel, wide, vectors),
            outs + [like((2 * EXTRA, LANES), F32)] * vectors,
            part,
            scalars=(jnp.stack([square, lot.astype(F32) if vectors else square]),),
        )
        return found if vectors else (*found, None)
    whole = part[:, :rows].astype(F32).reshape(-1, PLANE, rows, columns // wide, wide).sum(0)
    whole = whole.transpose(1, 2, 0, 3).reshape(rows, -1)
    square = square + jnp.sum(whole * whole)
    if not vectors:
        return whole, square.reshape(1, 1), None
    found = part[:, rows:, : 2 * LANES].astype(F32).sum(0)
    found = jnp.concatenate([found[:, :LANES], found[:, LANES:]], axis=0)
    mine = lax.dynamic_slice_in_dim(found, rows * lot, rows, axis=1)
    square = square + jnp.sum(mine * mine)
    return whole, jnp.full((n, 1, LANES), square), found


def update_kernel(square_ref, *refs):
    norm = jnp.sqrt(jnp.sum(square_ref[...], axis=0)[:, :1])
    refs[-1][...] = norm
    refs = refs[:-1]
    factor = jnp.minimum(1.0, CLIP_NORM / (norm + 1e-06))
    smooth_rate = min(0.999, (1.0 + STEP) / (10.0 + STEP))
    count = len(LEARNING_RATES)
    states, grads, outs = refs[: 3 * count], refs[3 * count : 4 * count], refs[4 * count :]
    for place, rate in enumerate(LEARNING_RATES):
        weight, moment, average = (ref[...] for ref in states[3 * place : 3 * place + 3])
        clipped = factor * grads[place][...] + WEIGHT_DECAY * weight
        velocity = MOMENTUM * moment + clipped
        updated = weight - rate * (clipped + MOMENTUM * velocity)
        outs[3 * place][...] = velocity
        outs[3 * place + 1][...] = updated
        outs[3 * place + 2][...] = smooth_rate * average + (1.0 - smooth_rate) * updated


def with_vectors(attend_grad, one_sums, two_sums, up_sums, spot, n, rows, hidden):
    columns, wide = attend_grad.shape
    planes, lots, in_lot = n // PLANE, columns // LANES, LANES // rows
    up_sums = lax.dynamic_update_slice_in_dim(
        jnp.zeros((planes, PLANE, hidden), F32), up_sums.reshape(planes, 1, hidden), spot, axis=1
    )
    part = jnp.concatenate([one_sums, two_sums, up_sums.reshape(-1, columns)], axis=0).astype(LOW)
    part = jnp.moveaxis(part.reshape(-1, lots, LANES), 1, 0)
    part = jnp.pad(part, ((0, 0), (0, 2 * EXTRA - part.shape[1]), (0, 0)))
    part = jnp.concatenate([part[:, :EXTRA], part[:, EXTRA:]], axis=2)
    part = jnp.pad(part, ((0, 0), (0, 0), (0, wide - 2 * LANES)))
    return jnp.concatenate([attend_grad.reshape(n, rows, wide), jnp.repeat(part, in_lot, axis=0)], axis=1)


def on_device(
    tokens,
    scene_lengths,
    cotangent,
    attend_weight,
    output_weight,
    expand_weight,
    reduce_weight,
    vector_params,
    attend_momentum,
    output_momentum,
    expand_momentum,
    reduce_momentum,
    vector_momentum,
    attend_average,
    output_average,
    expand_average,
    reduce_average,
    vector_average,
):
    n = lax.axis_size("seq")
    planes = n // PLANE
    device = lax.axis_index("seq")
    plane, spot = device // PLANE, device % PLANE
    place = jnp.stack([spot, plane]).astype(jnp.int32)
    number, columns = tokens.shape
    shared = number * PLANE
    rows = columns // n
    hidden = reduce_weight.shape[0]
    wide = columns // PLANE
    lots = columns // LANES
    in_lot = LANES // rows
    inner = planes * hidden
    near_like, far_like = like((4, number, columns), F32), like((3, number, columns), LOW)
    block_like, block_exact = like((number, columns), LOW), like((number, columns), F32)
    shared_scratch = pltpu.VMEM((shared, columns), LOW)
    square_scratch = pltpu.VMEM((columns, columns), LOW)

    vector_low = vector_params.astype(LOW)
    sides = spread_sides(tokens)
    attend = attend_weight.astype(LOW).reshape(rows, 3, PLANE, wide).transpose(2, 0, 1, 3).reshape(PLANE, rows, 3 * wide)
    vector_part = lax.dynamic_update_slice(
        jnp.zeros((2 * EXTRA, LANES), LOW), vector_low, (0, rows * (device % in_lot))
    )
    vector_part = jnp.concatenate([vector_part[:EXTRA], vector_part[EXTRA:]], axis=1)
    vector_part = jnp.pad(vector_part, ((0, 0), (0, 3 * wide - 2 * LANES)))
    attend = jnp.concatenate(
        [
            jnp.broadcast_to(attend[None], (planes,) + attend.shape).reshape(n, rows, 3 * wide),
            jnp.broadcast_to(vector_part[None], (n,) + vector_part.shape),
        ],
        axis=1,
    )
    attend = exchange(after(attend, *sides))
    lot_vectors = attend[:, rows:].reshape(lots, in_lot, EXTRA, 3 * wide).astype(F32).sum(1)
    corner = spread_corner(*sides)
    output = after(output_weight.astype(LOW), *sides)
    for bit in output_steps(planes)[:-3]:
        output = grow(output, bit)
    expand = (
        expand_weight.astype(LOW)
        .reshape(rows, planes, PLANE, hidden)
        .transpose(2, 0, 1, 3)
        .reshape(PLANE, rows, inner)
    )
    expand = jnp.broadcast_to(expand[None], (planes,) + expand.shape).reshape(n, rows, inner)
    expand = [expand[:, :, : inner // 2], expand[:, :, inner // 2 :]]
    shrink = reduce_weight.astype(LOW)
    corner, expand, shrink = tie(corner, expand, shrink)
    gathered = spread_far(tokens, sides, corner)
    gathered, output = tie(gathered, output)

    units, first_low, queries, pairs, attend, vectors = kernel_call(
        project_kernel,
        [
            like((shared, columns), LOW),
            like((shared, columns), LOW),
            like((shared, wide), LOW),
            like((shared, 2 * wide), LOW),
            like((columns, 3 * wide), LOW),
            like((2 * EXTRA, columns), F32),
        ],
        *gathered,
        attend,
        lot_vectors,
        scalars=(place,),
        scratch=[shared_scratch],
        flops=6 * shared * columns * wide,
    )
    bias_up = lax.dynamic_index_in_dim(
        vectors[5 : vector_params.shape[0]].reshape(planes, PLANE, hidden), spot, axis=1, keepdims=False
    ).reshape(1, inner)

    before, behind = move(pairs, PLANE), move(pairs, -PLANE)
    expand[0] = exchange(after(expand[0], pairs)).reshape(columns, inner // 2)
    output = grow(after(output, pairs), 4)
    cotangents = grow(after(cotangent, pairs), 2)
    queries, output, cotangents = tie(queries, output, cotangents)

    finish = jnp.cumsum(scene_lengths)
    begin = finish - scene_lengths
    base = (plane - 1) * shared
    position = plane * shared + jnp.arange(shared, dtype=jnp.int32)
    past = begin[None, :] <= position[:, None]
    span_begin = jnp.max(jnp.where(past, begin[None, :], 0), axis=1) - base
    span_end = jnp.min(jnp.where(finish[None, :] > position[:, None], finish[None, :], 1 << 30), axis=1) - base
    spans = jnp.stack([span_begin, span_end])
    bounds = jnp.stack([begin, finish]) - base
    bounds = jnp.pad(bounds, ((0, 0), (0, LANES - bounds.shape[1])))
    output = grow(output, 2)
    cotangents = grow(cotangents, 4)
    shrink_turns = {1: turn(after(shrink, queries), 1)}
    mixed_exact, mixed_low, logs = attention(spans, bounds, queries, before, pairs, behind)
    mixed_low, output, cotangents, expand[0], shrink_turns = tie(
        mixed_low, output, cotangents, expand[0], shrink_turns
    )

    mixed = exchange(mixed_low.reshape(PLANE, number, wide), plane_groups())
    output = [output, swap(output, 1)]
    cotangents = [cotangents, swap(cotangents, 1)]
    shrink_turns.update({s: turn(after(shrink, mixed_low), s) for s in range(2, planes)})
    output = ordered_output(device, planes, output)
    second, normed = kernel_call(
        functools.partial(mix_out_kernel, planes),
        [block_exact, block_like],
        mixed,
        tokens,
        vectors,
        *output,
        scalars=(place,),
        scratch=[square_scratch],
        flops=2 * number * columns * columns,
    )

    expand[1] = exchange(after(expand[1], mixed)).reshape(columns, inner // 2)
    sides = spread_sides(normed)
    sides, shrink_turns, cotangents = tie(sides, shrink_turns, cotangents)
    corner = spread_corner(*sides)
    shrink = [shrink] + [shrink_turns[s] for s in range(1, planes)]
    normed_all = spread_far(normed, sides, corner)

    inner_low = like((shared, inner), LOW)
    grad_near, grad_far, grad_corner, active, upper_grad, up_sums = kernel_call(
        functools.partial(feed_kernel, planes),
        [near_like, far_like, block_like, inner_low, inner_low, like((1, inner), F32)],
        *normed_all,
        *cotangents,
        *shrink,
        *expand,
        bias_up,
        scalars=(place,),
        scratch=[pltpu.VMEM((columns, inner), LOW), pltpu.VMEM((inner, columns), LOW), shared_scratch, shared_scratch],
        flops=6 * shared * columns * inner,
    )

    normed_grad = collect(grad_near, grad_far, grad_corner)
    shrink_grad = kernel_call(
        shrink_grad_kernel,
        [like((hidden, columns), LOW)] * planes,
        active,
        *cotangents,
        scalars=(place,),
        scratch=[pltpu.VMEM((inner, columns), F32), shared_scratch],
        flops=2 * shared * columns * inner,
    )
    shrink_turns = [turn(shrink_grad[s], s) for s in range(1, planes)]
    normed_grad, shrink_turns[:1] = tie(normed_grad, shrink_turns[:1])
    second_grad, branch_grad, mixed_grad, two_sums = kernel_call(
        functools.partial(norm_two_back_kernel, planes),
        [block_exact, block_like, like((PLANE, number, wide), LOW), like((3, columns), F32)],
        *normed_grad,
        second,
        cotangent,
        vectors,
        *output,
        scalars=(place,),
        scratch=[square_scratch],
        flops=2 * number * columns * columns,
    )

    mixed_grad = exchange(mixed_grad, plane_groups()).reshape(shared, wide)
    (expand_grad,) = kernel_call(
        expand_grad_kernel,
        [like((columns, inner), LOW)],
        after(upper_grad, branch_grad),
        *normed_all,
        scratch=[shared_scratch],
        flops=2 * shared * columns * inner,
    )
    branch_sides = spread_sides(branch_grad)
    mixed_grad, expand_grad, branch_sides, shrink_turns[:2] = tie(
        mixed_grad, expand_grad, branch_sides, shrink_turns[:2]
    )

    expand_part = exchange(after(expand_grad, mixed_grad).reshape(n, rows, inner))
    branch_corner = spread_corner(*branch_sides)
    query_grad, before_grad, own_grad, behind_grad = attention_back(
        spans, bounds, queries, before, pairs, behind, mixed_exact, logs, mixed_grad
    )
    before_grad, behind_grad, branch_corner = tie(before_grad, behind_grad, branch_corner)

    from_after, from_before = move(before_grad, -PLANE), move(behind_grad, PLANE)
    branch = jnp.concatenate([branch_grad, *branch_sides, *branch_corner], axis=0)
    output_grad = kernel_call(
        output_grad_kernel,
        [like((rows, columns), LOW)] * planes if rows % 16 == 0 else [like((wide, columns), LOW)],
        mixed_low,
        branch,
        swap(branch, 1),
        scalars=(place,),
        scratch=[pltpu.VMEM((wide, columns), F32), pltpu.VMEM((shared, wide), LOW), shared_scratch],
        flops=2 * shared * columns * wide,
    )
    if len(output_grad) == 1:
        output_grad = jnp.take(
            output_grad[0].reshape(planes, rows, columns), (plane + jnp.arange(planes)) % planes, axis=0, mode="clip"
        )
    output_grad = sum(
        lax.ppermute(
            output_grad[s],
            "seq",
            [(g * PLANE + j, j * planes + (g + s) % planes) for g in range(planes) for j in range(PLANE)],
        ).astype(F32)
        for s in range(planes)
    )
    from_after, from_before, output_grad = tie(from_after, from_before, output_grad)

    fused = rows % 16 == 0 and hidden == LANES
    attend_grad, first_near, first_far, first_corner, one_sums = kernel_call(
        functools.partial(first_back_kernel, planes),
        [
            like((n, rows + EXTRA, 3 * wide) if fused else (columns, 3 * wide), LOW),
            like((4, 2 * number, columns), F32),
            like((3, 2 * number, columns), LOW),
            like((2 * number, columns), LOW),
            like((2, columns), F32),
        ],
        own_grad,
        from_after,
        from_before,
        query_grad,
        first_low,
        units,
        attend,
        two_sums,
        up_sums,
        active,
        *shrink,
        scalars=(place,),
        scratch=[
            pltpu.VMEM((shared, 3 * wide), LOW),
            pltpu.VMEM((2 * EXTRA, columns), F32),
            pltpu.VMEM((inner, columns), LOW),
        ],
        flops=2 * shared * columns * 6 * wide,
    )
    more = vector_params.shape[0] - EXTRA
    attend_part = attend_grad
    if not fused:
        attend_part = with_vectors(attend_grad, one_sums, two_sums, up_sums, spot, n, rows, hidden)
    attend_part, first_near, first_far, first_corner, expand_part, shrink_turns = tie(
        attend_part, first_near, first_far, first_corner, expand_part, shrink_turns
    )
    shrink_grad = sum(g.astype(F32) for g in [shrink_grad[0], *shrink_turns])
    attend_part = exchange(attend_part)
    both = collect(first_near, first_far, first_corner)
    first_grad, block_output = zip(*[(t[:number], t[number:]) for t in both])
    (input_gradient,) = kernel_call(
        first_norm_back_kernel, [block_like], *first_grad, tokens, second_grad, vectors
    )
    block_output = (second + total(block_output) + vectors[4:5]).astype(LOW)

    squares = sum(jnp.sum(g * g) for g in (output_grad, shrink_grad))
    expand_grad, squares, _ = sum_parts(hidden, rows, expand_part, squares)
    attend_grad, squares, vector_grad = sum_parts(wide, rows, attend_part, squares[0, 0], device % in_lot)
    vector_grad = lax.dynamic_slice_in_dim(vector_grad, rows * (device % in_lot), rows, axis=1)
    vector_grad = vector_grad[: vector_params.shape[0]]
    squares, input_gradient, block_output = tie(exchange(squares), input_gradient, block_output)
    states = (
        (attend_weight, attend_momentum, attend_average),
        (output_weight, output_momentum, output_average),
        (expand_weight, expand_momentum, expand_average),
        (reduce_weight, reduce_momentum, reduce_average),
        (vector_params, vector_momentum, vector_average),
    )
    *updates, gradient_norm = kernel_call(
        update_kernel,
        [like(g[0].shape, F32) for g in states for _ in range(3)] + [like((1, 1), F32)],
        squares,
        *[a for g in states for a in g],
        attend_grad,
        output_grad,
        expand_grad,
        shrink_grad,
        vector_grad,
    )
    return (block_output, input_gradient, gradient_norm.reshape(()), *updates)


def solution(mesh):
    split, turned = P("seq", None), P(None, "seq")
    return jax.shard_map(
        on_device,
        mesh=mesh,
        in_specs=(split, P()) + (split,) * 5 + (turned,) + ((split,) * 4 + (turned,)) * 2,
        out_specs=(split, split, P()) + (split,) * 12 + (turned,) * 3,
        check_vma=False,
    )
```

```python
import functools

import jax
import jax.numpy as jnp
from jax import lax
from jax.experimental import pallas as pl
from jax.experimental.pallas import tpu as pltpu
from jax.sharding import PartitionSpec as P

HEADS = 16
STEP = 10
EPSILON = 1e-05
MOMENTUM = 0.9
LEARNING_RATES = (60.0, 480.0, 60.0, 60.0, 600.0)
WEIGHT_DECAY = 0.0001
CLIP_NORM = 1.0
MASK_FLOOR = -1e30
PLANE = 8
EXTRA = 8
LANES = 128
QUERY_TILE = 512
KEY_TILE = 640
F32 = jnp.float32
LOW = jnp.bfloat16
WHOLE = pl.BlockSpec()
SMEM = pl.BlockSpec(memory_space=pltpu.SMEM)


def like(shape, dtype):
    return jax.ShapeDtypeStruct(shape, dtype)


def kernel_call(body, outs, *args, scalars=(), scratch=(), flops=0, limit=56):
    moved = sum(a.size * a.dtype.itemsize for a in list(args) + list(outs))
    return pl.pallas_call(
        body,
        in_specs=[SMEM] * len(scalars) + [WHOLE] * len(args),
        out_specs=[WHOLE] * len(outs),
        out_shape=list(outs),
        scratch_shapes=list(scratch),
        cost_estimate=pl.CostEstimate(flops=flops, bytes_accessed=moved, transcendentals=0),
        compiler_params=pltpu.CompilerParams(vmem_limit_bytes=limit << 20),
    )(*scalars, *args)


def after(value, *others):
    return lax.optimization_barrier((value, *others))[0]


def tie(*values):
    return lax.optimization_barrier(values)


def swap(block, bit):
    n = lax.axis_size("seq")
    return lax.ppermute(block, "seq", [(i, i ^ bit) for i in range(n)])


def move(block, distance):
    n = lax.axis_size("seq")
    return lax.ppermute(
        block, "seq", [(i, i + distance) for i in range(n) if 0 <= i + distance < n]
    )


def turn(block, planes_on):
    n = lax.axis_size("seq")
    return lax.ppermute(block, "seq", [(i, (i + planes_on * PLANE) % n) for i in range(n)])


def plane_groups():
    n = lax.axis_size("seq")
    return [[g * PLANE + j for j in range(PLANE)] for g in range(n // PLANE)]


def cross_groups():
    n = lax.axis_size("seq")
    return [[g * PLANE + j for g in range(n // PLANE)] for j in range(PLANE)]


def exchange(blocks, groups=None):
    return lax.all_to_all(blocks, "seq", 0, 0, axis_index_groups=groups)


def spread_sides(block):
    return swap(block, 2), swap(block, 4)


def spread_corner(across, along):
    half = across.shape[0] // 2
    return swap(across[:half], 4), swap(along[half:], 2)


def grow(block, bit):
    return jnp.concatenate([block, swap(block, bit)], axis=0)


def spread_far(block, sides, corner):
    far = swap(jnp.stack([block, *sides]), 1)
    return [block, *sides, *corner, far, *[swap(c, 1) for c in corner]]


def spread(block):
    sides = spread_sides(block)
    return spread_far(block, sides, spread_corner(*sides))


SPREAD = 8


def join(refs, out):
    number = refs[0].shape[0]
    place = 0
    for ref in refs:
        if len(ref.shape) == 3:
            for m in range(ref.shape[0]):
                out[pl.ds(place, number), :] = ref[m]
                place += number
        else:
            out[pl.ds(place, ref.shape[0]), :] = ref[...]
            place += ref.shape[0]


def collect(near, far, far_corner):
    return collect_came(near, swap(far_corner, 1), swap(far, 1))


def collect_came(near, came_corner, came):
    half = near.shape[1] // 2
    corner = (near[3] + came_corner.astype(F32)).astype(LOW)
    by_across = swap(corner[:half], 2).astype(F32)
    by_along = swap(corner[half:], 4).astype(F32)
    across = near[1] + came[1].astype(F32)
    along = near[2] + came[2].astype(F32)
    across = jnp.concatenate([across[:half], across[half:] + by_along], axis=0).astype(LOW)
    along = jnp.concatenate([along[:half] + by_across, along[half:]], axis=0).astype(LOW)
    return near[0] + came[0].astype(F32), swap(across, 2), swap(along, 4)


def put_block(outs, k, m, value):
    if k == 0:
        outs[0][m] = value
    elif m < 3:
        outs[1][m] = value.astype(LOW)
    else:
        outs[2][...] = value.astype(LOW)


def total(terms):
    return terms[0] + terms[1].astype(F32) + terms[2].astype(F32)


def norm_parts(values):
    centre = values - jnp.mean(values, axis=-1, keepdims=True)
    spread_of = jnp.mean(centre * centre, axis=-1, keepdims=True)
    inverse = lax.rsqrt(spread_of + EPSILON)
    return centre * inverse, inverse


def norm_back(unit, inverse, gain, incoming):
    scaled = incoming * gain
    return inverse * (
        scaled
        - jnp.mean(scaled, axis=-1, keepdims=True)
        - unit * jnp.mean(scaled * unit, axis=-1, keepdims=True)
    )


def dot(a, b, dims=((1,), (0,))):
    return lax.dot_general(a, b, (dims, ((), ())), preferred_element_type=F32)


NT = ((1,), (1,))
TN = ((0,), (0,))


def block_rows(place, number):
    return pl.ds(pl.multiple_of(place * number, number), number)


def gather_planes(plane, refs, out):
    planes = len(refs)
    rows = refs[0].shape[0]
    for s, ref in enumerate(refs):
        out[block_rows(lax.rem(plane - s + planes, planes), rows), :] = ref[...]


def project_kernel(spot_ref, *refs):
    token_refs, refs = refs[:SPREAD], refs[SPREAD:]
    sent_ref, lots_ref, unit_ref, first_ref, query_ref, pair_ref, weight_ref, vector_ref, held = refs
    spot = spot_ref[0]
    number, columns = token_refs[0].shape
    devices = sent_ref.shape[0]
    rows = columns // devices
    for d in range(devices):
        weight_ref[pl.ds(d * rows, rows), :] = sent_ref[d, :rows, :]
    for g in range(lots_ref.shape[0]):
        lanes = slice(g * LANES, (g + 1) * LANES)
        vector_ref[:EXTRA, lanes] = lots_ref[g, :, :LANES]
        vector_ref[EXTRA:, lanes] = lots_ref[g, :, LANES : 2 * LANES]
    join(token_refs, held)
    gain, shift = vector_ref[0:1, :], vector_ref[1:2, :]
    for r in range(PLANE):
        here = pl.ds(r * number, number)
        unit, _ = norm_parts(held[here, :].astype(F32))
        first = (unit * gain + shift).astype(LOW)
        unit_ref[here, :] = unit.astype(LOW)
        held[here, :] = first
        first_ref[block_rows(spot ^ relative(r), number), :] = first
    joined = dot(held[...], weight_ref[...]).astype(LOW)
    wide = query_ref.shape[1]
    for r in range(PLANE):
        here = slice(r * number, (r + 1) * number)
        query_ref[block_rows(spot ^ relative(r), number), :] = joined[here, :wide]
        pair_ref[block_rows(spot ^ relative(r), number), :] = joined[here, wide:]


def relative(r):
    return 2 * (r % 4) + r // 4


def head_part(array, head):
    lanes = lax.broadcasted_iota(jnp.int32, array.shape, len(array.shape) - 1)
    return jnp.where(lanes // 64 == head, array, jnp.zeros_like(array))


def scene_marks(bound_ref, first, count, inside, outside):
    place = first + lax.broadcasted_iota(jnp.int32, (count, LANES), 0)
    here = (place >= bound_ref[0:1, :]) & (place < bound_ref[1:2, :])
    return jnp.where(here, inside, outside).astype(LOW)


def marked_queries(bound_ref, query_ref, first):
    queries = query_ref[...] * jnp.asarray(0.125, LOW)
    marks = scene_marks(bound_ref, first, queries.shape[0], MASK_FLOOR, 0.0)
    return [jnp.concatenate([head_part(queries, h), marks], axis=1) for h in range(2)]


def marked_keys(bound_ref, refs, keys):
    tokens = refs[0].shape[0]
    for place, ref in enumerate(refs):
        keys[pl.ds(place * tokens, tokens), :LANES] = ref[:, :LANES]
        keys[pl.ds(place * tokens, tokens), LANES:] = scene_marks(bound_ref, place * tokens, tokens, 0.0, 1.0)
    keys[3 * tokens :, :LANES] = jnp.zeros((keys.shape[0] - 3 * tokens, LANES), LOW)
    keys[3 * tokens :, LANES:] = jnp.ones((keys.shape[0] - 3 * tokens, LANES), LOW)


def attend_kernel(
    range_ref, query_ref, before_ref, own_ref, after_ref, bound_ref, mixed_ref, low_ref, log_ref, keys, values
):
    step = pl.program_id(0)
    tokens = own_ref.shape[0]
    here = query_ref.shape[0]

    @pl.when(step == 0)
    def _():
        refs = (before_ref, own_ref, after_ref)
        marked_keys(bound_ref, refs, keys)
        for place, ref in enumerate(refs):
            values[:, pl.ds(place * tokens, tokens)] = ref[:, LANES:].T
        values[:, 3 * tokens :] = jnp.zeros((LANES, values.shape[1] - 3 * tokens), LOW)

    queries = marked_queries(bound_ref, query_ref, tokens + step * here)
    origin = range_ref[0, step] * LANES

    def body(index, carry):
        start = pl.multiple_of(origin + index * KEY_TILE, LANES)
        block = keys[pl.ds(start, KEY_TILE), :]
        out = []
        for h in range(2):
            peak, whole, mixed = carry[h]
            scores = dot(block, queries[h], NT)
            raised_peak = jnp.maximum(peak, jnp.max(scores, axis=0, keepdims=True))
            raised = jnp.exp(scores - raised_peak)
            fade = jnp.exp(peak - raised_peak)
            whole = whole * fade + jnp.sum(raised, axis=0, keepdims=True)
            turned = values[64 * h : 64 * h + 64, pl.ds(start, KEY_TILE)]
            mixed = mixed * fade + dot(turned, raised.astype(LOW))
            out.append((raised_peak, whole, mixed))
        return tuple(out)

    init = tuple(
        (jnp.full((1, here), MASK_FLOOR, F32), jnp.zeros((1, here), F32), jnp.zeros((64, here), F32))
        for _ in range(2)
    )
    done = lax.fori_loop(0, range_ref[1, step], body, init)
    mixed = jnp.concatenate([m / t for _, t, m in done], axis=0).T
    mixed_ref[...] = mixed
    low_ref[...] = mixed.astype(LOW)
    log_ref[...] = jnp.concatenate([k + jnp.log(t) for k, t, _ in done], axis=0)


def attend_back_kernel(
    range_ref,
    query_ref,
    before_ref,
    own_ref,
    after_ref,
    bound_ref,
    mixed_ref,
    log_ref,
    grad_ref,
    query_grad_ref,
    before_grad_ref,
    own_grad_ref,
    after_grad_ref,
    keys,
    values,
    turned_keys,
    key_grad,
    value_grad,
):
    step = pl.program_id(0)
    tokens = own_ref.shape[0]
    here = query_ref.shape[0]

    @pl.when(step == 0)
    def _():
        refs = (before_ref, own_ref, after_ref)
        marked_keys(bound_ref, refs, keys)
        for place, ref in enumerate(refs):
            values[pl.ds(place * tokens, tokens), :] = ref[:, LANES:]
            turned_keys[:, pl.ds(place * tokens, tokens)] = ref[:, :LANES].T
        values[3 * tokens :, :] = jnp.zeros((values.shape[0] - 3 * tokens, LANES), LOW)
        turned_keys[:, 3 * tokens :] = jnp.zeros((LANES, values.shape[0] - 3 * tokens), LOW)
        key_grad[...] = jnp.zeros_like(key_grad)
        value_grad[...] = jnp.zeros_like(value_grad)

    queries = marked_queries(bound_ref, query_ref, tokens + step * here)
    grads = grad_ref[...]
    split_grads = [head_part(grads, h) for h in range(2)]
    product = (grads.astype(F32) * mixed_ref[...]).T
    centred = [jnp.sum(product[64 * h : 64 * h + 64], axis=0, keepdims=True) for h in range(2)]
    origin = range_ref[0, step] * LANES

    def body(index, carry):
        start = pl.multiple_of(origin + index * KEY_TILE, LANES)
        rows = pl.ds(start, KEY_TILE)
        out, key_part, value_part = [], 0, 0
        for h in range(2):
            shares = jnp.exp(dot(keys[rows, :], queries[h], NT) - log_ref[h : h + 1, :])
            value_part += dot(shares.astype(LOW), split_grads[h])
            share_grad = dot(values[rows, :], split_grads[h], NT)
            score_grad = (shares * (share_grad - centred[h])).astype(LOW)
            key_part += dot(score_grad, queries[h][:, :LANES])
            out.append(carry[h] + dot(turned_keys[64 * h : 64 * h + 64, rows], score_grad))
        key_grad[rows, :] += key_part
        value_grad[rows, :] += value_part
        return tuple(out)

    init = tuple(jnp.zeros((64, here), F32) for _ in range(2))
    done = lax.fori_loop(0, range_ref[1, step], body, init)
    query_grad_ref[...] = (jnp.concatenate(done, axis=0).T * 0.125).astype(LOW)

    @pl.when(step == pl.num_programs(0) - 1)
    def _():
        for place, ref in enumerate((before_grad_ref, own_grad_ref, after_grad_ref)):
            ref[:, :LANES] = key_grad[pl.ds(place * tokens, tokens), :].astype(ref.dtype)
            ref[:, LANES:] = value_grad[pl.ds(place * tokens, tokens), :].astype(ref.dtype)


def key_ranges(spans, query_tile, key_tile):
    first = spans[0, ::query_tile] // LANES
    return jnp.stack([first, (spans[1, query_tile - 1 :: query_tile] - first * LANES + key_tile - 1) // key_tile])


def attention(spans, bounds, queries, before, own, behind):
    tokens, wide = queries.shape
    whole = lambda shape: pl.BlockSpec(shape, lambda i, s: (0, 0))
    tile = pl.BlockSpec((QUERY_TILE, wide), lambda i, s: (i, 0))
    row = pl.BlockSpec((2, QUERY_TILE), lambda i, s: (0, i))
    window = 3 * tokens + KEY_TILE
    return pl.pallas_call(
        attend_kernel,
        grid_spec=pltpu.PrefetchScalarGridSpec(
            num_scalar_prefetch=1,
            grid=(tokens // QUERY_TILE,),
            in_specs=[tile] + [whole((tokens, 2 * wide))] * 3 + [whole(bounds.shape)],
            out_specs=[tile, tile, row],
            scratch_shapes=[pltpu.VMEM((window, 2 * wide), LOW), pltpu.VMEM((wide, window), LOW)],
        ),
        out_shape=[like((tokens, wide), F32), like((tokens, wide), LOW), like((2, tokens), F32)],
        cost_estimate=pl.CostEstimate(
            flops=40 * tokens * tokens * wide, bytes_accessed=16 * tokens * wide, transcendentals=2 * tokens * tokens
        ),
        compiler_params=pltpu.CompilerParams(vmem_limit_bytes=56 << 20),
    )(key_ranges(spans, QUERY_TILE, KEY_TILE), queries, before, own, behind, bounds)


def attention_back(spans, bounds, queries, before, own, behind, mixed, logs, grads):
    tokens, wide = queries.shape
    whole = lambda shape: pl.BlockSpec(shape, lambda i, s: (0, 0))
    tile = pl.BlockSpec((QUERY_TILE, wide), lambda i, s: (i, 0))
    row = pl.BlockSpec((2, QUERY_TILE), lambda i, s: (0, i))
    window = 3 * tokens + KEY_TILE
    return pl.pallas_call(
        attend_back_kernel,
        grid_spec=pltpu.PrefetchScalarGridSpec(
            num_scalar_prefetch=1,
            grid=(tokens // QUERY_TILE,),
            in_specs=[tile] + [whole((tokens, 2 * wide))] * 3 + [whole(bounds.shape), tile, row, tile],
            out_specs=[tile] + [whole((tokens, 2 * wide))] * 3,
            scratch_shapes=[
                pltpu.VMEM((window, 2 * wide), LOW),
                pltpu.VMEM((window, wide), LOW),
                pltpu.VMEM((wide, window), LOW),
                pltpu.VMEM((window, wide), F32),
                pltpu.VMEM((window, wide), F32),
            ],
        ),
        out_shape=[
            like((tokens, wide), LOW),
            like((tokens, 2 * wide), LOW),
            like((tokens, 2 * wide), F32),
            like((tokens, 2 * wide), LOW),
        ],
        cost_estimate=pl.CostEstimate(
            flops=60 * tokens * tokens * wide, bytes_accessed=32 * tokens * wide, transcendentals=2 * tokens * tokens
        ),
        compiler_params=pltpu.CompilerParams(vmem_limit_bytes=56 << 20),
    )(key_ranges(spans, QUERY_TILE, KEY_TILE), queries, before, own, behind, bounds, mixed, logs, grads)


def output_steps(planes):
    return [PLANE << i for i in range(planes.bit_length() - 1)] + [4, 2, 1]


def step_bits(index, steps):
    return sum(bit for i, bit in enumerate(steps) if index >> i & 1)


def place_output(planes, place_ref, refs, out):
    if len(refs) == 1:
        out[...] = refs[0][...]
        return
    devices = PLANE * planes
    rows = out.shape[0] // devices
    steps = output_steps(planes)
    device = place_ref[1] * PLANE + place_ref[0]
    for k, ref in enumerate(refs):
        for i in range(devices // 2):
            bits = step_bits(k * devices // 2 + i, steps)
            out[block_rows(device ^ bits, rows), :] = ref[pl.ds(i * rows, rows), :]


def ordered_output(device, planes, refs):
    devices = PLANE * planes
    rows = 2 * refs[0].shape[0] // devices
    if rows % 16 == 0:
        return refs
    whole = jnp.concatenate(refs, axis=0).reshape(devices, rows, -1)
    steps = output_steps(planes)
    bits = jnp.array([step_bits(i, steps) for i in range(devices)], jnp.int32)
    return [jnp.zeros_like(whole).at[device ^ bits].set(whole).reshape(devices * rows, -1)]


def mix_out_kernel(planes, place_ref, mixed_ref, tokens_ref, vector_ref, *refs):
    output_refs, (second_ref, normed_ref, output) = refs[:-3], refs[-3:]
    place_output(planes, place_ref, output_refs, output)
    mixed = jnp.concatenate([mixed_ref[j] for j in range(PLANE)], axis=1)
    second = tokens_ref[...].astype(F32) + dot(mixed, output[...])
    second_ref[...] = second
    unit, _ = norm_parts(second)
    normed_ref[...] = (unit * vector_ref[2:3, :] + vector_ref[3:4, :]).astype(LOW)


def feed_kernel(planes, place_ref, *refs):
    normed_refs, refs = refs[:SPREAD], refs[SPREAD:]
    cot_refs, refs = refs[:2], refs[2:]
    shrink_refs, refs = refs[:planes], refs[planes:]
    expand_refs, refs = refs[:2], refs[2:]
    bias_ref, near_out, far_out, corner_out, active_ref, grad_ref, bias_out, expand, shrink, x, c = refs
    part = expand.shape[1] // 2
    expand[:, :part] = expand_refs[0][...]
    expand[:, part:] = expand_refs[1][...]
    gather_planes(place_ref[1], shrink_refs, shrink)
    join(normed_refs, x)
    join(cot_refs, c)
    number = near_out.shape[1]
    sums = jnp.zeros(bias_ref.shape, F32)
    for k, m in ((1, 2), (1, 0), (0, 2), (0, 0)):
        rows = pl.ds((4 * k + m) * number, 2 * number)
        upper = dot(x[rows, :], expand[...]) + bias_ref[...]
        share = 0.5 + 0.5 * lax.erf(upper * 0.7071067811865476)
        density = 0.3989422804014327 * jnp.exp(-0.5 * upper * upper)
        active_ref[rows, :] = (upper * share).astype(LOW)
        grad = (dot(c[rows, :], shrink[...], NT) * (share + upper * density)).astype(LOW)
        grad_ref[rows, :] = grad
        sums += jnp.sum(grad.astype(F32), axis=0, keepdims=True)
        down = dot(grad, expand[...], NT)
        put_block((near_out, far_out, corner_out), k, m, down[:number])
        put_block((near_out, far_out, corner_out), k, m + 1, down[number:])
    bias_out[...] = sums


def plane_blocks(plane, whole, outs):
    planes = len(outs)
    tall = whole.shape[0] // planes
    for s, out in enumerate(outs):
        out[...] = whole[block_rows(lax.rem(plane + s, planes), tall), :].astype(out.dtype)


def shrink_grad_kernel(place_ref, active_ref, *refs):
    cot_refs, outs, (whole, cotangents) = refs[:2], refs[2:-2], refs[-2:]
    join(cot_refs, cotangents)
    whole[...] = dot(active_ref[...], cotangents[...], TN)
    plane_blocks(place_ref[1], whole, outs)


def expand_grad_kernel(grad_ref, *refs):
    normed_refs, (out_ref, normed) = refs[:SPREAD], refs[SPREAD:]
    join(normed_refs, normed)
    out_ref[...] = dot(normed[...], grad_ref[...], TN).astype(LOW)


def norm_two_back_kernel(
    planes, place_ref, one_ref, two_ref, three_ref, second_ref, cotangent_ref, vector_ref, *refs
):
    output_refs, (second_grad_ref, branch_ref, mixed_ref, sums_ref, output) = refs[:-5], refs[-5:]
    place_output(planes, place_ref, output_refs, output)
    incoming = one_ref[...] + two_ref[...].astype(F32) + three_ref[...].astype(F32)
    unit, inverse = norm_parts(second_ref[...])
    cotangent = cotangent_ref[...].astype(F32)
    second_grad = cotangent + norm_back(unit, inverse, vector_ref[2:3, :], incoming)
    second_grad_ref[...] = second_grad
    branch = second_grad.astype(LOW)
    branch_ref[...] = branch
    mixed = dot(branch, output[...], NT).astype(LOW)
    wide = mixed_ref.shape[2]
    for j in range(PLANE):
        mixed_ref[j] = mixed[:, wide * j : wide * j + wide]
    sums_ref[...] = jnp.concatenate(
        [
            jnp.sum(incoming * unit, axis=0, keepdims=True),
            jnp.sum(incoming, axis=0, keepdims=True),
            jnp.sum(cotangent, axis=0, keepdims=True),
        ],
        axis=0,
    )


def output_grad_kernel(place_ref, mixed_ref, *refs):
    branch_refs, outs, (whole, left, right) = refs[:2], refs[2:-3], refs[-3:]
    join(branch_refs, right)
    number = right.shape[0] // PLANE
    for r in range(PLANE):
        left[pl.ds(r * number, number), :] = mixed_ref[block_rows(place_ref[0] ^ relative(r), number), :]
    whole[...] = dot(left[...], right[...], TN)
    if len(outs) == 1:
        outs[0][...] = whole[...].astype(LOW)
    else:
        plane_blocks(place_ref[1], whole, outs)


def first_back_kernel(
    planes, place_ref, own_ref, from_after_ref, from_before_ref, query_ref, first_ref, unit_ref,
    weight, two_sums_ref, up_sums_ref, active_ref, *refs
):
    shrink_refs, (grad_ref, near_ref, far_ref, corner_ref, sums_ref, joined, vectors, shrink) = refs[:planes], refs[planes:]
    gather_planes(place_ref[1], shrink_refs, shrink)
    spot = place_ref[0]
    number, columns = near_ref.shape[1] // 2, near_ref.shape[2]
    wide = query_ref.shape[1]
    pairs = (own_ref[...] + from_after_ref[...].astype(F32) + from_before_ref[...].astype(F32)).astype(LOW)
    joined[:, :wide] = query_ref[...]
    joined[:, wide:] = pairs
    grad = dot(first_ref[...], joined[...], TN).astype(LOW)
    gain = jnp.zeros((1, columns), F32)
    shift = jnp.zeros((1, columns), F32)
    for k, m in ((1, 2), (1, 0), (0, 2), (0, 0)):
        part = jnp.concatenate(
            [joined[block_rows(spot ^ (2 * (m + i) + k), number), :] for i in range(2)], axis=0
        )
        down = dot(part, weight[...], NT)
        unit = unit_ref[pl.ds((4 * k + m) * number, 2 * number), :].astype(F32)
        gain += jnp.sum(down * unit, axis=0, keepdims=True)
        shift += jnp.sum(down, axis=0, keepdims=True)
        lower = dot(active_ref[pl.ds((4 * k + m) * number, 2 * number), :], shrink[...])
        outs = (near_ref, far_ref, corner_ref)
        put_block(outs, k, m, jnp.concatenate([down[:number], lower[:number]], axis=0))
        put_block(outs, k, m + 1, jnp.concatenate([down[number:], lower[number:]], axis=0))
    sums_ref[...] = jnp.concatenate([gain, shift], axis=0)
    if len(grad_ref.shape) == 2:
        grad_ref[...] = grad
        return
    devices, tall, _ = grad_ref.shape
    rows = tall - EXTRA
    vectors[...] = jnp.zeros_like(vectors)
    vectors[0:2, :] = sums_ref[...]
    vectors[2:5, :] = two_sums_ref[...]
    for g in range(up_sums_ref.shape[1] // LANES):
        lanes = pl.ds(pl.multiple_of(spot * LANES, LANES), LANES)
        vectors[5 + g : 6 + g, lanes] = up_sums_ref[:, g * LANES : (g + 1) * LANES]
    grad_ref[:, rows:, :] = jnp.zeros((devices, EXTRA, grad_ref.shape[2]), LOW)
    for d in range(devices):
        lot = slice(d * rows // LANES * LANES, (d * rows // LANES + 1) * LANES)
        grad_ref[d, :rows, :] = grad[d * rows : (d + 1) * rows]
        grad_ref[d, rows:, :LANES] = vectors[:EXTRA, lot].astype(LOW)
        grad_ref[d, rows:, LANES : 2 * LANES] = vectors[EXTRA:, lot].astype(LOW)


def last_kernel(one_ref, two_ref, three_ref, tokens_ref, second_grad_ref, second_ref, vector_ref, out_ref, block_ref):
    number = tokens_ref.shape[0]
    both = one_ref[...] + two_ref[...].astype(F32) + three_ref[...].astype(F32)
    unit, inverse = norm_parts(tokens_ref[...].astype(F32))
    back = norm_back(unit, inverse, vector_ref[0:1, :], both[:number])
    out_ref[...] = (second_grad_ref[...] + back).astype(LOW)
    block_ref[...] = (second_ref[...] + both[number:] + vector_ref[4:5, :]).astype(LOW)


def sum_kernel(wide, with_vectors, whole_count, parts_count, square_ref, *refs):
    others, parts, refs = refs[:whole_count], refs[whole_count : whole_count + parts_count], refs[whole_count + parts_count :]
    part_ref, grad_ref, total_ref = refs[:3]
    devices = part_ref.shape[0]
    rows = grad_ref.shape[0]
    square = jnp.zeros((rows, wide), F32)
    start = 0
    for c in range(part_ref.shape[2] // wide):
        for j in range(PLANE):
            sources = range(j, devices, PLANE)
            whole = sum(part_ref[d, :rows, c * wide : (c + 1) * wide].astype(F32) for d in sources)
            grad_ref[:, start : start + wide] = whole
            square += whole * whole
            start += wide
    found = jnp.sum(square, keepdims=True) + square_ref[0]
    for ref in others:
        found += jnp.sum(ref[...] * ref[...], keepdims=True)
    if parts:
        whole = sum(ref[...].astype(F32) for ref in parts)
        refs[-1][...] = whole
        found += jnp.sum(whole * whole, keepdims=True)
    if with_vectors:
        vectors = sum(part_ref[d, rows:, : 2 * LANES].astype(F32) for d in range(devices))
        refs[3][:EXTRA, :] = vectors[:, :LANES]
        refs[3][EXTRA:, :] = vectors[:, LANES:]
        lanes = lax.broadcasted_iota(jnp.int32, (2 * EXTRA, LANES), 1)
        mine = lanes // rows == square_ref[1].astype(jnp.int32)
        found += jnp.sum(jnp.where(mine, refs[3][...] * refs[3][...], 0.0), keepdims=True)
    total_ref[...] = jnp.broadcast_to(found.reshape((1,) * len(total_ref.shape)), total_ref.shape)


def sum_parts(wide, rows, part, square, lot=None, others=(), parts=()):
    n, _, columns = part.shape
    vectors = lot is not None
    if wide % LANES == 0 and rows % 16 == 0:
        outs = [like((rows, PLANE * columns), F32), like((n, 1, LANES) if vectors else (1, 1), F32)]
        found = kernel_call(
            functools.partial(sum_kernel, wide, vectors, len(others), len(parts)),
            outs + [like((2 * EXTRA, LANES), F32)] * vectors + [like(p.shape, F32) for p in parts[:1]],
            *others,
            *parts,
            part,
            scalars=(jnp.stack([square, lot.astype(F32) if vectors else square]),),
        )
        return found
    whole = part[:, :rows].astype(F32).reshape(-1, PLANE, rows, columns // wide, wide).sum(0)
    whole = whole.transpose(1, 2, 0, 3).reshape(rows, -1)
    square = square + jnp.sum(whole * whole) + sum(jnp.sum(g * g) for g in others)
    if not vectors:
        joined = sum(p.astype(F32) for p in parts)
        return whole, (square + jnp.sum(joined * joined)).reshape(1, 1), joined
    found = part[:, rows:, : 2 * LANES].astype(F32).sum(0)
    found = jnp.concatenate([found[:, :LANES], found[:, LANES:]], axis=0)
    mine = lax.dynamic_slice_in_dim(found, rows * lot, rows, axis=1)
    square = square + jnp.sum(mine * mine)
    return whole, jnp.full((n, 1, LANES), square), found


def update_kernel(square_ref, *refs):
    norm = jnp.sqrt(jnp.sum(square_ref[...], axis=0)[:, :1])
    refs[-1][...] = norm
    refs = refs[:-1]
    factor = jnp.minimum(1.0, CLIP_NORM / (norm + 1e-06))
    smooth_rate = min(0.999, (1.0 + STEP) / (10.0 + STEP))
    count = len(LEARNING_RATES)
    states, grads, outs = refs[: 3 * count], refs[3 * count : 4 * count], refs[4 * count :]
    for place, rate in enumerate(LEARNING_RATES):
        weight, moment, average = (ref[...] for ref in states[3 * place : 3 * place + 3])
        clipped = factor * grads[place][...] + WEIGHT_DECAY * weight
        velocity = MOMENTUM * moment + clipped
        updated = weight - rate * (clipped + MOMENTUM * velocity)
        outs[3 * place][...] = velocity
        outs[3 * place + 1][...] = updated
        outs[3 * place + 2][...] = smooth_rate * average + (1.0 - smooth_rate) * updated


def with_vectors(attend_grad, one_sums, two_sums, up_sums, spot, n, rows, hidden):
    columns, wide = attend_grad.shape
    planes, lots, in_lot = n // PLANE, columns // LANES, LANES // rows
    up_sums = lax.dynamic_update_slice_in_dim(
        jnp.zeros((planes, PLANE, hidden), F32), up_sums.reshape(planes, 1, hidden), spot, axis=1
    )
    part = jnp.concatenate([one_sums, two_sums, up_sums.reshape(-1, columns)], axis=0).astype(LOW)
    part = jnp.moveaxis(part.reshape(-1, lots, LANES), 1, 0)
    part = jnp.pad(part, ((0, 0), (0, 2 * EXTRA - part.shape[1]), (0, 0)))
    part = jnp.concatenate([part[:, :EXTRA], part[:, EXTRA:]], axis=2)
    part = jnp.pad(part, ((0, 0), (0, 0), (0, wide - 2 * LANES)))
    return jnp.concatenate([attend_grad.reshape(n, rows, wide), jnp.repeat(part, in_lot, axis=0)], axis=1)


def on_device(
    tokens,
    scene_lengths,
    cotangent,
    attend_weight,
    output_weight,
    expand_weight,
    reduce_weight,
    vector_params,
    attend_momentum,
    output_momentum,
    expand_momentum,
    reduce_momentum,
    vector_momentum,
    attend_average,
    output_average,
    expand_average,
    reduce_average,
    vector_average,
):
    n = lax.axis_size("seq")
    planes = n // PLANE
    device = lax.axis_index("seq")
    plane, spot = device // PLANE, device % PLANE
    place = jnp.stack([spot, plane]).astype(jnp.int32)
    number, columns = tokens.shape
    shared = number * PLANE
    rows = columns // n
    hidden = reduce_weight.shape[0]
    wide = columns // PLANE
    lots = columns // LANES
    in_lot = LANES // rows
    inner = planes * hidden
    near_like, far_like = like((4, number, columns), F32), like((3, number, columns), LOW)
    block_like, block_exact = like((number, columns), LOW), like((number, columns), F32)
    shared_scratch = pltpu.VMEM((shared, columns), LOW)
    square_scratch = pltpu.VMEM((columns, columns), LOW)

    vector_low = vector_params.astype(LOW)
    sides = spread_sides(tokens)
    attend = attend_weight.astype(LOW).reshape(rows, 3, PLANE, wide).transpose(2, 0, 1, 3).reshape(PLANE, rows, 3 * wide)
    vector_part = lax.dynamic_update_slice(
        jnp.zeros((2 * EXTRA, LANES), LOW), vector_low, (0, rows * (device % in_lot))
    )
    vector_part = jnp.concatenate([vector_part[:EXTRA], vector_part[EXTRA:]], axis=1)
    vector_part = jnp.pad(vector_part, ((0, 0), (0, 3 * wide - 2 * LANES)))
    attend = jnp.concatenate(
        [
            jnp.broadcast_to(attend[None], (planes,) + attend.shape).reshape(n, rows, 3 * wide),
            jnp.broadcast_to(vector_part[None], (n,) + vector_part.shape),
        ],
        axis=1,
    )
    attend = exchange(after(attend, *sides))
    lot_vectors = attend[:, rows:].reshape(lots, in_lot, EXTRA, 3 * wide).astype(F32).sum(1)
    corner = spread_corner(*sides)
    output = after(output_weight.astype(LOW), *sides)
    for bit in output_steps(planes)[:-3]:
        output = grow(output, bit)
    expand = (
        expand_weight.astype(LOW)
        .reshape(rows, planes, PLANE, hidden)
        .transpose(2, 0, 1, 3)
        .reshape(PLANE, rows, inner)
    )
    expand = jnp.broadcast_to(expand[None], (planes,) + expand.shape).reshape(n, rows, inner)
    expand = [expand[:, :, : inner // 2], expand[:, :, inner // 2 :]]
    shrink = reduce_weight.astype(LOW)
    corner, expand, shrink = tie(corner, expand, shrink)
    gathered = spread_far(tokens, sides, corner)
    gathered, output = tie(gathered, output)

    units, first_low, queries, pairs, attend, vectors = kernel_call(
        project_kernel,
        [
            like((shared, columns), LOW),
            like((shared, columns), LOW),
            like((shared, wide), LOW),
            like((shared, 2 * wide), LOW),
            like((columns, 3 * wide), LOW),
            like((2 * EXTRA, columns), F32),
        ],
        *gathered,
        attend,
        lot_vectors,
        scalars=(place,),
        scratch=[shared_scratch],
        flops=6 * shared * columns * wide,
    )
    bias_up = lax.dynamic_index_in_dim(
        vectors[5 : vector_params.shape[0]].reshape(planes, PLANE, hidden), spot, axis=1, keepdims=False
    ).reshape(1, inner)

    before, behind = move(pairs, PLANE), move(pairs, -PLANE)
    expand[0] = exchange(after(expand[0], pairs)).reshape(columns, inner // 2)
    output = grow(after(output, pairs), 4)
    cotangents = grow(after(cotangent, pairs), 2)
    queries, output, cotangents = tie(queries, output, cotangents)

    finish = jnp.cumsum(scene_lengths)
    begin = finish - scene_lengths
    base = (plane - 1) * shared
    position = plane * shared + jnp.arange(shared, dtype=jnp.int32)
    past = begin[None, :] <= position[:, None]
    span_begin = jnp.max(jnp.where(past, begin[None, :], 0), axis=1) - base
    span_end = jnp.min(jnp.where(finish[None, :] > position[:, None], finish[None, :], 1 << 30), axis=1) - base
    spans = jnp.stack([span_begin, span_end])
    bounds = jnp.stack([begin, finish]) - base
    bounds = jnp.pad(bounds, ((0, 0), (0, LANES - bounds.shape[1])))
    output = grow(output, 2)
    cotangents = grow(cotangents, 4)
    shrink_turns = {1: turn(after(shrink, queries), 1)}
    mixed_exact, mixed_low, logs = attention(spans, bounds, queries, before, pairs, behind)
    mixed_low, output, cotangents, expand[0], shrink_turns = tie(
        mixed_low, output, cotangents, expand[0], shrink_turns
    )

    mixed = exchange(mixed_low.reshape(PLANE, number, wide), plane_groups())
    output = [output, swap(output, 1)]
    cotangents = [cotangents, swap(cotangents, 1)]
    shrink_turns.update({s: turn(after(shrink, mixed_low), s) for s in range(2, planes)})
    output = ordered_output(device, planes, output)
    second, normed = kernel_call(
        functools.partial(mix_out_kernel, planes),
        [block_exact, block_like],
        mixed,
        tokens,
        vectors,
        *output,
        scalars=(place,),
        scratch=[square_scratch],
        flops=2 * number * columns * columns,
    )

    expand[1] = exchange(after(expand[1], mixed)).reshape(columns, inner // 2)
    sides = spread_sides(normed)
    sides, shrink_turns, cotangents = tie(sides, shrink_turns, cotangents)
    corner = spread_corner(*sides)
    shrink = [shrink] + [shrink_turns[s] for s in range(1, planes)]
    normed_all = spread_far(normed, sides, corner)

    inner_low = like((shared, inner), LOW)
    grad_near, grad_far, grad_corner, active, upper_grad, up_sums = kernel_call(
        functools.partial(feed_kernel, planes),
        [near_like, far_like, block_like, inner_low, inner_low, like((1, inner), F32)],
        *normed_all,
        *cotangents,
        *shrink,
        *expand,
        bias_up,
        scalars=(place,),
        scratch=[pltpu.VMEM((columns, inner), LOW), pltpu.VMEM((inner, columns), LOW), shared_scratch, shared_scratch],
        flops=6 * shared * columns * inner,
    )

    normed_grad = collect(grad_near, grad_far, grad_corner)
    shrink_grad = kernel_call(
        shrink_grad_kernel,
        [like((hidden, columns), LOW)] * planes,
        active,
        *cotangents,
        scalars=(place,),
        scratch=[pltpu.VMEM((inner, columns), F32), shared_scratch],
        flops=2 * shared * columns * inner,
    )
    shrink_turns = [turn(shrink_grad[s], s) for s in range(1, planes)]
    normed_grad, shrink_turns[:1] = tie(normed_grad, shrink_turns[:1])
    second_grad, branch_grad, mixed_grad, two_sums = kernel_call(
        functools.partial(norm_two_back_kernel, planes),
        [block_exact, block_like, like((PLANE, number, wide), LOW), like((3, columns), F32)],
        *normed_grad,
        second,
        cotangent,
        vectors,
        *output,
        scalars=(place,),
        scratch=[square_scratch],
        flops=2 * number * columns * columns,
    )

    mixed_grad = exchange(mixed_grad, plane_groups()).reshape(shared, wide)
    (expand_grad,) = kernel_call(
        expand_grad_kernel,
        [like((columns, inner), LOW)],
        after(upper_grad, branch_grad),
        *normed_all,
        scratch=[shared_scratch],
        flops=2 * shared * columns * inner,
    )
    branch_sides = spread_sides(branch_grad)
    mixed_grad, expand_grad, branch_sides, shrink_turns = tie(mixed_grad, expand_grad, branch_sides, shrink_turns)
    shrink_grad = sum(g.astype(F32) for g in [shrink_grad[0], *shrink_turns])

    expand_part = exchange(after(expand_grad, mixed_grad).reshape(n, rows, inner))
    branch_corner = spread_corner(*branch_sides)
    query_grad, before_grad, own_grad, behind_grad = attention_back(
        spans, bounds, queries, before, pairs, behind, mixed_exact, logs, mixed_grad
    )
    before_grad, behind_grad, branch_corner = tie(before_grad, behind_grad, branch_corner)

    from_after, from_before = move(before_grad, -PLANE), move(behind_grad, PLANE)
    branch = jnp.concatenate([branch_grad, *branch_sides, *branch_corner], axis=0)
    output_grad = kernel_call(
        output_grad_kernel,
        [like((rows, columns), LOW)] * planes if rows % 16 == 0 else [like((wide, columns), LOW)],
        mixed_low,
        branch,
        swap(branch, 1),
        scalars=(place,),
        scratch=[pltpu.VMEM((wide, columns), F32), pltpu.VMEM((shared, wide), LOW), shared_scratch],
        flops=2 * shared * columns * wide,
    )
    if len(output_grad) == 1:
        output_grad = jnp.take(
            output_grad[0].reshape(planes, rows, columns), (plane + jnp.arange(planes)) % planes, axis=0, mode="clip"
        )
    output_parts = [
        lax.ppermute(
            output_grad[s],
            "seq",
            [(g * PLANE + j, j * planes + (g + s) % planes) for g in range(planes) for j in range(PLANE)],
        )
        for s in range(planes)
    ]
    from_after, from_before, output_parts[:2] = tie(from_after, from_before, output_parts[:2])

    fused = rows % 16 == 0 and hidden == LANES
    attend_grad, first_near, first_far, first_corner, one_sums = kernel_call(
        functools.partial(first_back_kernel, planes),
        [
            like((n, rows + EXTRA, 3 * wide) if fused else (columns, 3 * wide), LOW),
            like((4, 2 * number, columns), F32),
            like((3, 2 * number, columns), LOW),
            like((2 * number, columns), LOW),
            like((2, columns), F32),
        ],
        own_grad,
        from_after,
        from_before,
        query_grad,
        first_low,
        units,
        attend,
        two_sums,
        up_sums,
        active,
        *shrink,
        scalars=(place,),
        scratch=[
            pltpu.VMEM((shared, 3 * wide), LOW),
            pltpu.VMEM((2 * EXTRA, columns), F32),
            pltpu.VMEM((inner, columns), LOW),
        ],
        flops=2 * shared * columns * 6 * wide,
    )
    more = vector_params.shape[0] - EXTRA
    attend_part = attend_grad
    if not fused:
        attend_part = with_vectors(attend_grad, one_sums, two_sums, up_sums, spot, n, rows, hidden)
    attend_part, first_near, first_far, first_corner, expand_part, output_parts = tie(
        attend_part, first_near, first_far, first_corner, expand_part, output_parts
    )
    attend_part = exchange(attend_part)
    both = collect(first_near, first_far, first_corner)
    input_gradient, block_output = kernel_call(
        last_kernel, [block_like, block_like], *both, tokens, second_grad, second, vectors
    )
    expand_grad, squares, output_grad = sum_parts(
        hidden, rows, expand_part, jnp.zeros((), F32), others=[shrink_grad], parts=output_parts
    )
    attend_grad, squares, vector_grad = sum_parts(wide, rows, attend_part, squares[0, 0], device % in_lot)
    vector_grad = lax.dynamic_slice_in_dim(vector_grad, rows * (device % in_lot), rows, axis=1)
    vector_grad = vector_grad[: vector_params.shape[0]]
    squares, input_gradient, block_output = tie(exchange(squares), input_gradient, block_output)
    states = (
        (attend_weight, attend_momentum, attend_average),
        (output_weight, output_momentum, output_average),
        (expand_weight, expand_momentum, expand_average),
        (reduce_weight, reduce_momentum, reduce_average),
        (vector_params, vector_momentum, vector_average),
    )
    *updates, gradient_norm = kernel_call(
        update_kernel,
        [like(g[0].shape, F32) for g in states for _ in range(3)] + [like((1, 1), F32)],
        squares,
        *[a for g in states for a in g],
        attend_grad,
        output_grad,
        expand_grad,
        shrink_grad,
        vector_grad,
    )
    return (block_output, input_gradient, gradient_norm.reshape(()), *updates)


def solution(mesh):
    split, turned = P("seq", None), P(None, "seq")
    return jax.shard_map(
        on_device,
        mesh=mesh,
        in_specs=(split, P()) + (split,) * 5 + (turned,) + ((split,) * 4 + (turned,)) * 2,
        out_specs=(split, split, P()) + (split,) * 12 + (turned,) * 3,
        check_vma=False,
    )
```

```python
import functools

import jax
import jax.numpy as jnp
from jax import lax
from jax.experimental import pallas as pl
from jax.experimental.pallas import tpu as pltpu
from jax.sharding import PartitionSpec as P

HEADS = 16
STEP = 10
EPSILON = 1e-05
MOMENTUM = 0.9
LEARNING_RATES = (60.0, 480.0, 60.0, 60.0, 600.0)
WEIGHT_DECAY = 0.0001
CLIP_NORM = 1.0
MASK_FLOOR = -1e30
PLANE = 8
EXTRA = 8
LANES = 128
QUERY_TILE = 512
KEY_TILE = 640
F32 = jnp.float32
LOW = jnp.bfloat16
WHOLE = pl.BlockSpec()
SMEM = pl.BlockSpec(memory_space=pltpu.SMEM)


def like(shape, dtype):
    return jax.ShapeDtypeStruct(shape, dtype)


def kernel_call(body, outs, *args, scalars=(), scratch=(), flops=0, limit=56):
    moved = sum(a.size * a.dtype.itemsize for a in list(args) + list(outs))
    return pl.pallas_call(
        body,
        in_specs=[SMEM] * len(scalars) + [WHOLE] * len(args),
        out_specs=[WHOLE] * len(outs),
        out_shape=list(outs),
        scratch_shapes=list(scratch),
        cost_estimate=pl.CostEstimate(flops=flops, bytes_accessed=moved, transcendentals=0),
        compiler_params=pltpu.CompilerParams(vmem_limit_bytes=limit << 20),
    )(*scalars, *args)


def after(value, *others):
    return lax.optimization_barrier((value, *others))[0]


def tie(*values):
    return lax.optimization_barrier(values)


def swap(block, bit):
    n = lax.axis_size("seq")
    return lax.ppermute(block, "seq", [(i, i ^ bit) for i in range(n)])


def move(block, distance):
    n = lax.axis_size("seq")
    return lax.ppermute(
        block, "seq", [(i, i + distance) for i in range(n) if 0 <= i + distance < n]
    )


def turn(block, planes_on):
    n = lax.axis_size("seq")
    return lax.ppermute(block, "seq", [(i, (i + planes_on * PLANE) % n) for i in range(n)])


def plane_groups():
    n = lax.axis_size("seq")
    return [[g * PLANE + j for j in range(PLANE)] for g in range(n // PLANE)]


def cross_groups():
    n = lax.axis_size("seq")
    return [[g * PLANE + j for g in range(n // PLANE)] for j in range(PLANE)]


def exchange(blocks, groups=None):
    return lax.all_to_all(blocks, "seq", 0, 0, axis_index_groups=groups)


def spread_sides(block):
    return swap(block, 2), swap(block, 4)


def spread_corner(across, along):
    half = across.shape[0] // 2
    return swap(across[:half], 4), swap(along[half:], 2)


def grow(block, bit):
    return jnp.concatenate([block, swap(block, bit)], axis=0)


def spread_far(block, sides, corner):
    far = swap(jnp.stack([block, *sides]), 1)
    return [block, *sides, *corner, far, *[swap(c, 1) for c in corner]]


def spread(block):
    sides = spread_sides(block)
    return spread_far(block, sides, spread_corner(*sides))


SPREAD = 8


def join(refs, out):
    number = refs[0].shape[0]
    place = 0
    for ref in refs:
        if len(ref.shape) == 3:
            for m in range(ref.shape[0]):
                out[pl.ds(place, number), :] = ref[m]
                place += number
        else:
            out[pl.ds(place, ref.shape[0]), :] = ref[...]
            place += ref.shape[0]


def collect(near, far, far_corner):
    return collect_came(near, swap(far_corner, 1), swap(far, 1))


def collect_came(near, came_corner, came):
    half = near.shape[1] // 2
    corner = (near[3] + came_corner.astype(F32)).astype(LOW)
    by_across = swap(corner[:half], 2).astype(F32)
    by_along = swap(corner[half:], 4).astype(F32)
    across = near[1] + came[1].astype(F32)
    along = near[2] + came[2].astype(F32)
    across = jnp.concatenate([across[:half], across[half:] + by_along], axis=0).astype(LOW)
    along = jnp.concatenate([along[:half] + by_across, along[half:]], axis=0).astype(LOW)
    return near[0] + came[0].astype(F32), swap(across, 2), swap(along, 4)


def put_block(outs, k, m, value):
    if k == 0:
        outs[0][m] = value
    elif m < 3:
        outs[1][m] = value.astype(LOW)
    else:
        outs[2][...] = value.astype(LOW)


def total(terms):
    return terms[0] + terms[1].astype(F32) + terms[2].astype(F32)


def norm_parts(values):
    centre = values - jnp.mean(values, axis=-1, keepdims=True)
    spread_of = jnp.mean(centre * centre, axis=-1, keepdims=True)
    inverse = lax.rsqrt(spread_of + EPSILON)
    return centre * inverse, inverse


def norm_back(unit, inverse, gain, incoming):
    scaled = incoming * gain
    return inverse * (
        scaled
        - jnp.mean(scaled, axis=-1, keepdims=True)
        - unit * jnp.mean(scaled * unit, axis=-1, keepdims=True)
    )


def dot(a, b, dims=((1,), (0,))):
    return lax.dot_general(a, b, (dims, ((), ())), preferred_element_type=F32)


NT = ((1,), (1,))
TN = ((0,), (0,))


def block_rows(place, number):
    return pl.ds(pl.multiple_of(place * number, number), number)


def gather_planes(plane, refs, out):
    planes = len(refs)
    rows = refs[0].shape[0]
    for s, ref in enumerate(refs):
        out[block_rows(lax.rem(plane - s + planes, planes), rows), :] = ref[...]


def project_kernel(spot_ref, *refs):
    token_refs, refs = refs[:SPREAD], refs[SPREAD:]
    sent_ref, lots_ref, unit_ref, first_ref, query_ref, pair_ref, weight_ref, vector_ref, held = refs
    spot = spot_ref[0]
    number, columns = token_refs[0].shape
    devices = sent_ref.shape[0]
    rows = columns // devices
    if len(sent_ref.shape) == 2:
        weight_ref[...] = sent_ref[...]
    wide = query_ref.shape[1]
    for d in range(devices if len(sent_ref.shape) == 3 else 0):
        for c in range(3):
            weight_ref[pl.ds(d * rows, rows), c * wide : (c + 1) * wide] = sent_ref[d, c * rows : (c + 1) * rows, :]
    for g in range(lots_ref.shape[0]):
        lanes = slice(g * LANES, (g + 1) * LANES)
        vector_ref[:EXTRA, lanes] = lots_ref[g, :, :LANES]
        vector_ref[EXTRA:, lanes] = lots_ref[g, :, LANES : 2 * LANES]
    join(token_refs, held)
    gain, shift = vector_ref[0:1, :], vector_ref[1:2, :]
    for r in range(PLANE):
        here = pl.ds(r * number, number)
        unit, _ = norm_parts(held[here, :].astype(F32))
        first = (unit * gain + shift).astype(LOW)
        unit_ref[here, :] = unit.astype(LOW)
        held[here, :] = first
        first_ref[block_rows(spot ^ relative(r), number), :] = first
    joined = dot(held[...], weight_ref[...]).astype(LOW)
    for r in range(PLANE):
        here = slice(r * number, (r + 1) * number)
        query_ref[block_rows(spot ^ relative(r), number), :] = joined[here, :wide]
        pair_ref[block_rows(spot ^ relative(r), number), :] = joined[here, wide:]


def relative(r):
    return 2 * (r % 4) + r // 4


def head_part(array, head):
    lanes = lax.broadcasted_iota(jnp.int32, array.shape, len(array.shape) - 1)
    return jnp.where(lanes // 64 == head, array, jnp.zeros_like(array))


def scene_marks(bound_ref, first, count, inside, outside):
    place = first + lax.broadcasted_iota(jnp.int32, (count, LANES), 0)
    here = (place >= bound_ref[0:1, :]) & (place < bound_ref[1:2, :])
    return jnp.where(here, inside, outside).astype(LOW)


def marked_queries(bound_ref, query_ref, first):
    queries = query_ref[...] * jnp.asarray(0.125, LOW)
    marks = scene_marks(bound_ref, first, queries.shape[0], MASK_FLOOR, 0.0)
    return [jnp.concatenate([head_part(queries, h), marks], axis=1) for h in range(2)]


def marked_keys(bound_ref, refs, keys):
    tokens = refs[0].shape[0]
    for place, ref in enumerate(refs):
        keys[pl.ds(place * tokens, tokens), :LANES] = ref[:, :LANES]
        keys[pl.ds(place * tokens, tokens), LANES:] = scene_marks(bound_ref, place * tokens, tokens, 0.0, 1.0)
    keys[3 * tokens :, :LANES] = jnp.zeros((keys.shape[0] - 3 * tokens, LANES), LOW)
    keys[3 * tokens :, LANES:] = jnp.ones((keys.shape[0] - 3 * tokens, LANES), LOW)


def attend_kernel(
    range_ref, query_ref, before_ref, own_ref, after_ref, bound_ref, mixed_ref, low_ref, log_ref, keys, values
):
    step = pl.program_id(0)
    tokens = own_ref.shape[0]
    here = query_ref.shape[0]

    @pl.when(step == 0)
    def _():
        refs = (before_ref, own_ref, after_ref)
        marked_keys(bound_ref, refs, keys)
        for place, ref in enumerate(refs):
            values[:, pl.ds(place * tokens, tokens)] = ref[:, LANES:].T
        values[:, 3 * tokens :] = jnp.zeros((LANES, values.shape[1] - 3 * tokens), LOW)

    queries = marked_queries(bound_ref, query_ref, tokens + step * here)
    origin = range_ref[0, step] * LANES

    def body(index, carry):
        start = pl.multiple_of(origin + index * KEY_TILE, LANES)
        block = keys[pl.ds(start, KEY_TILE), :]
        out = []
        for h in range(2):
            peak, whole, mixed = carry[h]
            scores = dot(block, queries[h], NT)
            raised_peak = jnp.maximum(peak, jnp.max(scores, axis=0, keepdims=True))
            raised = jnp.exp(scores - raised_peak)
            fade = jnp.exp(peak - raised_peak)
            whole = whole * fade + jnp.sum(raised, axis=0, keepdims=True)
            turned = values[64 * h : 64 * h + 64, pl.ds(start, KEY_TILE)]
            mixed = mixed * fade + dot(turned, raised.astype(LOW))
            out.append((raised_peak, whole, mixed))
        return tuple(out)

    init = tuple(
        (jnp.full((1, here), MASK_FLOOR, F32), jnp.zeros((1, here), F32), jnp.zeros((64, here), F32))
        for _ in range(2)
    )
    done = lax.fori_loop(0, range_ref[1, step], body, init)
    mixed = jnp.concatenate([m / t for _, t, m in done], axis=0).T
    mixed_ref[...] = mixed
    low_ref[...] = mixed.astype(LOW)
    log_ref[...] = jnp.concatenate([k + jnp.log(t) for k, t, _ in done], axis=0)


def attend_back_kernel(
    range_ref,
    query_ref,
    before_ref,
    own_ref,
    after_ref,
    bound_ref,
    mixed_ref,
    log_ref,
    grad_ref,
    query_grad_ref,
    before_grad_ref,
    own_grad_ref,
    after_grad_ref,
    keys,
    values,
    turned_keys,
    key_grad,
    value_grad,
):
    step = pl.program_id(0)
    tokens = own_ref.shape[0]
    here = query_ref.shape[0]

    @pl.when(step == 0)
    def _():
        refs = (before_ref, own_ref, after_ref)
        marked_keys(bound_ref, refs, keys)
        for place, ref in enumerate(refs):
            values[pl.ds(place * tokens, tokens), :] = ref[:, LANES:]
            turned_keys[:, pl.ds(place * tokens, tokens)] = ref[:, :LANES].T
        values[3 * tokens :, :] = jnp.zeros((values.shape[0] - 3 * tokens, LANES), LOW)
        turned_keys[:, 3 * tokens :] = jnp.zeros((LANES, values.shape[0] - 3 * tokens), LOW)
        key_grad[...] = jnp.zeros_like(key_grad)
        value_grad[...] = jnp.zeros_like(value_grad)

    queries = marked_queries(bound_ref, query_ref, tokens + step * here)
    grads = grad_ref[...]
    split_grads = [head_part(grads, h) for h in range(2)]
    product = (grads.astype(F32) * mixed_ref[...]).T
    centred = [jnp.sum(product[64 * h : 64 * h + 64], axis=0, keepdims=True) for h in range(2)]
    origin = range_ref[0, step] * LANES

    def body(index, carry):
        start = pl.multiple_of(origin + index * KEY_TILE, LANES)
        rows = pl.ds(start, KEY_TILE)
        out, key_part, value_part = [], 0, 0
        for h in range(2):
            shares = jnp.exp(dot(keys[rows, :], queries[h], NT) - log_ref[h : h + 1, :])
            value_part += dot(shares.astype(LOW), split_grads[h])
            share_grad = dot(values[rows, :], split_grads[h], NT)
            score_grad = (shares * (share_grad - centred[h])).astype(LOW)
            key_part += dot(score_grad, queries[h][:, :LANES])
            out.append(carry[h] + dot(turned_keys[64 * h : 64 * h + 64, rows], score_grad))
        key_grad[rows, :] += key_part
        value_grad[rows, :] += value_part
        return tuple(out)

    init = tuple(jnp.zeros((64, here), F32) for _ in range(2))
    done = lax.fori_loop(0, range_ref[1, step], body, init)
    query_grad_ref[...] = (jnp.concatenate(done, axis=0).T * 0.125).astype(LOW)

    @pl.when(step == pl.num_programs(0) - 1)
    def _():
        for place, ref in enumerate((before_grad_ref, own_grad_ref, after_grad_ref)):
            ref[:, :LANES] = key_grad[pl.ds(place * tokens, tokens), :].astype(ref.dtype)
            ref[:, LANES:] = value_grad[pl.ds(place * tokens, tokens), :].astype(ref.dtype)


def key_ranges(spans, query_tile, key_tile):
    first = spans[0, ::query_tile] // LANES
    return jnp.stack([first, (spans[1, query_tile - 1 :: query_tile] - first * LANES + key_tile - 1) // key_tile])


def attention(spans, bounds, queries, before, own, behind):
    tokens, wide = queries.shape
    whole = lambda shape: pl.BlockSpec(shape, lambda i, s: (0, 0))
    tile = pl.BlockSpec((QUERY_TILE, wide), lambda i, s: (i, 0))
    row = pl.BlockSpec((2, QUERY_TILE), lambda i, s: (0, i))
    window = 3 * tokens + KEY_TILE
    return pl.pallas_call(
        attend_kernel,
        grid_spec=pltpu.PrefetchScalarGridSpec(
            num_scalar_prefetch=1,
            grid=(tokens // QUERY_TILE,),
            in_specs=[tile] + [whole((tokens, 2 * wide))] * 3 + [whole(bounds.shape)],
            out_specs=[tile, tile, row],
            scratch_shapes=[pltpu.VMEM((window, 2 * wide), LOW), pltpu.VMEM((wide, window), LOW)],
        ),
        out_shape=[like((tokens, wide), F32), like((tokens, wide), LOW), like((2, tokens), F32)],
        cost_estimate=pl.CostEstimate(
            flops=40 * tokens * tokens * wide, bytes_accessed=16 * tokens * wide, transcendentals=2 * tokens * tokens
        ),
        compiler_params=pltpu.CompilerParams(vmem_limit_bytes=56 << 20),
    )(key_ranges(spans, QUERY_TILE, KEY_TILE), queries, before, own, behind, bounds)


def attention_back(spans, bounds, queries, before, own, behind, mixed, logs, grads):
    tokens, wide = queries.shape
    whole = lambda shape: pl.BlockSpec(shape, lambda i, s: (0, 0))
    tile = pl.BlockSpec((QUERY_TILE, wide), lambda i, s: (i, 0))
    row = pl.BlockSpec((2, QUERY_TILE), lambda i, s: (0, i))
    window = 3 * tokens + KEY_TILE
    return pl.pallas_call(
        attend_back_kernel,
        grid_spec=pltpu.PrefetchScalarGridSpec(
            num_scalar_prefetch=1,
            grid=(tokens // QUERY_TILE,),
            in_specs=[tile] + [whole((tokens, 2 * wide))] * 3 + [whole(bounds.shape), tile, row, tile],
            out_specs=[tile] + [whole((tokens, 2 * wide))] * 3,
            scratch_shapes=[
                pltpu.VMEM((window, 2 * wide), LOW),
                pltpu.VMEM((window, wide), LOW),
                pltpu.VMEM((wide, window), LOW),
                pltpu.VMEM((window, wide), F32),
                pltpu.VMEM((window, wide), F32),
            ],
        ),
        out_shape=[
            like((tokens, wide), LOW),
            like((tokens, 2 * wide), LOW),
            like((tokens, 2 * wide), F32),
            like((tokens, 2 * wide), LOW),
        ],
        cost_estimate=pl.CostEstimate(
            flops=60 * tokens * tokens * wide, bytes_accessed=32 * tokens * wide, transcendentals=2 * tokens * tokens
        ),
        compiler_params=pltpu.CompilerParams(vmem_limit_bytes=56 << 20),
    )(key_ranges(spans, QUERY_TILE, KEY_TILE), queries, before, own, behind, bounds, mixed, logs, grads)


def output_steps(planes):
    return [PLANE << i for i in range(planes.bit_length() - 1)] + [4, 2, 1]


def step_bits(index, steps):
    return sum(bit for i, bit in enumerate(steps) if index >> i & 1)


def place_output(planes, place_ref, refs, out):
    if len(refs) == 1:
        out[...] = refs[0][...]
        return
    devices = PLANE * planes
    rows = out.shape[0] // devices
    steps = output_steps(planes)
    device = place_ref[1] * PLANE + place_ref[0]
    for k, ref in enumerate(refs):
        for i in range(devices // 2):
            bits = step_bits(k * devices // 2 + i, steps)
            out[block_rows(device ^ bits, rows), :] = ref[pl.ds(i * rows, rows), :]


def ordered_output(device, planes, refs):
    devices = PLANE * planes
    rows = 2 * refs[0].shape[0] // devices
    if rows % 16 == 0:
        return refs
    whole = jnp.concatenate(refs, axis=0).reshape(devices, rows, -1)
    steps = output_steps(planes)
    bits = jnp.array([step_bits(i, steps) for i in range(devices)], jnp.int32)
    return [jnp.zeros_like(whole).at[device ^ bits].set(whole).reshape(devices * rows, -1)]


def mix_out_kernel(planes, place_ref, mixed_ref, tokens_ref, vector_ref, *refs):
    output_refs, (second_ref, normed_ref, output) = refs[:-3], refs[-3:]
    place_output(planes, place_ref, output_refs, output)
    mixed = jnp.concatenate([mixed_ref[j] for j in range(PLANE)], axis=1)
    second = tokens_ref[...].astype(F32) + dot(mixed, output[...])
    second_ref[...] = second
    unit, _ = norm_parts(second)
    normed_ref[...] = (unit * vector_ref[2:3, :] + vector_ref[3:4, :]).astype(LOW)


def feed_kernel(planes, place_ref, *refs):
    normed_refs, refs = refs[:SPREAD], refs[SPREAD:]
    cot_refs, refs = refs[:2], refs[2:]
    shrink_refs, refs = refs[:planes], refs[planes:]
    expand_refs, refs = refs[:2], refs[2:]
    bias_ref, near_out, far_out, corner_out, active_ref, grad_ref, bias_out, expand, shrink, x, c = refs
    part = expand.shape[1] // 2
    expand[:, :part] = expand_refs[0][...]
    expand[:, part:] = expand_refs[1][...]
    gather_planes(place_ref[1], shrink_refs, shrink)
    join(normed_refs, x)
    join(cot_refs, c)
    number = near_out.shape[1]
    sums = jnp.zeros(bias_ref.shape, F32)
    for k, m in ((1, 2), (1, 0), (0, 2), (0, 0)):
        rows = pl.ds((4 * k + m) * number, 2 * number)
        upper = dot(x[rows, :], expand[...]) + bias_ref[...]
        share = 0.5 + 0.5 * lax.erf(upper * 0.7071067811865476)
        density = 0.3989422804014327 * jnp.exp(-0.5 * upper * upper)
        active_ref[rows, :] = (upper * share).astype(LOW)
        grad = (dot(c[rows, :], shrink[...], NT) * (share + upper * density)).astype(LOW)
        grad_ref[rows, :] = grad
        sums += jnp.sum(grad.astype(F32), axis=0, keepdims=True)
        down = dot(grad, expand[...], NT)
        put_block((near_out, far_out, corner_out), k, m, down[:number])
        put_block((near_out, far_out, corner_out), k, m + 1, down[number:])
    bias_out[...] = sums


def plane_blocks(plane, whole, outs):
    planes = len(outs)
    tall = whole.shape[0] // planes
    for s, out in enumerate(outs):
        out[...] = whole[block_rows(lax.rem(plane + s, planes), tall), :].astype(out.dtype)


def shrink_grad_kernel(place_ref, active_ref, *refs):
    cot_refs, outs, (whole, cotangents) = refs[:2], refs[2:-2], refs[-2:]
    join(cot_refs, cotangents)
    whole[...] = dot(active_ref[...], cotangents[...], TN)
    plane_blocks(place_ref[1], whole, outs)


def expand_grad_kernel(grad_ref, *refs):
    normed_refs, (out_ref, normed) = refs[:SPREAD], refs[SPREAD:]
    join(normed_refs, normed)
    out_ref[...] = dot(normed[...], grad_ref[...], TN).astype(LOW)


def norm_two_back_kernel(
    planes, place_ref, one_ref, two_ref, three_ref, second_ref, cotangent_ref, vector_ref, *refs
):
    output_refs, (second_grad_ref, branch_ref, mixed_ref, sums_ref, output) = refs[:-5], refs[-5:]
    place_output(planes, place_ref, output_refs, output)
    incoming = one_ref[...] + two_ref[...].astype(F32) + three_ref[...].astype(F32)
    unit, inverse = norm_parts(second_ref[...])
    cotangent = cotangent_ref[...].astype(F32)
    second_grad = cotangent + norm_back(unit, inverse, vector_ref[2:3, :], incoming)
    second_grad_ref[...] = second_grad
    branch = second_grad.astype(LOW)
    branch_ref[...] = branch
    mixed = dot(branch, output[...], NT).astype(LOW)
    wide = mixed_ref.shape[2]
    for j in range(PLANE):
        mixed_ref[j] = mixed[:, wide * j : wide * j + wide]
    sums_ref[...] = jnp.concatenate(
        [
            jnp.sum(incoming * unit, axis=0, keepdims=True),
            jnp.sum(incoming, axis=0, keepdims=True),
            jnp.sum(cotangent, axis=0, keepdims=True),
        ],
        axis=0,
    )


def output_grad_kernel(place_ref, mixed_ref, *refs):
    branch_refs, outs, (whole, left, right) = refs[:2], refs[2:-3], refs[-3:]
    join(branch_refs, right)
    number = right.shape[0] // PLANE
    for r in range(PLANE):
        left[pl.ds(r * number, number), :] = mixed_ref[block_rows(place_ref[0] ^ relative(r), number), :]
    whole[...] = dot(left[...], right[...], TN)
    if len(outs) == 1:
        outs[0][...] = whole[...].astype(LOW)
    else:
        plane_blocks(place_ref[1], whole, outs)


def first_back_kernel(
    planes, place_ref, own_ref, from_after_ref, from_before_ref, query_ref, first_ref, unit_ref,
    weight, two_sums_ref, up_sums_ref, active_ref, *refs
):
    shrink_refs, (grad_ref, near_ref, far_ref, corner_ref, sums_ref, joined, vectors, shrink) = refs[:planes], refs[planes:]
    gather_planes(place_ref[1], shrink_refs, shrink)
    spot = place_ref[0]
    number, columns = near_ref.shape[1] // 2, near_ref.shape[2]
    wide = query_ref.shape[1]
    pairs = (own_ref[...] + from_after_ref[...].astype(F32) + from_before_ref[...].astype(F32)).astype(LOW)
    joined[:, :wide] = query_ref[...]
    joined[:, wide:] = pairs
    grad = dot(first_ref[...], joined[...], TN).astype(LOW)
    gain = jnp.zeros((1, columns), F32)
    shift = jnp.zeros((1, columns), F32)
    for k, m in ((1, 2), (1, 0), (0, 2), (0, 0)):
        part = jnp.concatenate(
            [joined[block_rows(spot ^ (2 * (m + i) + k), number), :] for i in range(2)], axis=0
        )
        down = dot(part, weight[...], NT)
        unit = unit_ref[pl.ds((4 * k + m) * number, 2 * number), :].astype(F32)
        gain += jnp.sum(down * unit, axis=0, keepdims=True)
        shift += jnp.sum(down, axis=0, keepdims=True)
        lower = dot(active_ref[pl.ds((4 * k + m) * number, 2 * number), :], shrink[...])
        outs = (near_ref, far_ref, corner_ref)
        put_block(outs, k, m, jnp.concatenate([down[:number], lower[:number]], axis=0))
        put_block(outs, k, m + 1, jnp.concatenate([down[number:], lower[number:]], axis=0))
    sums_ref[...] = jnp.concatenate([gain, shift], axis=0)
    if len(grad_ref.shape) == 2:
        grad_ref[...] = grad
        return
    devices, tall, _ = grad_ref.shape
    rows = (tall - EXTRA) // 3
    vectors[...] = jnp.zeros_like(vectors)
    vectors[0:2, :] = sums_ref[...]
    vectors[2:5, :] = two_sums_ref[...]
    for g in range(up_sums_ref.shape[1] // LANES):
        lanes = pl.ds(pl.multiple_of(spot * LANES, LANES), LANES)
        vectors[5 + g : 6 + g, lanes] = up_sums_ref[:, g * LANES : (g + 1) * LANES]
    in_lot = LANES // rows
    part = lax.broadcasted_iota(jnp.int32, (EXTRA, LANES), 1) // rows
    top = lax.broadcasted_iota(jnp.int32, (EXTRA, LANES), 0) == 0
    for lot in range(devices // in_lot):
        values = vectors[:EXTRA, lot * LANES : (lot + 1) * LANES]
        last = vectors[EXTRA : EXTRA + 1, lot * LANES : (lot + 1) * LANES]
        last = jnp.concatenate([last[:, LANES - rows :], last[:, : LANES - rows]], axis=1)
        for i in range(in_lot):
            d = lot * in_lot + i
            sums = jnp.where(part == i, values, jnp.where((part == (i + 1) % in_lot) & top, last, 0.0))
            grad_ref[d, 3 * rows :, :] = sums.astype(LOW)
            for c in range(3):
                grad_ref[d, c * rows : (c + 1) * rows, :] = grad[
                    d * rows : (d + 1) * rows, c * wide : (c + 1) * wide
                ]


def last_kernel(one_ref, two_ref, three_ref, tokens_ref, second_grad_ref, second_ref, vector_ref, out_ref, block_ref):
    number = tokens_ref.shape[0]
    both = one_ref[...] + two_ref[...].astype(F32) + three_ref[...].astype(F32)
    unit, inverse = norm_parts(tokens_ref[...].astype(F32))
    back = norm_back(unit, inverse, vector_ref[0:1, :], both[:number])
    out_ref[...] = (second_grad_ref[...] + back).astype(LOW)
    block_ref[...] = (second_ref[...] + both[number:] + vector_ref[4:5, :]).astype(LOW)


def sum_kernel(wide, with_vectors, whole_count, parts_count, square_ref, *refs):
    others, parts, refs = refs[:whole_count], refs[whole_count : whole_count + parts_count], refs[whole_count + parts_count :]
    part_ref, grad_ref, total_ref = refs[:3]
    stacked = with_vectors
    devices = part_ref.shape[0]
    rows = grad_ref.shape[0]
    square = jnp.zeros((rows, wide), F32)
    start = 0
    for c in range(part_ref.shape[2] // wide if not stacked else part_ref.shape[1] // rows):
        here = (slice(c * rows, (c + 1) * rows), slice(None)) if stacked else (slice(rows), slice(c * wide, (c + 1) * wide))
        for j in range(PLANE):
            sources = range(j, devices, PLANE)
            whole = sum(part_ref[(d, *here)].astype(F32) for d in sources)
            grad_ref[:, start : start + wide] = whole
            square += whole * whole
            start += wide
    found = jnp.sum(square, keepdims=True) + square_ref[0]
    for ref in others:
        found += jnp.sum(ref[...] * ref[...], keepdims=True)
    if parts:
        whole = sum(ref[...].astype(F32) for ref in parts)
        refs[-1][...] = whole
        found += jnp.sum(whole * whole, keepdims=True)
    if with_vectors:
        vectors = sum(part_ref[d, 3 * rows :, :].astype(F32) for d in range(devices))
        refs[3][...] = jnp.zeros_like(refs[3])
        refs[3][:EXTRA, :] = vectors
        refs[3][EXTRA : EXTRA + 1, :] = jnp.concatenate([vectors[:1, rows:], vectors[:1, :rows]], axis=1)
        lanes = lax.broadcasted_iota(jnp.int32, (2 * EXTRA, LANES), 1)
        mine = lanes // rows == square_ref[1].astype(jnp.int32)
        found += jnp.sum(jnp.where(mine, refs[3][...] * refs[3][...], 0.0), keepdims=True)
    total_ref[...] = jnp.broadcast_to(found.reshape((1,) * len(total_ref.shape)), total_ref.shape)


def sum_parts(wide, rows, part, square, lot=None, others=(), parts=()):
    vectors = lot is not None
    n, _, columns = part.shape
    columns = 3 * columns if vectors else columns
    if wide % LANES == 0 and rows % 16 == 0:
        outs = [like((rows, PLANE * columns), F32), like((n, 1, LANES) if vectors else (1, 1), F32)]
        found = kernel_call(
            functools.partial(sum_kernel, wide, vectors, len(others), len(parts)),
            outs + [like((2 * EXTRA, LANES), F32)] * vectors + [like(p.shape, F32) for p in parts[:1]],
            *others,
            *parts,
            part,
            scalars=(jnp.stack([square, lot.astype(F32) if vectors else square]),),
        )
        return found
    whole = part.astype(F32)
    if vectors:
        whole = whole[:, : 3 * rows].reshape(n, 3, rows, wide).transpose(0, 2, 1, 3)
    whole = whole.reshape(-1, PLANE, rows, columns // wide, wide).sum(0)
    whole = whole.transpose(1, 2, 0, 3).reshape(rows, -1)
    square = square + jnp.sum(whole * whole) + sum(jnp.sum(g * g) for g in others)
    if not vectors:
        joined = sum(p.astype(F32) for p in parts)
        return whole, (square + jnp.sum(joined * joined)).reshape(1, 1), joined
    found = part[:, 3 * rows :].astype(F32).sum(0)
    found = jnp.concatenate([found, jnp.roll(found[:1], -rows, axis=1)], axis=0)
    mine = lax.dynamic_slice_in_dim(found, rows * lot, rows, axis=1)
    square = square + jnp.sum(mine * mine)
    return whole, jnp.full((n, 1, LANES), square), found


def update_kernel(square_ref, *refs):
    norm = jnp.sqrt(jnp.sum(square_ref[...], axis=0)[:, :1])
    refs[-1][...] = norm
    refs = refs[:-1]
    factor = jnp.minimum(1.0, CLIP_NORM / (norm + 1e-06))
    smooth_rate = min(0.999, (1.0 + STEP) / (10.0 + STEP))
    count = len(LEARNING_RATES)
    states, grads, outs = refs[: 3 * count], refs[3 * count : 4 * count], refs[4 * count :]
    for place, rate in enumerate(LEARNING_RATES):
        weight, moment, average = (ref[...] for ref in states[3 * place : 3 * place + 3])
        clipped = factor * grads[place][...] + WEIGHT_DECAY * weight
        velocity = MOMENTUM * moment + clipped
        updated = weight - rate * (clipped + MOMENTUM * velocity)
        outs[3 * place][...] = velocity
        outs[3 * place + 1][...] = updated
        outs[3 * place + 2][...] = smooth_rate * average + (1.0 - smooth_rate) * updated


def with_vectors(attend_grad, one_sums, two_sums, up_sums, spot, n, rows, hidden):
    columns = attend_grad.shape[0]
    planes, lots, in_lot = n // PLANE, columns // LANES, LANES // rows
    up_sums = lax.dynamic_update_slice_in_dim(
        jnp.zeros((planes, PLANE, hidden), F32), up_sums.reshape(planes, 1, hidden), spot, axis=1
    )
    sums = jnp.concatenate([one_sums, two_sums, up_sums.reshape(-1, columns)], axis=0)
    sums = jnp.moveaxis(sums.reshape(-1, lots, LANES), 1, 0)
    last = jnp.roll(sums[:, EXTRA:], rows, axis=2)
    each, part = jnp.arange(in_lot)[:, None, None], jnp.arange(LANES) // rows
    top = jnp.arange(EXTRA)[:, None] == 0
    sums = jnp.where(
        part == each, sums[:, None, :EXTRA], jnp.where((part == (each + 1) % in_lot) & top, last[:, None], 0.0)
    )
    grad = attend_grad.reshape(n, rows, 3, -1).transpose(0, 2, 1, 3).reshape(n, 3 * rows, -1)
    return jnp.concatenate([grad, sums.astype(LOW).reshape(n, EXTRA, LANES)], axis=1)


def on_device(
    tokens,
    scene_lengths,
    cotangent,
    attend_weight,
    output_weight,
    expand_weight,
    reduce_weight,
    vector_params,
    attend_momentum,
    output_momentum,
    expand_momentum,
    reduce_momentum,
    vector_momentum,
    attend_average,
    output_average,
    expand_average,
    reduce_average,
    vector_average,
):
    n = lax.axis_size("seq")
    planes = n // PLANE
    device = lax.axis_index("seq")
    plane, spot = device // PLANE, device % PLANE
    place = jnp.stack([spot, plane]).astype(jnp.int32)
    number, columns = tokens.shape
    shared = number * PLANE
    rows = columns // n
    hidden = reduce_weight.shape[0]
    wide = columns // PLANE
    lots = columns // LANES
    in_lot = LANES // rows
    inner = planes * hidden
    near_like, far_like = like((4, number, columns), F32), like((3, number, columns), LOW)
    block_like, block_exact = like((number, columns), LOW), like((number, columns), F32)
    shared_scratch = pltpu.VMEM((shared, columns), LOW)
    square_scratch = pltpu.VMEM((columns, columns), LOW)

    vector_low = vector_params.astype(LOW)
    sides = spread_sides(tokens)
    attend = attend_weight.astype(LOW).reshape(rows, 3, PLANE, wide).transpose(2, 1, 0, 3).reshape(PLANE, 3 * rows, wide)
    part, following = device % in_lot, (device + 1) % in_lot
    vector_part = lax.dynamic_update_slice(jnp.zeros((EXTRA, LANES), LOW), vector_low[:EXTRA], (0, rows * part))
    vector_part = lax.dynamic_update_slice(vector_part, vector_low[EXTRA:], (0, rows * following))
    attend = jnp.concatenate(
        [
            jnp.broadcast_to(attend[None], (planes,) + attend.shape).reshape(n, 3 * rows, wide),
            jnp.broadcast_to(vector_part[None], (n,) + vector_part.shape),
        ],
        axis=1,
    )
    attend = exchange(after(attend, *sides))
    pieces = attend[:, 3 * rows :].reshape(lots, in_lot, EXTRA, LANES).astype(F32)
    lane_part = jnp.arange(LANES) // rows
    each = jnp.arange(in_lot)[:, None, None]
    main = jnp.sum(jnp.where(lane_part == each, pieces, 0.0), axis=1)
    last = jnp.sum(jnp.where(lane_part == (each + 1) % in_lot, pieces[:, :, :1], 0.0), axis=1)
    last = jnp.concatenate([last[:, :, rows:], last[:, :, :rows]], axis=2)
    lot_vectors = jnp.concatenate([main, jnp.broadcast_to(last, main.shape)], axis=2)
    if rows % 16:
        attend = attend[:, : 3 * rows].reshape(n, 3, rows, wide).transpose(0, 2, 1, 3).reshape(columns, 3 * wide)
    corner = spread_corner(*sides)
    output = after(output_weight.astype(LOW), *sides)
    for bit in output_steps(planes)[:-3]:
        output = grow(output, bit)
    expand = (
        expand_weight.astype(LOW)
        .reshape(rows, planes, PLANE, hidden)
        .transpose(2, 0, 1, 3)
        .reshape(PLANE, rows, inner)
    )
    expand = jnp.broadcast_to(expand[None], (planes,) + expand.shape).reshape(n, rows, inner)
    expand = [expand[:, :, : inner // 2], expand[:, :, inner // 2 :]]
    shrink = reduce_weight.astype(LOW)
    corner, expand, shrink = tie(corner, expand, shrink)
    gathered = spread_far(tokens, sides, corner)
    gathered, output = tie(gathered, output)

    units, first_low, queries, pairs, attend, vectors = kernel_call(
        project_kernel,
        [
            like((shared, columns), LOW),
            like((shared, columns), LOW),
            like((shared, wide), LOW),
            like((shared, 2 * wide), LOW),
            like((columns, 3 * wide), LOW),
            like((2 * EXTRA, columns), F32),
        ],
        *gathered,
        attend,
        lot_vectors,
        scalars=(place,),
        scratch=[shared_scratch],
        flops=6 * shared * columns * wide,
    )
    bias_up = lax.dynamic_index_in_dim(
        vectors[5 : vector_params.shape[0]].reshape(planes, PLANE, hidden), spot, axis=1, keepdims=False
    ).reshape(1, inner)

    before, behind = move(pairs, PLANE), move(pairs, -PLANE)
    expand[0] = exchange(after(expand[0], pairs)).reshape(columns, inner // 2)
    output = grow(after(output, pairs), 4)
    cotangents = grow(after(cotangent, pairs), 2)
    queries, output, cotangents = tie(queries, output, cotangents)

    finish = jnp.cumsum(scene_lengths)
    begin = finish - scene_lengths
    base = (plane - 1) * shared
    position = plane * shared + jnp.arange(shared, dtype=jnp.int32)
    past = begin[None, :] <= position[:, None]
    span_begin = jnp.max(jnp.where(past, begin[None, :], 0), axis=1) - base
    span_end = jnp.min(jnp.where(finish[None, :] > position[:, None], finish[None, :], 1 << 30), axis=1) - base
    spans = jnp.stack([span_begin, span_end])
    bounds = jnp.stack([begin, finish]) - base
    bounds = jnp.pad(bounds, ((0, 0), (0, LANES - bounds.shape[1])))
    output = grow(output, 2)
    cotangents = grow(cotangents, 4)
    shrink_turns = {1: turn(after(shrink, queries), 1)}
    mixed_exact, mixed_low, logs = attention(spans, bounds, queries, before, pairs, behind)
    mixed_low, output, cotangents, expand[0], shrink_turns = tie(
        mixed_low, output, cotangents, expand[0], shrink_turns
    )

    mixed = exchange(mixed_low.reshape(PLANE, number, wide), plane_groups())
    output = [output, swap(output, 1)]
    cotangents = [cotangents, swap(cotangents, 1)]
    shrink_turns.update({s: turn(after(shrink, mixed_low), s) for s in range(2, planes)})
    output = ordered_output(device, planes, output)
    second, normed = kernel_call(
        functools.partial(mix_out_kernel, planes),
        [block_exact, block_like],
        mixed,
        tokens,
        vectors,
        *output,
        scalars=(place,),
        scratch=[square_scratch],
        flops=2 * number * columns * columns,
    )

    expand[1] = exchange(after(expand[1], mixed)).reshape(columns, inner // 2)
    sides = spread_sides(normed)
    sides, shrink_turns, cotangents = tie(sides, shrink_turns, cotangents)
    corner = spread_corner(*sides)
    shrink = [shrink] + [shrink_turns[s] for s in range(1, planes)]
    normed_all = spread_far(normed, sides, corner)

    inner_low = like((shared, inner), LOW)
    grad_near, grad_far, grad_corner, active, upper_grad, up_sums = kernel_call(
        functools.partial(feed_kernel, planes),
        [near_like, far_like, block_like, inner_low, inner_low, like((1, inner), F32)],
        *normed_all,
        *cotangents,
        *shrink,
        *expand,
        bias_up,
        scalars=(place,),
        scratch=[pltpu.VMEM((columns, inner), LOW), pltpu.VMEM((inner, columns), LOW), shared_scratch, shared_scratch],
        flops=6 * shared * columns * inner,
    )

    normed_grad = collect(grad_near, grad_far, grad_corner)
    shrink_grad = kernel_call(
        shrink_grad_kernel,
        [like((hidden, columns), LOW)] * planes,
        active,
        *cotangents,
        scalars=(place,),
        scratch=[pltpu.VMEM((inner, columns), F32), shared_scratch],
        flops=2 * shared * columns * inner,
    )
    shrink_turns = [turn(shrink_grad[s], s) for s in range(1, planes)]
    normed_grad, shrink_turns[:1] = tie(normed_grad, shrink_turns[:1])
    second_grad, branch_grad, mixed_grad, two_sums = kernel_call(
        functools.partial(norm_two_back_kernel, planes),
        [block_exact, block_like, like((PLANE, number, wide), LOW), like((3, columns), F32)],
        *normed_grad,
        second,
        cotangent,
        vectors,
        *output,
        scalars=(place,),
        scratch=[square_scratch],
        flops=2 * number * columns * columns,
    )

    mixed_grad = exchange(mixed_grad, plane_groups()).reshape(shared, wide)
    (expand_grad,) = kernel_call(
        expand_grad_kernel,
        [like((columns, inner), LOW)],
        after(upper_grad, branch_grad),
        *normed_all,
        scratch=[shared_scratch],
        flops=2 * shared * columns * inner,
    )
    branch_sides = spread_sides(branch_grad)
    mixed_grad, expand_grad, branch_sides, shrink_turns = tie(mixed_grad, expand_grad, branch_sides, shrink_turns)
    shrink_grad = sum(g.astype(F32) for g in [shrink_grad[0], *shrink_turns])

    expand_part = exchange(after(expand_grad, mixed_grad).reshape(n, rows, inner))
    branch_corner = spread_corner(*branch_sides)
    query_grad, before_grad, own_grad, behind_grad = attention_back(
        spans, bounds, queries, before, pairs, behind, mixed_exact, logs, mixed_grad
    )
    before_grad, behind_grad, branch_corner = tie(before_grad, behind_grad, branch_corner)

    from_after, from_before = move(before_grad, -PLANE), move(behind_grad, PLANE)
    branch = jnp.concatenate([branch_grad, *branch_sides, *branch_corner], axis=0)
    output_grad = kernel_call(
        output_grad_kernel,
        [like((rows, columns), LOW)] * planes if rows % 16 == 0 else [like((wide, columns), LOW)],
        mixed_low,
        branch,
        swap(branch, 1),
        scalars=(place,),
        scratch=[pltpu.VMEM((wide, columns), F32), pltpu.VMEM((shared, wide), LOW), shared_scratch],
        flops=2 * shared * columns * wide,
    )
    if len(output_grad) == 1:
        output_grad = jnp.take(
            output_grad[0].reshape(planes, rows, columns), (plane + jnp.arange(planes)) % planes, axis=0, mode="clip"
        )
    output_parts = [
        lax.ppermute(
            output_grad[s],
            "seq",
            [(g * PLANE + j, j * planes + (g + s) % planes) for g in range(planes) for j in range(PLANE)],
        )
        for s in range(planes)
    ]
    from_after, from_before, output_parts[:2] = tie(from_after, from_before, output_parts[:2])

    fused = rows % 16 == 0 and hidden == LANES
    attend_grad, first_near, first_far, first_corner, one_sums = kernel_call(
        functools.partial(first_back_kernel, planes),
        [
            like((n, 3 * rows + EXTRA, wide) if fused else (columns, 3 * wide), LOW),
            like((4, 2 * number, columns), F32),
            like((3, 2 * number, columns), LOW),
            like((2 * number, columns), LOW),
            like((2, columns), F32),
        ],
        own_grad,
        from_after,
        from_before,
        query_grad,
        first_low,
        units,
        attend,
        two_sums,
        up_sums,
        active,
        *shrink,
        scalars=(place,),
        scratch=[
            pltpu.VMEM((shared, 3 * wide), LOW),
            pltpu.VMEM((2 * EXTRA, columns), F32),
            pltpu.VMEM((inner, columns), LOW),
        ],
        flops=2 * shared * columns * 6 * wide,
    )
    more = vector_params.shape[0] - EXTRA
    attend_part = attend_grad
    if not fused:
        attend_part = with_vectors(attend_grad, one_sums, two_sums, up_sums, spot, n, rows, hidden)
    attend_part, first_near, first_far, first_corner, expand_part, output_parts = tie(
        attend_part, first_near, first_far, first_corner, expand_part, output_parts
    )
    attend_part = exchange(attend_part)
    both = collect(first_near, first_far, first_corner)
    input_gradient, block_output = kernel_call(
        last_kernel, [block_like, block_like], *both, tokens, second_grad, second, vectors
    )
    expand_grad, squares, output_grad = sum_parts(
        hidden, rows, expand_part, jnp.zeros((), F32), others=[shrink_grad], parts=output_parts
    )
    attend_grad, squares, vector_grad = sum_parts(wide, rows, attend_part, squares[0, 0], device % in_lot)
    vector_grad = lax.dynamic_slice_in_dim(vector_grad, rows * (device % in_lot), rows, axis=1)
    vector_grad = vector_grad[: vector_params.shape[0]]
    squares, input_gradient, block_output = tie(exchange(squares), input_gradient, block_output)
    states = (
        (attend_weight, attend_momentum, attend_average),
        (output_weight, output_momentum, output_average),
        (expand_weight, expand_momentum, expand_average),
        (reduce_weight, reduce_momentum, reduce_average),
        (vector_params, vector_momentum, vector_average),
    )
    *updates, gradient_norm = kernel_call(
        update_kernel,
        [like(g[0].shape, F32) for g in states for _ in range(3)] + [like((1, 1), F32)],
        squares,
        *[a for g in states for a in g],
        attend_grad,
        output_grad,
        expand_grad,
        shrink_grad,
        vector_grad,
    )
    return (block_output, input_gradient, gradient_norm.reshape(()), *updates)


def solution(mesh):
    split, turned = P("seq", None), P(None, "seq")
    return jax.shard_map(
        on_device,
        mesh=mesh,
        in_specs=(split, P()) + (split,) * 5 + (turned,) + ((split,) * 4 + (turned,)) * 2,
        out_specs=(split, split, P()) + (split,) * 12 + (turned,) * 3,
        check_vma=False,
    )
```

```python
import functools

import jax
import jax.numpy as jnp
from jax import lax
from jax.experimental import pallas as pl
from jax.experimental.pallas import tpu as pltpu
from jax.sharding import PartitionSpec as P

HEADS = 16
STEP = 10
EPSILON = 1e-05
MOMENTUM = 0.9
LEARNING_RATES = (60.0, 480.0, 60.0, 60.0, 600.0)
WEIGHT_DECAY = 0.0001
CLIP_NORM = 1.0
MASK_FLOOR = -1e30
PLANE = 8
EXTRA = 8
LANES = 128
QUERY_TILE = 512
KEY_TILE = 640
F32 = jnp.float32
LOW = jnp.bfloat16
WHOLE = pl.BlockSpec()
SMEM = pl.BlockSpec(memory_space=pltpu.SMEM)


def like(shape, dtype):
    return jax.ShapeDtypeStruct(shape, dtype)


def kernel_call(body, outs, *args, scalars=(), scratch=(), flops=0, limit=56):
    moved = sum(a.size * a.dtype.itemsize for a in list(args) + list(outs))
    return pl.pallas_call(
        body,
        in_specs=[SMEM] * len(scalars) + [WHOLE] * len(args),
        out_specs=[WHOLE] * len(outs),
        out_shape=list(outs),
        scratch_shapes=list(scratch),
        cost_estimate=pl.CostEstimate(flops=flops, bytes_accessed=moved, transcendentals=0),
        compiler_params=pltpu.CompilerParams(vmem_limit_bytes=limit << 20),
    )(*scalars, *args)


def after(value, *others):
    return lax.optimization_barrier((value, *others))[0]


def tie(*values):
    return lax.optimization_barrier(values)


def swap(block, bit):
    n = lax.axis_size("seq")
    return lax.ppermute(block, "seq", [(i, i ^ bit) for i in range(n)])


def move(block, distance):
    n = lax.axis_size("seq")
    return lax.ppermute(
        block, "seq", [(i, i + distance) for i in range(n) if 0 <= i + distance < n]
    )


def turn(block, planes_on):
    n = lax.axis_size("seq")
    return lax.ppermute(block, "seq", [(i, (i + planes_on * PLANE) % n) for i in range(n)])


def plane_groups():
    n = lax.axis_size("seq")
    return [[g * PLANE + j for j in range(PLANE)] for g in range(n // PLANE)]


def cross_groups():
    n = lax.axis_size("seq")
    return [[g * PLANE + j for g in range(n // PLANE)] for j in range(PLANE)]


def exchange(blocks, groups=None):
    return lax.all_to_all(blocks, "seq", 0, 0, axis_index_groups=groups)


def spread_sides(block):
    return swap(block, 2), swap(block, 4)


def spread_corner(across, along):
    half = across.shape[0] // 2
    return swap(across[:half], 4), swap(along[half:], 2)


def grow(block, bit):
    return jnp.concatenate([block, swap(block, bit)], axis=0)


def spread_far(block, sides, corner):
    far = swap(jnp.stack([block, *sides]), 1)
    return [block, *sides, *corner, far, *[swap(c, 1) for c in corner]]


def spread(block):
    sides = spread_sides(block)
    return spread_far(block, sides, spread_corner(*sides))


SPREAD = 8


def join(refs, out):
    number = refs[0].shape[0]
    place = 0
    for ref in refs:
        if len(ref.shape) == 3:
            for m in range(ref.shape[0]):
                out[pl.ds(place, number), :] = ref[m]
                place += number
        else:
            out[pl.ds(place, ref.shape[0]), :] = ref[...]
            place += ref.shape[0]


def collect(near, far, far_corner):
    return collect_came(near, swap(far_corner, 1), swap(far, 1))


def collect_came(near, came_corner, came):
    half = near.shape[1] // 2
    corner = (near[3] + came_corner.astype(F32)).astype(LOW)
    by_across = swap(corner[:half], 2).astype(F32)
    by_along = swap(corner[half:], 4).astype(F32)
    across = near[1] + came[1].astype(F32)
    along = near[2] + came[2].astype(F32)
    across = jnp.concatenate([across[:half], across[half:] + by_along], axis=0).astype(LOW)
    along = jnp.concatenate([along[:half] + by_across, along[half:]], axis=0).astype(LOW)
    return near[0] + came[0].astype(F32), swap(across, 2), swap(along, 4)


def put_block(outs, k, m, value):
    if k == 0:
        outs[0][m] = value
    elif m < 3:
        outs[1][m] = value.astype(LOW)
    else:
        outs[2][...] = value.astype(LOW)


def total(terms):
    return terms[0] + terms[1].astype(F32) + terms[2].astype(F32)


def norm_parts(values):
    centre = values - jnp.mean(values, axis=-1, keepdims=True)
    spread_of = jnp.mean(centre * centre, axis=-1, keepdims=True)
    inverse = lax.rsqrt(spread_of + EPSILON)
    return centre * inverse, inverse


def norm_back(unit, inverse, gain, incoming):
    scaled = incoming * gain
    return inverse * (
        scaled
        - jnp.mean(scaled, axis=-1, keepdims=True)
        - unit * jnp.mean(scaled * unit, axis=-1, keepdims=True)
    )


def dot(a, b, dims=((1,), (0,))):
    return lax.dot_general(a, b, (dims, ((), ())), preferred_element_type=F32)


NT = ((1,), (1,))
TN = ((0,), (0,))


def block_rows(place, number):
    return pl.ds(pl.multiple_of(place * number, number), number)


def gather_planes(plane, refs, out):
    planes = len(refs)
    rows = refs[0].shape[0]
    for s, ref in enumerate(refs):
        out[block_rows(lax.rem(plane - s + planes, planes), rows), :] = ref[...]


def project_kernel(spot_ref, *refs):
    token_refs, refs = refs[:SPREAD], refs[SPREAD:]
    sent_ref, lots_ref, unit_ref, first_ref, query_ref, pair_ref, weight_ref, vector_ref, held = refs
    spot = spot_ref[0]
    number, columns = token_refs[0].shape
    devices = sent_ref.shape[0]
    rows = columns // devices
    if len(sent_ref.shape) == 2:
        weight_ref[...] = sent_ref[...]
    wide = query_ref.shape[1]
    for d in range(devices if len(sent_ref.shape) == 3 else 0):
        for c in range(3):
            weight_ref[pl.ds(d * rows, rows), c * wide : (c + 1) * wide] = sent_ref[d, c * rows : (c + 1) * rows, :]
    for g in range(lots_ref.shape[0]):
        lanes = slice(g * LANES, (g + 1) * LANES)
        vector_ref[:EXTRA, lanes] = lots_ref[g, :, :LANES]
        vector_ref[EXTRA:, lanes] = lots_ref[g, :, LANES : 2 * LANES]
    join(token_refs, held)
    gain, shift = vector_ref[0:1, :], vector_ref[1:2, :]
    for r in range(PLANE):
        here = pl.ds(r * number, number)
        unit, _ = norm_parts(held[here, :].astype(F32))
        first = (unit * gain + shift).astype(LOW)
        unit_ref[here, :] = unit.astype(LOW)
        held[here, :] = first
        first_ref[block_rows(spot ^ relative(r), number), :] = first
    joined = dot(held[...], weight_ref[...]).astype(LOW)
    for r in range(PLANE):
        here = slice(r * number, (r + 1) * number)
        query_ref[block_rows(spot ^ relative(r), number), :] = joined[here, :wide]
        pair_ref[block_rows(spot ^ relative(r), number), :] = joined[here, wide:]


def relative(r):
    return 2 * (r % 4) + r // 4


def head_part(array, head):
    lanes = lax.broadcasted_iota(jnp.int32, array.shape, len(array.shape) - 1)
    return jnp.where(lanes // 64 == head, array, jnp.zeros_like(array))


def scene_marks(bound_ref, first, count, inside, outside):
    place = first + lax.broadcasted_iota(jnp.int32, (count, LANES), 0)
    here = (place >= bound_ref[0:1, :]) & (place < bound_ref[1:2, :])
    return jnp.where(here, inside, outside).astype(LOW)


def marked_queries(bound_ref, query_ref, first):
    queries = query_ref[...] * jnp.asarray(0.125, LOW)
    marks = scene_marks(bound_ref, first, queries.shape[0], MASK_FLOOR, 0.0)
    return [jnp.concatenate([head_part(queries, h), marks], axis=1) for h in range(2)]


def marked_keys(bound_ref, refs, keys):
    tokens = refs[0].shape[0]
    for place, ref in enumerate(refs):
        keys[pl.ds(place * tokens, tokens), :LANES] = ref[:, :LANES]
        keys[pl.ds(place * tokens, tokens), LANES:] = scene_marks(bound_ref, place * tokens, tokens, 0.0, 1.0)
    keys[3 * tokens :, :LANES] = jnp.zeros((keys.shape[0] - 3 * tokens, LANES), LOW)
    keys[3 * tokens :, LANES:] = jnp.ones((keys.shape[0] - 3 * tokens, LANES), LOW)


def attend_kernel(
    range_ref, query_ref, before_ref, own_ref, after_ref, bound_ref, mixed_ref, low_ref, log_ref, keys, values
):
    step = pl.program_id(0)
    tokens = own_ref.shape[0]
    here = query_ref.shape[0]

    @pl.when(step == 0)
    def _():
        refs = (before_ref, own_ref, after_ref)
        marked_keys(bound_ref, refs, keys)
        for place, ref in enumerate(refs):
            values[:, pl.ds(place * tokens, tokens)] = ref[:, LANES:].T
        values[:, 3 * tokens :] = jnp.zeros((LANES, values.shape[1] - 3 * tokens), LOW)

    queries = marked_queries(bound_ref, query_ref, tokens + step * here)
    origin = range_ref[0, step] * LANES

    def body(index, carry):
        start = pl.multiple_of(origin + index * KEY_TILE, LANES)
        block = keys[pl.ds(start, KEY_TILE), :]
        out = []
        for h in range(2):
            peak, whole, mixed = carry[h]
            scores = dot(block, queries[h], NT)
            raised_peak = jnp.maximum(peak, jnp.max(scores, axis=0, keepdims=True))
            raised = jnp.exp(scores - raised_peak)
            fade = jnp.exp(peak - raised_peak)
            whole = whole * fade + jnp.sum(raised, axis=0, keepdims=True)
            turned = values[64 * h : 64 * h + 64, pl.ds(start, KEY_TILE)]
            mixed = mixed * fade + dot(turned, raised.astype(LOW))
            out.append((raised_peak, whole, mixed))
        return tuple(out)

    init = tuple(
        (jnp.full((1, here), MASK_FLOOR, F32), jnp.zeros((1, here), F32), jnp.zeros((64, here), F32))
        for _ in range(2)
    )
    done = lax.fori_loop(0, range_ref[1, step], body, init)
    mixed = jnp.concatenate([m / t for _, t, m in done], axis=0).T
    mixed_ref[...] = mixed
    low_ref[...] = mixed.astype(LOW)
    log_ref[...] = jnp.concatenate([k + jnp.log(t) for k, t, _ in done], axis=0)


def attend_back_kernel(
    range_ref,
    query_ref,
    before_ref,
    own_ref,
    after_ref,
    bound_ref,
    mixed_ref,
    log_ref,
    grad_ref,
    query_grad_ref,
    before_grad_ref,
    own_grad_ref,
    after_grad_ref,
    keys,
    values,
    turned_keys,
    key_grad,
    value_grad,
):
    step = pl.program_id(0)
    tokens = own_ref.shape[0]
    here = query_ref.shape[0]

    @pl.when(step == 0)
    def _():
        refs = (before_ref, own_ref, after_ref)
        marked_keys(bound_ref, refs, keys)
        for place, ref in enumerate(refs):
            values[pl.ds(place * tokens, tokens), :] = ref[:, LANES:]
            turned_keys[:, pl.ds(place * tokens, tokens)] = ref[:, :LANES].T
        values[3 * tokens :, :] = jnp.zeros((values.shape[0] - 3 * tokens, LANES), LOW)
        turned_keys[:, 3 * tokens :] = jnp.zeros((LANES, values.shape[0] - 3 * tokens), LOW)
        key_grad[...] = jnp.zeros_like(key_grad)
        value_grad[...] = jnp.zeros_like(value_grad)

    queries = marked_queries(bound_ref, query_ref, tokens + step * here)
    grads = grad_ref[...]
    split_grads = [head_part(grads, h) for h in range(2)]
    product = (grads.astype(F32) * mixed_ref[...]).T
    centred = [jnp.sum(product[64 * h : 64 * h + 64], axis=0, keepdims=True) for h in range(2)]
    origin = range_ref[0, step] * LANES

    def body(index, carry):
        start = pl.multiple_of(origin + index * KEY_TILE, LANES)
        rows = pl.ds(start, KEY_TILE)
        out, key_part, value_part = [], 0, 0
        for h in range(2):
            shares = jnp.exp(dot(keys[rows, :], queries[h], NT) - log_ref[h : h + 1, :])
            value_part += dot(shares.astype(LOW), split_grads[h])
            share_grad = dot(values[rows, :], split_grads[h], NT)
            score_grad = (shares * (share_grad - centred[h])).astype(LOW)
            key_part += dot(score_grad, queries[h][:, :LANES])
            out.append(carry[h] + dot(turned_keys[64 * h : 64 * h + 64, rows], score_grad))
        key_grad[rows, :] += key_part
        value_grad[rows, :] += value_part
        return tuple(out)

    init = tuple(jnp.zeros((64, here), F32) for _ in range(2))
    done = lax.fori_loop(0, range_ref[1, step], body, init)
    query_grad_ref[...] = (jnp.concatenate(done, axis=0).T * 0.125).astype(LOW)

    @pl.when(step == pl.num_programs(0) - 1)
    def _():
        for place, ref in enumerate((before_grad_ref, own_grad_ref, after_grad_ref)):
            ref[:, :LANES] = key_grad[pl.ds(place * tokens, tokens), :].astype(ref.dtype)
            ref[:, LANES:] = value_grad[pl.ds(place * tokens, tokens), :].astype(ref.dtype)


def key_ranges(spans, query_tile, key_tile):
    first = spans[0, ::query_tile] // LANES
    return jnp.stack([first, (spans[1, query_tile - 1 :: query_tile] - first * LANES + key_tile - 1) // key_tile])


def attention(spans, bounds, queries, before, own, behind):
    tokens, wide = queries.shape
    whole = lambda shape: pl.BlockSpec(shape, lambda i, s: (0, 0))
    tile = pl.BlockSpec((QUERY_TILE, wide), lambda i, s: (i, 0))
    row = pl.BlockSpec((2, QUERY_TILE), lambda i, s: (0, i))
    window = 3 * tokens + KEY_TILE
    return pl.pallas_call(
        attend_kernel,
        grid_spec=pltpu.PrefetchScalarGridSpec(
            num_scalar_prefetch=1,
            grid=(tokens // QUERY_TILE,),
            in_specs=[tile] + [whole((tokens, 2 * wide))] * 3 + [whole(bounds.shape)],
            out_specs=[tile, tile, row],
            scratch_shapes=[pltpu.VMEM((window, 2 * wide), LOW), pltpu.VMEM((wide, window), LOW)],
        ),
        out_shape=[like((tokens, wide), F32), like((tokens, wide), LOW), like((2, tokens), F32)],
        cost_estimate=pl.CostEstimate(
            flops=40 * tokens * tokens * wide, bytes_accessed=16 * tokens * wide, transcendentals=2 * tokens * tokens
        ),
        compiler_params=pltpu.CompilerParams(vmem_limit_bytes=56 << 20),
    )(key_ranges(spans, QUERY_TILE, KEY_TILE), queries, before, own, behind, bounds)


def attention_back(spans, bounds, queries, before, own, behind, mixed, logs, grads):
    tokens, wide = queries.shape
    whole = lambda shape: pl.BlockSpec(shape, lambda i, s: (0, 0))
    tile = pl.BlockSpec((QUERY_TILE, wide), lambda i, s: (i, 0))
    row = pl.BlockSpec((2, QUERY_TILE), lambda i, s: (0, i))
    window = 3 * tokens + KEY_TILE
    return pl.pallas_call(
        attend_back_kernel,
        grid_spec=pltpu.PrefetchScalarGridSpec(
            num_scalar_prefetch=1,
            grid=(tokens // QUERY_TILE,),
            in_specs=[tile] + [whole((tokens, 2 * wide))] * 3 + [whole(bounds.shape), tile, row, tile],
            out_specs=[tile] + [whole((tokens, 2 * wide))] * 3,
            scratch_shapes=[
                pltpu.VMEM((window, 2 * wide), LOW),
                pltpu.VMEM((window, wide), LOW),
                pltpu.VMEM((wide, window), LOW),
                pltpu.VMEM((window, wide), F32),
                pltpu.VMEM((window, wide), F32),
            ],
        ),
        out_shape=[
            like((tokens, wide), LOW),
            like((tokens, 2 * wide), LOW),
            like((tokens, 2 * wide), F32),
            like((tokens, 2 * wide), LOW),
        ],
        cost_estimate=pl.CostEstimate(
            flops=60 * tokens * tokens * wide, bytes_accessed=32 * tokens * wide, transcendentals=2 * tokens * tokens
        ),
        compiler_params=pltpu.CompilerParams(vmem_limit_bytes=56 << 20),
    )(key_ranges(spans, QUERY_TILE, KEY_TILE), queries, before, own, behind, bounds, mixed, logs, grads)


def output_steps(planes):
    return [PLANE << i for i in range(planes.bit_length() - 1)] + [4, 2, 1]


def step_bits(index, steps):
    return sum(bit for i, bit in enumerate(steps) if index >> i & 1)


def place_output(planes, place_ref, refs, out):
    if len(refs) == 1:
        out[...] = refs[0][...]
        return
    devices = PLANE * planes
    rows = out.shape[0] // devices
    steps = output_steps(planes)
    device = place_ref[1] * PLANE + place_ref[0]
    for k, ref in enumerate(refs):
        for i in range(devices // 2):
            bits = step_bits(k * devices // 2 + i, steps)
            out[block_rows(device ^ bits, rows), :] = ref[pl.ds(i * rows, rows), :]


def ordered_output(device, planes, refs):
    devices = PLANE * planes
    rows = 2 * refs[0].shape[0] // devices
    if rows % 16 == 0:
        return refs
    whole = jnp.concatenate(refs, axis=0).reshape(devices, rows, -1)
    steps = output_steps(planes)
    bits = jnp.array([step_bits(i, steps) for i in range(devices)], jnp.int32)
    return [jnp.zeros_like(whole).at[device ^ bits].set(whole).reshape(devices * rows, -1)]


def mix_out_kernel(planes, place_ref, mixed_ref, tokens_ref, vector_ref, *refs):
    output_refs, (second_ref, normed_ref, output) = refs[:-3], refs[-3:]
    place_output(planes, place_ref, output_refs, output)
    mixed = jnp.concatenate([mixed_ref[j] for j in range(PLANE)], axis=1)
    second = tokens_ref[...].astype(F32) + dot(mixed, output[...])
    second_ref[...] = second
    unit, _ = norm_parts(second)
    normed_ref[...] = (unit * vector_ref[2:3, :] + vector_ref[3:4, :]).astype(LOW)


def feed_kernel(planes, place_ref, *refs):
    normed_refs, refs = refs[:SPREAD], refs[SPREAD:]
    cot_refs, refs = refs[:2], refs[2:]
    shrink_refs, refs = refs[:planes], refs[planes:]
    expand_refs, refs = refs[:2], refs[2:]
    bias_ref, near_out, far_out, corner_out, active_ref, grad_ref, bias_out, expand, shrink, x, c = refs
    part = expand.shape[1] // 2
    expand[:, :part] = expand_refs[0][...]
    expand[:, part:] = expand_refs[1][...]
    gather_planes(place_ref[1], shrink_refs, shrink)
    join(normed_refs, x)
    join(cot_refs, c)
    number = near_out.shape[1]
    sums = jnp.zeros(bias_ref.shape, F32)
    for k, m in ((1, 2), (1, 0), (0, 2), (0, 0)):
        rows = pl.ds((4 * k + m) * number, 2 * number)
        upper = dot(x[rows, :], expand[...]) + bias_ref[...]
        share = 0.5 + 0.5 * lax.erf(upper * 0.7071067811865476)
        density = 0.3989422804014327 * jnp.exp(-0.5 * upper * upper)
        active_ref[rows, :] = (upper * share).astype(LOW)
        grad = (dot(c[rows, :], shrink[...], NT) * (share + upper * density)).astype(LOW)
        grad_ref[rows, :] = grad
        sums += jnp.sum(grad.astype(F32), axis=0, keepdims=True)
        down = dot(grad, expand[...], NT)
        put_block((near_out, far_out, corner_out), k, m, down[:number])
        put_block((near_out, far_out, corner_out), k, m + 1, down[number:])
    bias_out[...] = sums


def plane_blocks(plane, whole, outs):
    planes = len(outs)
    tall = whole.shape[0] // planes
    for s, out in enumerate(outs):
        out[...] = whole[block_rows(lax.rem(plane + s, planes), tall), :].astype(out.dtype)


def shrink_grad_kernel(place_ref, active_ref, *refs):
    cot_refs, outs, (whole, cotangents) = refs[:2], refs[2:-2], refs[-2:]
    join(cot_refs, cotangents)
    whole[...] = dot(active_ref[...], cotangents[...], TN)
    plane_blocks(place_ref[1], whole, outs)


def expand_grad_kernel(grad_ref, *refs):
    normed_refs, (out_ref, normed) = refs[:SPREAD], refs[SPREAD:]
    join(normed_refs, normed)
    out_ref[...] = dot(normed[...], grad_ref[...], TN).astype(LOW)


def norm_two_back_kernel(
    planes, place_ref, one_ref, two_ref, three_ref, second_ref, cotangent_ref, vector_ref, *refs
):
    output_refs, (second_grad_ref, branch_ref, mixed_ref, sums_ref, output) = refs[:-5], refs[-5:]
    place_output(planes, place_ref, output_refs, output)
    incoming = one_ref[...] + two_ref[...].astype(F32) + three_ref[...].astype(F32)
    unit, inverse = norm_parts(second_ref[...])
    cotangent = cotangent_ref[...].astype(F32)
    second_grad = cotangent + norm_back(unit, inverse, vector_ref[2:3, :], incoming)
    second_grad_ref[...] = second_grad
    branch = second_grad.astype(LOW)
    branch_ref[...] = branch
    mixed = dot(branch, output[...], NT).astype(LOW)
    wide = mixed_ref.shape[2]
    for j in range(PLANE):
        mixed_ref[j] = mixed[:, wide * j : wide * j + wide]
    sums_ref[...] = jnp.concatenate(
        [
            jnp.sum(incoming * unit, axis=0, keepdims=True),
            jnp.sum(incoming, axis=0, keepdims=True),
            jnp.sum(cotangent, axis=0, keepdims=True),
        ],
        axis=0,
    )


def output_grad_kernel(place_ref, mixed_ref, *refs):
    branch_refs, outs, (whole, left, right) = refs[:2], refs[2:-3], refs[-3:]
    join(branch_refs, right)
    number = right.shape[0] // PLANE
    for r in range(PLANE):
        left[pl.ds(r * number, number), :] = mixed_ref[block_rows(place_ref[0] ^ relative(r), number), :]
    whole[...] = dot(left[...], right[...], TN)
    if len(outs) == 1:
        outs[0][...] = whole[...].astype(LOW)
    else:
        for q, out in enumerate(outs):
            pair = block_rows((place_ref[1] >> 1) ^ q, whole.shape[0] // len(outs))
            out[...] = whole[pair, :].astype(LOW)


def first_back_kernel(
    planes, place_ref, own_ref, from_after_ref, from_before_ref, query_ref, first_ref, unit_ref,
    weight, two_sums_ref, up_sums_ref, active_ref, *refs
):
    shrink_refs, (grad_ref, near_ref, far_ref, corner_ref, sums_ref, joined, vectors, shrink) = refs[:planes], refs[planes:]
    gather_planes(place_ref[1], shrink_refs, shrink)
    spot = place_ref[0]
    number, columns = near_ref.shape[1] // 2, near_ref.shape[2]
    wide = query_ref.shape[1]
    pairs = (own_ref[...] + from_after_ref[...].astype(F32) + from_before_ref[...].astype(F32)).astype(LOW)
    joined[:, :wide] = query_ref[...]
    joined[:, wide:] = pairs
    grad = dot(first_ref[...], joined[...], TN).astype(LOW)
    gain = jnp.zeros((1, columns), F32)
    shift = jnp.zeros((1, columns), F32)
    for k, m in ((1, 2), (1, 0), (0, 2), (0, 0)):
        part = jnp.concatenate(
            [joined[block_rows(spot ^ (2 * (m + i) + k), number), :] for i in range(2)], axis=0
        )
        down = dot(part, weight[...], NT)
        unit = unit_ref[pl.ds((4 * k + m) * number, 2 * number), :].astype(F32)
        gain += jnp.sum(down * unit, axis=0, keepdims=True)
        shift += jnp.sum(down, axis=0, keepdims=True)
        lower = dot(active_ref[pl.ds((4 * k + m) * number, 2 * number), :], shrink[...])
        outs = (near_ref, far_ref, corner_ref)
        put_block(outs, k, m, jnp.concatenate([down[:number], lower[:number]], axis=0))
        put_block(outs, k, m + 1, jnp.concatenate([down[number:], lower[number:]], axis=0))
    sums_ref[...] = jnp.concatenate([gain, shift], axis=0)
    if len(grad_ref.shape) == 2:
        grad_ref[...] = grad
        return
    devices, tall, _ = grad_ref.shape
    rows = (tall - EXTRA) // 3
    vectors[...] = jnp.zeros_like(vectors)
    vectors[0:2, :] = sums_ref[...]
    vectors[2:5, :] = two_sums_ref[...]
    for g in range(up_sums_ref.shape[1] // LANES):
        lanes = pl.ds(pl.multiple_of(spot * LANES, LANES), LANES)
        vectors[5 + g : 6 + g, lanes] = up_sums_ref[:, g * LANES : (g + 1) * LANES]
    in_lot = LANES // rows
    part = lax.broadcasted_iota(jnp.int32, (EXTRA, LANES), 1) // rows
    top = lax.broadcasted_iota(jnp.int32, (EXTRA, LANES), 0) == 0
    for lot in range(devices // in_lot):
        values = vectors[:EXTRA, lot * LANES : (lot + 1) * LANES]
        last = vectors[EXTRA : EXTRA + 1, lot * LANES : (lot + 1) * LANES]
        last = jnp.concatenate([last[:, LANES - rows :], last[:, : LANES - rows]], axis=1)
        for i in range(in_lot):
            d = lot * in_lot + i
            sums = jnp.where(part == i, values, jnp.where((part == (i + 1) % in_lot) & top, last, 0.0))
            grad_ref[d, 3 * rows :, :] = sums.astype(LOW)
            for c in range(3):
                grad_ref[d, c * rows : (c + 1) * rows, :] = grad[
                    d * rows : (d + 1) * rows, c * wide : (c + 1) * wide
                ]


def last_kernel(one_ref, two_ref, three_ref, tokens_ref, second_grad_ref, second_ref, vector_ref, out_ref, block_ref):
    number = tokens_ref.shape[0]
    both = one_ref[...] + two_ref[...].astype(F32) + three_ref[...].astype(F32)
    unit, inverse = norm_parts(tokens_ref[...].astype(F32))
    back = norm_back(unit, inverse, vector_ref[0:1, :], both[:number])
    out_ref[...] = (second_grad_ref[...] + back).astype(LOW)
    block_ref[...] = (second_ref[...] + both[number:] + vector_ref[4:5, :]).astype(LOW)


def sum_kernel(wide, with_vectors, whole_count, parts_count, place_ref, square_ref, *refs):
    others, parts, refs = refs[:whole_count], refs[whole_count : whole_count + parts_count], refs[whole_count + parts_count :]
    part_ref, grad_ref, total_ref = refs[:3]
    stacked = with_vectors
    devices = part_ref.shape[0]
    rows = grad_ref.shape[0]
    square = jnp.zeros((rows, wide), F32)
    start = 0
    for c in range(part_ref.shape[2] // wide if not stacked else part_ref.shape[1] // rows):
        here = (slice(c * rows, (c + 1) * rows), slice(None)) if stacked else (slice(rows), slice(c * wide, (c + 1) * wide))
        for j in range(PLANE):
            sources = range(j, devices, PLANE)
            whole = sum(part_ref[(d, *here)].astype(F32) for d in sources)
            grad_ref[:, start : start + wide] = whole
            square += whole * whole
            start += wide
    found = jnp.sum(square, keepdims=True) + square_ref[...]
    for ref in others:
        found += jnp.sum(ref[...] * ref[...], keepdims=True)
    if parts:
        whole = sum(ref[...].astype(F32) for ref in parts)
        refs[-1][...] = whole
        found += jnp.sum(whole * whole, keepdims=True)
    if with_vectors:
        vectors = sum(part_ref[d, 3 * rows :, :].astype(F32) for d in range(devices))
        refs[3][...] = jnp.zeros_like(refs[3])
        refs[3][:EXTRA, :] = vectors
        refs[3][EXTRA : EXTRA + 1, :] = jnp.concatenate([vectors[:1, rows:], vectors[:1, :rows]], axis=1)
        lanes = lax.broadcasted_iota(jnp.int32, (2 * EXTRA, LANES), 1)
        mine = lanes // rows == lax.rem(place_ref[1] * PLANE + place_ref[0], LANES // rows)
        found += jnp.sum(jnp.where(mine, refs[3][...] * refs[3][...], 0.0), keepdims=True)
    total_ref[...] = jnp.broadcast_to(found.reshape((1,) * len(total_ref.shape)), total_ref.shape)


def sum_parts(wide, rows, part, square, place, lot=None, others=(), parts=()):
    vectors = lot is not None
    n, _, columns = part.shape
    columns = 3 * columns if vectors else columns
    if wide % LANES == 0 and rows % 16 == 0:
        outs = [like((rows, PLANE * columns), F32), like((n, 1, LANES) if vectors else (1, 1), F32)]
        found = kernel_call(
            functools.partial(sum_kernel, wide, vectors, len(others), len(parts)),
            outs + [like((2 * EXTRA, LANES), F32)] * vectors + [like(p.shape, F32) for p in parts[:1]],
            square,
            *others,
            *parts,
            part,
            scalars=(place,),
        )
        return found
    whole = part.astype(F32)
    if vectors:
        whole = whole[:, : 3 * rows].reshape(n, 3, rows, wide).transpose(0, 2, 1, 3)
    whole = whole.reshape(-1, PLANE, rows, columns // wide, wide).sum(0)
    whole = whole.transpose(1, 2, 0, 3).reshape(rows, -1)
    square = square[0, 0] + jnp.sum(whole * whole) + sum(jnp.sum(g * g) for g in others)
    if not vectors:
        return whole, square.reshape(1, 1)
    joined = sum(p.astype(F32) for p in parts)
    found = part[:, 3 * rows :].astype(F32).sum(0)
    found = jnp.concatenate([found, jnp.roll(found[:1], -rows, axis=1)], axis=0)
    mine = lax.dynamic_slice_in_dim(found, rows * lot, rows, axis=1)
    square = square + jnp.sum(mine * mine) + jnp.sum(joined * joined)
    return whole, jnp.full((n, 1, LANES), square), found, joined


def update_kernel(square_ref, *refs):
    norm = jnp.sqrt(jnp.sum(square_ref[...], axis=0)[:, :1])
    refs[-1][...] = norm
    refs = refs[:-1]
    factor = jnp.minimum(1.0, CLIP_NORM / (norm + 1e-06))
    smooth_rate = min(0.999, (1.0 + STEP) / (10.0 + STEP))
    count = len(LEARNING_RATES)
    states, grads, outs = refs[: 3 * count], refs[3 * count : 4 * count], refs[4 * count :]
    for place, rate in enumerate(LEARNING_RATES):
        weight, moment, average = (ref[...] for ref in states[3 * place : 3 * place + 3])
        clipped = factor * grads[place][...] + WEIGHT_DECAY * weight
        velocity = MOMENTUM * moment + clipped
        updated = weight - rate * (clipped + MOMENTUM * velocity)
        outs[3 * place][...] = velocity
        outs[3 * place + 1][...] = updated
        outs[3 * place + 2][...] = smooth_rate * average + (1.0 - smooth_rate) * updated


def with_vectors(attend_grad, one_sums, two_sums, up_sums, spot, n, rows, hidden):
    columns = attend_grad.shape[0]
    planes, lots, in_lot = n // PLANE, columns // LANES, LANES // rows
    up_sums = lax.dynamic_update_slice_in_dim(
        jnp.zeros((planes, PLANE, hidden), F32), up_sums.reshape(planes, 1, hidden), spot, axis=1
    )
    sums = jnp.concatenate([one_sums, two_sums, up_sums.reshape(-1, columns)], axis=0)
    sums = jnp.moveaxis(sums.reshape(-1, lots, LANES), 1, 0)
    last = jnp.roll(sums[:, EXTRA:], rows, axis=2)
    each, part = jnp.arange(in_lot)[:, None, None], jnp.arange(LANES) // rows
    top = jnp.arange(EXTRA)[:, None] == 0
    sums = jnp.where(
        part == each, sums[:, None, :EXTRA], jnp.where((part == (each + 1) % in_lot) & top, last[:, None], 0.0)
    )
    grad = attend_grad.reshape(n, rows, 3, -1).transpose(0, 2, 1, 3).reshape(n, 3 * rows, -1)
    return jnp.concatenate([grad, sums.astype(LOW).reshape(n, EXTRA, LANES)], axis=1)


def on_device(
    tokens,
    scene_lengths,
    cotangent,
    attend_weight,
    output_weight,
    expand_weight,
    reduce_weight,
    vector_params,
    attend_momentum,
    output_momentum,
    expand_momentum,
    reduce_momentum,
    vector_momentum,
    attend_average,
    output_average,
    expand_average,
    reduce_average,
    vector_average,
):
    n = lax.axis_size("seq")
    planes = n // PLANE
    device = lax.axis_index("seq")
    plane, spot = device // PLANE, device % PLANE
    place = jnp.stack([spot, plane]).astype(jnp.int32)
    number, columns = tokens.shape
    shared = number * PLANE
    rows = columns // n
    hidden = reduce_weight.shape[0]
    wide = columns // PLANE
    lots = columns // LANES
    in_lot = LANES // rows
    inner = planes * hidden
    near_like, far_like = like((4, number, columns), F32), like((3, number, columns), LOW)
    block_like, block_exact = like((number, columns), LOW), like((number, columns), F32)
    shared_scratch = pltpu.VMEM((shared, columns), LOW)
    square_scratch = pltpu.VMEM((columns, columns), LOW)

    vector_low = vector_params.astype(LOW)
    sides = spread_sides(tokens)
    attend = attend_weight.astype(LOW).reshape(rows, 3, PLANE, wide).transpose(2, 1, 0, 3).reshape(PLANE, 3 * rows, wide)
    part, following = device % in_lot, (device + 1) % in_lot
    vector_part = lax.dynamic_update_slice(jnp.zeros((EXTRA, LANES), LOW), vector_low[:EXTRA], (0, rows * part))
    vector_part = lax.dynamic_update_slice(vector_part, vector_low[EXTRA:], (0, rows * following))
    attend = jnp.concatenate(
        [
            jnp.broadcast_to(attend[None], (planes,) + attend.shape).reshape(n, 3 * rows, wide),
            jnp.broadcast_to(vector_part[None], (n,) + vector_part.shape),
        ],
        axis=1,
    )
    attend = exchange(after(attend, *sides))
    pieces = attend[:, 3 * rows :].reshape(lots, in_lot, EXTRA, LANES).astype(F32)
    lane_part = jnp.arange(LANES) // rows
    each = jnp.arange(in_lot)[:, None, None]
    main = jnp.sum(jnp.where(lane_part == each, pieces, 0.0), axis=1)
    last = jnp.sum(jnp.where(lane_part == (each + 1) % in_lot, pieces[:, :, :1], 0.0), axis=1)
    last = jnp.concatenate([last[:, :, rows:], last[:, :, :rows]], axis=2)
    lot_vectors = jnp.concatenate([main, jnp.broadcast_to(last, main.shape)], axis=2)
    if rows % 16:
        attend = attend[:, : 3 * rows].reshape(n, 3, rows, wide).transpose(0, 2, 1, 3).reshape(columns, 3 * wide)
    corner = spread_corner(*sides)
    output = after(output_weight.astype(LOW), *sides)
    for bit in output_steps(planes)[:-3]:
        output = grow(output, bit)
    expand = (
        expand_weight.astype(LOW)
        .reshape(rows, planes, PLANE, hidden)
        .transpose(2, 0, 1, 3)
        .reshape(PLANE, rows, inner)
    )
    expand = jnp.broadcast_to(expand[None], (planes,) + expand.shape).reshape(n, rows, inner)
    expand = [expand[:, :, : inner // 2], expand[:, :, inner // 2 :]]
    shrink = reduce_weight.astype(LOW)
    corner, expand, shrink = tie(corner, expand, shrink)
    gathered = spread_far(tokens, sides, corner)
    gathered, output = tie(gathered, output)

    units, first_low, queries, pairs, attend, vectors = kernel_call(
        project_kernel,
        [
            like((shared, columns), LOW),
            like((shared, columns), LOW),
            like((shared, wide), LOW),
            like((shared, 2 * wide), LOW),
            like((columns, 3 * wide), LOW),
            like((2 * EXTRA, columns), F32),
        ],
        *gathered,
        attend,
        lot_vectors,
        scalars=(place,),
        scratch=[shared_scratch],
        flops=6 * shared * columns * wide,
    )
    bias_up = lax.dynamic_index_in_dim(
        vectors[5 : vector_params.shape[0]].reshape(planes, PLANE, hidden), spot, axis=1, keepdims=False
    ).reshape(1, inner)

    before, behind = move(pairs, PLANE), move(pairs, -PLANE)
    expand[0] = exchange(after(expand[0], pairs)).reshape(columns, inner // 2)
    output = grow(after(output, pairs), 4)
    cotangents = grow(after(cotangent, pairs), 2)
    queries, output, cotangents = tie(queries, output, cotangents)

    finish = jnp.cumsum(scene_lengths)
    begin = finish - scene_lengths
    base = (plane - 1) * shared
    position = plane * shared + jnp.arange(shared, dtype=jnp.int32)
    past = begin[None, :] <= position[:, None]
    span_begin = jnp.max(jnp.where(past, begin[None, :], 0), axis=1) - base
    span_end = jnp.min(jnp.where(finish[None, :] > position[:, None], finish[None, :], 1 << 30), axis=1) - base
    spans = jnp.stack([span_begin, span_end])
    bounds = jnp.stack([begin, finish]) - base
    bounds = jnp.pad(bounds, ((0, 0), (0, LANES - bounds.shape[1])))
    output = grow(output, 2)
    cotangents = grow(cotangents, 4)
    shrink_turns = {1: turn(after(shrink, queries), 1)}
    mixed_exact, mixed_low, logs = attention(spans, bounds, queries, before, pairs, behind)
    mixed_low, output, cotangents, expand[0], shrink_turns = tie(
        mixed_low, output, cotangents, expand[0], shrink_turns
    )

    mixed = exchange(mixed_low.reshape(PLANE, number, wide), plane_groups())
    output = [output, swap(output, 1)]
    cotangents = [cotangents, swap(cotangents, 1)]
    shrink_turns.update({s: turn(after(shrink, mixed_low), s) for s in range(2, planes)})
    output = ordered_output(device, planes, output)
    second, normed = kernel_call(
        functools.partial(mix_out_kernel, planes),
        [block_exact, block_like],
        mixed,
        tokens,
        vectors,
        *output,
        scalars=(place,),
        scratch=[square_scratch],
        flops=2 * number * columns * columns,
    )

    expand[1] = exchange(after(expand[1], mixed)).reshape(columns, inner // 2)
    sides = spread_sides(normed)
    sides, shrink_turns, cotangents = tie(sides, shrink_turns, cotangents)
    corner = spread_corner(*sides)
    shrink = [shrink] + [shrink_turns[s] for s in range(1, planes)]
    normed_all = spread_far(normed, sides, corner)

    inner_low = like((shared, inner), LOW)
    grad_near, grad_far, grad_corner, active, upper_grad, up_sums = kernel_call(
        functools.partial(feed_kernel, planes),
        [near_like, far_like, block_like, inner_low, inner_low, like((1, inner), F32)],
        *normed_all,
        *cotangents,
        *shrink,
        *expand,
        bias_up,
        scalars=(place,),
        scratch=[pltpu.VMEM((columns, inner), LOW), pltpu.VMEM((inner, columns), LOW), shared_scratch, shared_scratch],
        flops=6 * shared * columns * inner,
    )

    normed_grad = collect(grad_near, grad_far, grad_corner)
    shrink_grad = kernel_call(
        shrink_grad_kernel,
        [like((hidden, columns), LOW)] * planes,
        active,
        *cotangents,
        scalars=(place,),
        scratch=[pltpu.VMEM((inner, columns), F32), shared_scratch],
        flops=2 * shared * columns * inner,
    )
    shrink_turns = [turn(shrink_grad[s], s) for s in range(1, planes)]
    normed_grad, shrink_turns[:1] = tie(normed_grad, shrink_turns[:1])
    second_grad, branch_grad, mixed_grad, two_sums = kernel_call(
        functools.partial(norm_two_back_kernel, planes),
        [block_exact, block_like, like((PLANE, number, wide), LOW), like((3, columns), F32)],
        *normed_grad,
        second,
        cotangent,
        vectors,
        *output,
        scalars=(place,),
        scratch=[square_scratch],
        flops=2 * number * columns * columns,
    )

    mixed_grad = exchange(mixed_grad, plane_groups()).reshape(shared, wide)
    (expand_grad,) = kernel_call(
        expand_grad_kernel,
        [like((columns, inner), LOW)],
        after(upper_grad, branch_grad),
        *normed_all,
        scratch=[shared_scratch],
        flops=2 * shared * columns * inner,
    )
    branch_sides = spread_sides(branch_grad)
    mixed_grad, expand_grad, branch_sides, shrink_turns = tie(mixed_grad, expand_grad, branch_sides, shrink_turns)
    shrink_grad = sum(g.astype(F32) for g in [shrink_grad[0], *shrink_turns])

    expand_part = exchange(after(expand_grad, mixed_grad).reshape(n, rows, inner))
    branch_corner = spread_corner(*branch_sides)
    query_grad, before_grad, own_grad, behind_grad = attention_back(
        spans, bounds, queries, before, pairs, behind, mixed_exact, logs, mixed_grad
    )
    before_grad, behind_grad, branch_corner = tie(before_grad, behind_grad, branch_corner)

    from_after, from_before = move(before_grad, -PLANE), move(behind_grad, PLANE)
    branch = jnp.concatenate([branch_grad, *branch_sides, *branch_corner], axis=0)
    output_grad = kernel_call(
        output_grad_kernel,
        [like((2 * rows, columns), LOW)] * (planes // 2) if rows % 16 == 0 else [like((wide, columns), LOW)],
        mixed_low,
        branch,
        swap(branch, 1),
        scalars=(place,),
        scratch=[pltpu.VMEM((wide, columns), F32), pltpu.VMEM((shared, wide), LOW), shared_scratch],
        flops=2 * shared * columns * wide,
    )
    if len(output_grad) == 1:
        pairs_of = (plane >> 1) ^ jnp.arange(planes // 2)
        output_grad = jnp.take(output_grad[0].reshape(-1, 2 * rows, columns), pairs_of, axis=0, mode="clip")
    expand_grad, squares = sum_parts(hidden, rows, expand_part, jnp.zeros((1, 1), F32), place, others=[shrink_grad])
    from_after, from_before, output_grad, expand_grad, squares = tie(
        from_after, from_before, output_grad, expand_grad, squares
    )
    output_pairs = [
        lax.ppermute(
            output_grad[q],
            "seq",
            [(g * PLANE + j, j * planes + 2 * ((g >> 1) ^ q) + (g & 1)) for g in range(planes) for j in range(PLANE)],
        )
        for q in range(planes // 2)
    ]

    fused = rows % 16 == 0 and hidden == LANES
    attend_grad, first_near, first_far, first_corner, one_sums = kernel_call(
        functools.partial(first_back_kernel, planes),
        [
            like((n, 3 * rows + EXTRA, wide) if fused else (columns, 3 * wide), LOW),
            like((4, 2 * number, columns), F32),
            like((3, 2 * number, columns), LOW),
            like((2 * number, columns), LOW),
            like((2, columns), F32),
        ],
        own_grad,
        from_after,
        from_before,
        query_grad,
        first_low,
        units,
        attend,
        two_sums,
        up_sums,
        active,
        *shrink,
        scalars=(place,),
        scratch=[
            pltpu.VMEM((shared, 3 * wide), LOW),
            pltpu.VMEM((2 * EXTRA, columns), F32),
            pltpu.VMEM((inner, columns), LOW),
        ],
        flops=2 * shared * columns * 6 * wide,
    )
    more = vector_params.shape[0] - EXTRA
    attend_part = attend_grad
    if not fused:
        attend_part = with_vectors(attend_grad, one_sums, two_sums, up_sums, spot, n, rows, hidden)
    attend_part, first_near, first_far, first_corner, output_pairs = tie(
        attend_part, first_near, first_far, first_corner, output_pairs
    )
    both_cores = sum(g.astype(F32) for g in output_pairs)
    output_parts = [
        lax.dynamic_slice_in_dim(both_cores, rows * (device & 1), rows, axis=0),
        swap(lax.dynamic_slice_in_dim(both_cores, rows * (1 - (device & 1)), rows, axis=0).astype(LOW), 1),
    ]
    attend_part = exchange(attend_part)
    both = collect(first_near, first_far, first_corner)
    input_gradient, block_output = kernel_call(
        last_kernel, [block_like, block_like], *both, tokens, second_grad, second, vectors
    )
    attend_grad, squares, vector_grad, output_grad = sum_parts(
        wide, rows, attend_part, squares, place, device % in_lot, parts=output_parts
    )
    vector_grad = lax.dynamic_slice_in_dim(vector_grad, rows * (device % in_lot), rows, axis=1)
    vector_grad = vector_grad[: vector_params.shape[0]]
    squares, input_gradient, block_output = tie(exchange(squares), input_gradient, block_output)
    states = (
        (attend_weight, attend_momentum, attend_average),
        (output_weight, output_momentum, output_average),
        (expand_weight, expand_momentum, expand_average),
        (reduce_weight, reduce_momentum, reduce_average),
        (vector_params, vector_momentum, vector_average),
    )
    *updates, gradient_norm = kernel_call(
        update_kernel,
        [like(g[0].shape, F32) for g in states for _ in range(3)] + [like((1, 1), F32)],
        squares,
        *[a for g in states for a in g],
        attend_grad,
        output_grad,
        expand_grad,
        shrink_grad,
        vector_grad,
    )
    return (block_output, input_gradient, gradient_norm.reshape(()), *updates)


def solution(mesh):
    split, turned = P("seq", None), P(None, "seq")
    return jax.shard_map(
        on_device,
        mesh=mesh,
        in_specs=(split, P()) + (split,) * 5 + (turned,) + ((split,) * 4 + (turned,)) * 2,
        out_specs=(split, split, P()) + (split,) * 12 + (turned,) * 3,
        check_vma=False,
    )
```

```python
import functools

import jax
import jax.numpy as jnp
from jax import lax
from jax.experimental import pallas as pl
from jax.experimental.pallas import tpu as pltpu
from jax.sharding import PartitionSpec as P

HEADS = 16
STEP = 10
EPSILON = 1e-05
MOMENTUM = 0.9
LEARNING_RATES = (60.0, 480.0, 60.0, 60.0, 600.0)
WEIGHT_DECAY = 0.0001
CLIP_NORM = 1.0
MASK_FLOOR = -1e30
PLANE = 8
EXTRA = 8
LANES = 128
QUERY_TILE = 512
KEY_TILE = 640
F32 = jnp.float32
LOW = jnp.bfloat16
WHOLE = pl.BlockSpec()
SMEM = pl.BlockSpec(memory_space=pltpu.SMEM)


def like(shape, dtype):
    return jax.ShapeDtypeStruct(shape, dtype)


def kernel_call(body, outs, *args, scalars=(), scratch=(), flops=0, limit=53):
    moved = sum(a.size * a.dtype.itemsize for a in list(args) + list(outs))
    return pl.pallas_call(
        body,
        in_specs=[SMEM] * len(scalars) + [WHOLE] * len(args),
        out_specs=[WHOLE] * len(outs),
        out_shape=list(outs),
        scratch_shapes=list(scratch),
        cost_estimate=pl.CostEstimate(flops=flops, bytes_accessed=moved, transcendentals=0),
        compiler_params=pltpu.CompilerParams(vmem_limit_bytes=limit << 20),
    )(*scalars, *args)


def after(value, *others):
    return lax.optimization_barrier((value, *others))[0]


def tie(*values):
    return lax.optimization_barrier(values)


def swap(block, bit):
    n = lax.axis_size("seq")
    return lax.ppermute(block, "seq", [(i, i ^ bit) for i in range(n)])


def move(block, distance):
    n = lax.axis_size("seq")
    return lax.ppermute(
        block, "seq", [(i, i + distance) for i in range(n) if 0 <= i + distance < n]
    )


def turn(block, planes_on):
    n = lax.axis_size("seq")
    return lax.ppermute(block, "seq", [(i, (i + planes_on * PLANE) % n) for i in range(n)])


def plane_groups():
    n = lax.axis_size("seq")
    return [[g * PLANE + j for j in range(PLANE)] for g in range(n // PLANE)]


def cross_groups():
    n = lax.axis_size("seq")
    return [[g * PLANE + j for g in range(n // PLANE)] for j in range(PLANE)]


def exchange(blocks, groups=None):
    return lax.all_to_all(blocks, "seq", 0, 0, axis_index_groups=groups)


def spread_sides(block):
    return swap(block, 2), swap(block, 4)


def spread_corner(across, along):
    half = across.shape[0] // 2
    return swap(across[:half], 4), swap(along[half:], 2)


def grow(block, bit):
    return jnp.concatenate([block, swap(block, bit)], axis=0)


def spread_far(block, sides, corner):
    far = swap(jnp.stack([block, *sides]), 1)
    return [block, *sides, *corner, far, *[swap(c, 1) for c in corner]]


def spread(block):
    sides = spread_sides(block)
    return spread_far(block, sides, spread_corner(*sides))


SPREAD = 8


def join(refs, out):
    number = refs[0].shape[0]
    place = 0
    for ref in refs:
        if len(ref.shape) == 3:
            for m in range(ref.shape[0]):
                out[pl.ds(place, number), :] = ref[m]
                place += number
        else:
            out[pl.ds(place, ref.shape[0]), :] = ref[...]
            place += ref.shape[0]


def collect(near, far, far_corner):
    return collect_came(near, swap(far_corner, 1), swap(far, 1))


def collect_came(near, came_corner, came):
    half = near.shape[1] // 2
    corner = (near[3] + came_corner.astype(F32)).astype(LOW)
    by_across = swap(corner[:half], 2).astype(F32)
    by_along = swap(corner[half:], 4).astype(F32)
    across = near[1] + came[1].astype(F32)
    along = near[2] + came[2].astype(F32)
    across = jnp.concatenate([across[:half], across[half:] + by_along], axis=0).astype(LOW)
    along = jnp.concatenate([along[:half] + by_across, along[half:]], axis=0).astype(LOW)
    return near[0] + came[0].astype(F32), swap(across, 2), swap(along, 4)


def put_block(outs, k, m, value):
    if k == 0:
        outs[0][m] = value
    elif m < 3:
        outs[1][m] = value.astype(LOW)
    else:
        outs[2][...] = value.astype(LOW)


def total(terms):
    return terms[0] + terms[1].astype(F32) + terms[2].astype(F32)


def norm_parts(values):
    centre = values - jnp.mean(values, axis=-1, keepdims=True)
    spread_of = jnp.mean(centre * centre, axis=-1, keepdims=True)
    inverse = lax.rsqrt(spread_of + EPSILON)
    return centre * inverse, inverse


def norm_back(unit, inverse, gain, incoming):
    scaled = incoming * gain
    return inverse * (
        scaled
        - jnp.mean(scaled, axis=-1, keepdims=True)
        - unit * jnp.mean(scaled * unit, axis=-1, keepdims=True)
    )


def dot(a, b, dims=((1,), (0,))):
    return lax.dot_general(a, b, (dims, ((), ())), preferred_element_type=F32)


NT = ((1,), (1,))
TN = ((0,), (0,))


def block_rows(place, number):
    return pl.ds(pl.multiple_of(place * number, number), number)


def gather_planes(plane, refs, out):
    planes = len(refs)
    rows = refs[0].shape[0]
    for s, ref in enumerate(refs):
        out[block_rows(lax.rem(plane - s + planes, planes), rows), :] = ref[...]


def project_kernel(spot_ref, *refs):
    token_refs, refs = refs[:SPREAD], refs[SPREAD:]
    sent_ref, lots_ref, unit_ref, first_ref, query_ref, pair_ref, weight_ref, vector_ref, held = refs
    spot = spot_ref[0]
    number, columns = token_refs[0].shape
    devices = sent_ref.shape[0]
    rows = columns // devices
    if len(sent_ref.shape) == 2:
        weight_ref[...] = sent_ref[...]
    wide = query_ref.shape[1]
    for d in range(devices if len(sent_ref.shape) == 3 else 0):
        for c in range(3):
            weight_ref[pl.ds(d * rows, rows), c * wide : (c + 1) * wide] = sent_ref[d, c * rows : (c + 1) * rows, :]
    for g in range(lots_ref.shape[0]):
        lanes = slice(g * LANES, (g + 1) * LANES)
        vector_ref[:EXTRA, lanes] = lots_ref[g, :, :LANES]
        vector_ref[EXTRA:, lanes] = lots_ref[g, :, LANES : 2 * LANES]
    join(token_refs, held)
    gain, shift = vector_ref[0:1, :], vector_ref[1:2, :]
    for r in range(PLANE):
        here = pl.ds(r * number, number)
        unit, _ = norm_parts(held[here, :].astype(F32))
        first = (unit * gain + shift).astype(LOW)
        unit_ref[here, :] = unit.astype(LOW)
        held[here, :] = first
        first_ref[block_rows(spot ^ relative(r), number), :] = first
    joined = dot(held[...], weight_ref[...]).astype(LOW)
    for r in range(PLANE):
        here = slice(r * number, (r + 1) * number)
        query_ref[block_rows(spot ^ relative(r), number), :] = joined[here, :wide]
        pair_ref[block_rows(spot ^ relative(r), number), :] = joined[here, wide:]


def relative(r):
    return 2 * (r % 4) + r // 4


def head_part(array, head):
    lanes = lax.broadcasted_iota(jnp.int32, array.shape, len(array.shape) - 1)
    return jnp.where(lanes // 64 == head, array, jnp.zeros_like(array))


def scene_marks(bound_ref, first, count, inside, outside):
    place = first + lax.broadcasted_iota(jnp.int32, (count, LANES), 0)
    here = (place >= bound_ref[0:1, :]) & (place < bound_ref[1:2, :])
    return jnp.where(here, inside, outside).astype(LOW)


def marked_queries(bound_ref, query_ref, first):
    queries = query_ref[...] * jnp.asarray(0.125, LOW)
    marks = scene_marks(bound_ref, first, queries.shape[0], MASK_FLOOR, 0.0)
    return [jnp.concatenate([head_part(queries, h), marks], axis=1) for h in range(2)]


def marked_keys(bound_ref, refs, keys):
    tokens = refs[0].shape[0]
    for place, ref in enumerate(refs):
        keys[pl.ds(place * tokens, tokens), :LANES] = ref[:, :LANES]
        keys[pl.ds(place * tokens, tokens), LANES:] = scene_marks(bound_ref, place * tokens, tokens, 0.0, 1.0)
    keys[3 * tokens :, :LANES] = jnp.zeros((keys.shape[0] - 3 * tokens, LANES), LOW)
    keys[3 * tokens :, LANES:] = jnp.ones((keys.shape[0] - 3 * tokens, LANES), LOW)


def attend_kernel(
    range_ref, query_ref, before_ref, own_ref, after_ref, bound_ref, mixed_ref, low_ref, log_ref, keys, values
):
    step = pl.program_id(0)
    tokens = own_ref.shape[0]
    here = query_ref.shape[0]

    @pl.when(step == 0)
    def _():
        refs = (before_ref, own_ref, after_ref)
        marked_keys(bound_ref, refs, keys)
        for place, ref in enumerate(refs):
            values[:, pl.ds(place * tokens, tokens)] = ref[:, LANES:].T
        values[:, 3 * tokens :] = jnp.zeros((LANES, values.shape[1] - 3 * tokens), LOW)

    queries = marked_queries(bound_ref, query_ref, tokens + step * here)
    origin = range_ref[0, step] * LANES

    def body(index, carry):
        start = pl.multiple_of(origin + index * KEY_TILE, LANES)
        block = keys[pl.ds(start, KEY_TILE), :]
        out = []
        for h in range(2):
            peak, whole, mixed = carry[h]
            scores = dot(block, queries[h], NT)
            raised_peak = jnp.maximum(peak, jnp.max(scores, axis=0, keepdims=True))
            raised = jnp.exp(scores - raised_peak)
            fade = jnp.exp(peak - raised_peak)
            whole = whole * fade + jnp.sum(raised, axis=0, keepdims=True)
            turned = values[64 * h : 64 * h + 64, pl.ds(start, KEY_TILE)]
            mixed = mixed * fade + dot(turned, raised.astype(LOW))
            out.append((raised_peak, whole, mixed))
        return tuple(out)

    init = tuple(
        (jnp.full((1, here), MASK_FLOOR, F32), jnp.zeros((1, here), F32), jnp.zeros((64, here), F32))
        for _ in range(2)
    )
    done = lax.fori_loop(0, range_ref[1, step], body, init)
    mixed = jnp.concatenate([m / t for _, t, m in done], axis=0).T
    mixed_ref[...] = mixed
    low_ref[...] = mixed.astype(LOW)
    log_ref[...] = jnp.concatenate([k + jnp.log(t) for k, t, _ in done], axis=0)


def attend_back_kernel(
    range_ref,
    query_ref,
    before_ref,
    own_ref,
    after_ref,
    bound_ref,
    mixed_ref,
    log_ref,
    grad_ref,
    query_grad_ref,
    before_grad_ref,
    own_grad_ref,
    after_grad_ref,
    keys,
    values,
    turned_keys,
    key_grad,
    value_grad,
):
    step = pl.program_id(0)
    tokens = own_ref.shape[0]
    here = query_ref.shape[0]

    @pl.when(step == 0)
    def _():
        refs = (before_ref, own_ref, after_ref)
        marked_keys(bound_ref, refs, keys)
        for place, ref in enumerate(refs):
            values[pl.ds(place * tokens, tokens), :] = ref[:, LANES:]
            turned_keys[:, pl.ds(place * tokens, tokens)] = ref[:, :LANES].T
        values[3 * tokens :, :] = jnp.zeros((values.shape[0] - 3 * tokens, LANES), LOW)
        turned_keys[:, 3 * tokens :] = jnp.zeros((LANES, values.shape[0] - 3 * tokens), LOW)
        key_grad[...] = jnp.zeros_like(key_grad)
        value_grad[...] = jnp.zeros_like(value_grad)

    queries = marked_queries(bound_ref, query_ref, tokens + step * here)
    grads = grad_ref[...]
    split_grads = [head_part(grads, h) for h in range(2)]
    product = (grads.astype(F32) * mixed_ref[...]).T
    centred = [jnp.sum(product[64 * h : 64 * h + 64], axis=0, keepdims=True) for h in range(2)]
    origin = range_ref[0, step] * LANES

    def body(index, carry):
        start = pl.multiple_of(origin + index * KEY_TILE, LANES)
        rows = pl.ds(start, KEY_TILE)
        out, key_part, value_part = [], 0, 0
        for h in range(2):
            shares = jnp.exp(dot(keys[rows, :], queries[h], NT) - log_ref[h : h + 1, :])
            value_part += dot(shares.astype(LOW), split_grads[h])
            share_grad = dot(values[rows, :], split_grads[h], NT)
            score_grad = (shares * (share_grad - centred[h])).astype(LOW)
            key_part += dot(score_grad, queries[h][:, :LANES])
            out.append(carry[h] + dot(turned_keys[64 * h : 64 * h + 64, rows], score_grad))
        key_grad[rows, :] += key_part
        value_grad[rows, :] += value_part
        return tuple(out)

    init = tuple(jnp.zeros((64, here), F32) for _ in range(2))
    done = lax.fori_loop(0, range_ref[1, step], body, init)
    query_grad_ref[...] = (jnp.concatenate(done, axis=0).T * 0.125).astype(LOW)

    @pl.when(step == pl.num_programs(0) - 1)
    def _():
        for place, ref in enumerate((before_grad_ref, own_grad_ref, after_grad_ref)):
            ref[:, :LANES] = key_grad[pl.ds(place * tokens, tokens), :].astype(ref.dtype)
            ref[:, LANES:] = value_grad[pl.ds(place * tokens, tokens), :].astype(ref.dtype)


def key_ranges(spans, query_tile, key_tile):
    first = spans[0, ::query_tile] // LANES
    return jnp.stack([first, (spans[1, query_tile - 1 :: query_tile] - first * LANES + key_tile - 1) // key_tile])


def attention(spans, bounds, queries, before, own, behind):
    tokens, wide = queries.shape
    whole = lambda shape: pl.BlockSpec(shape, lambda i, s: (0, 0))
    tile = pl.BlockSpec((QUERY_TILE, wide), lambda i, s: (i, 0))
    row = pl.BlockSpec((2, QUERY_TILE), lambda i, s: (0, i))
    window = 3 * tokens + KEY_TILE
    return pl.pallas_call(
        attend_kernel,
        grid_spec=pltpu.PrefetchScalarGridSpec(
            num_scalar_prefetch=1,
            grid=(tokens // QUERY_TILE,),
            in_specs=[tile] + [whole((tokens, 2 * wide))] * 3 + [whole(bounds.shape)],
            out_specs=[tile, tile, row],
            scratch_shapes=[pltpu.VMEM((window, 2 * wide), LOW), pltpu.VMEM((wide, window), LOW)],
        ),
        out_shape=[like((tokens, wide), F32), like((tokens, wide), LOW), like((2, tokens), F32)],
        cost_estimate=pl.CostEstimate(
            flops=40 * tokens * tokens * wide, bytes_accessed=16 * tokens * wide, transcendentals=2 * tokens * tokens
        ),
        compiler_params=pltpu.CompilerParams(vmem_limit_bytes=53 << 20),
    )(key_ranges(spans, QUERY_TILE, KEY_TILE), queries, before, own, behind, bounds)


def attention_back(spans, bounds, queries, before, own, behind, mixed, logs, grads):
    tokens, wide = queries.shape
    whole = lambda shape: pl.BlockSpec(shape, lambda i, s: (0, 0))
    tile = pl.BlockSpec((QUERY_TILE, wide), lambda i, s: (i, 0))
    row = pl.BlockSpec((2, QUERY_TILE), lambda i, s: (0, i))
    window = 3 * tokens + KEY_TILE
    return pl.pallas_call(
        attend_back_kernel,
        grid_spec=pltpu.PrefetchScalarGridSpec(
            num_scalar_prefetch=1,
            grid=(tokens // QUERY_TILE,),
            in_specs=[tile] + [whole((tokens, 2 * wide))] * 3 + [whole(bounds.shape), tile, row, tile],
            out_specs=[tile] + [whole((tokens, 2 * wide))] * 3,
            scratch_shapes=[
                pltpu.VMEM((window, 2 * wide), LOW),
                pltpu.VMEM((window, wide), LOW),
                pltpu.VMEM((wide, window), LOW),
                pltpu.VMEM((window, wide), F32),
                pltpu.VMEM((window, wide), F32),
            ],
        ),
        out_shape=[
            like((tokens, wide), LOW),
            like((tokens, 2 * wide), LOW),
            like((tokens, 2 * wide), F32),
            like((tokens, 2 * wide), LOW),
        ],
        cost_estimate=pl.CostEstimate(
            flops=60 * tokens * tokens * wide, bytes_accessed=32 * tokens * wide, transcendentals=2 * tokens * tokens
        ),
        compiler_params=pltpu.CompilerParams(vmem_limit_bytes=53 << 20),
    )(key_ranges(spans, QUERY_TILE, KEY_TILE), queries, before, own, behind, bounds, mixed, logs, grads)


def output_steps(planes):
    return [PLANE << i for i in range(planes.bit_length() - 1)] + [4, 2, 1]


def step_bits(index, steps):
    return sum(bit for i, bit in enumerate(steps) if index >> i & 1)


def place_output(planes, place_ref, refs, out):
    if len(refs) == 1:
        out[...] = refs[0][...]
        return
    devices = PLANE * planes
    rows = out.shape[0] // devices
    steps = output_steps(planes)
    device = place_ref[1] * PLANE + place_ref[0]
    for k, ref in enumerate(refs):
        for i in range(devices // 2):
            bits = step_bits(k * devices // 2 + i, steps)
            out[block_rows(device ^ bits, rows), :] = ref[pl.ds(i * rows, rows), :]


def ordered_output(device, planes, refs):
    devices = PLANE * planes
    rows = 2 * refs[0].shape[0] // devices
    if rows % 16 == 0:
        return refs
    whole = jnp.concatenate(refs, axis=0).reshape(devices, rows, -1)
    steps = output_steps(planes)
    bits = jnp.array([step_bits(i, steps) for i in range(devices)], jnp.int32)
    return [jnp.zeros_like(whole).at[device ^ bits].set(whole).reshape(devices * rows, -1)]


def mix_out_kernel(planes, place_ref, mixed_ref, tokens_ref, vector_ref, *refs):
    output_refs, (second_ref, normed_ref, output) = refs[:-3], refs[-3:]
    place_output(planes, place_ref, output_refs, output)
    mixed = jnp.concatenate([mixed_ref[j] for j in range(PLANE)], axis=1)
    second = tokens_ref[...].astype(F32) + dot(mixed, output[...])
    second_ref[...] = second
    unit, _ = norm_parts(second)
    normed_ref[...] = (unit * vector_ref[2:3, :] + vector_ref[3:4, :]).astype(LOW)


def feed_kernel(planes, place_ref, *refs):
    normed_refs, refs = refs[:SPREAD], refs[SPREAD:]
    cot_refs, refs = refs[:2], refs[2:]
    shrink_refs, refs = refs[:planes], refs[planes:]
    expand_refs, refs = refs[:2], refs[2:]
    bias_ref, near_out, far_out, corner_out, active_ref, grad_ref, bias_out, expand, shrink, x, c = refs
    part = expand.shape[1] // 2
    expand[:, :part] = expand_refs[0][...]
    expand[:, part:] = expand_refs[1][...]
    gather_planes(place_ref[1], shrink_refs, shrink)
    join(normed_refs, x)
    join(cot_refs, c)
    number = near_out.shape[1]
    sums = jnp.zeros(bias_ref.shape, F32)
    for k, m in ((1, 2), (1, 0), (0, 2), (0, 0)):
        rows = pl.ds((4 * k + m) * number, 2 * number)
        upper = dot(x[rows, :], expand[...]) + bias_ref[...]
        share = 0.5 + 0.5 * lax.erf(upper * 0.7071067811865476)
        density = 0.3989422804014327 * jnp.exp(-0.5 * upper * upper)
        active_ref[rows, :] = (upper * share).astype(LOW)
        grad = (dot(c[rows, :], shrink[...], NT) * (share + upper * density)).astype(LOW)
        grad_ref[rows, :] = grad
        sums += jnp.sum(grad.astype(F32), axis=0, keepdims=True)
        down = dot(grad, expand[...], NT)
        put_block((near_out, far_out, corner_out), k, m, down[:number])
        put_block((near_out, far_out, corner_out), k, m + 1, down[number:])
    bias_out[...] = sums


def plane_blocks(plane, whole, outs):
    planes = len(outs)
    tall = whole.shape[0] // planes
    for s, out in enumerate(outs):
        out[...] = whole[block_rows(lax.rem(plane + s, planes), tall), :].astype(out.dtype)


def shrink_grad_kernel(place_ref, active_ref, *refs):
    cot_refs, outs, (whole, cotangents) = refs[:2], refs[2:-2], refs[-2:]
    join(cot_refs, cotangents)
    whole[...] = dot(active_ref[...], cotangents[...], TN)
    plane_blocks(place_ref[1], whole, outs)


def expand_grad_kernel(grad_ref, *refs):
    normed_refs, (out_ref, normed) = refs[:SPREAD], refs[SPREAD:]
    join(normed_refs, normed)
    out_ref[...] = dot(normed[...], grad_ref[...], TN).astype(LOW)


def norm_two_back_kernel(
    planes, place_ref, one_ref, two_ref, three_ref, second_ref, cotangent_ref, vector_ref, *refs
):
    output_refs, (second_grad_ref, branch_ref, mixed_ref, sums_ref, output) = refs[:-5], refs[-5:]
    place_output(planes, place_ref, output_refs, output)
    incoming = one_ref[...] + two_ref[...].astype(F32) + three_ref[...].astype(F32)
    unit, inverse = norm_parts(second_ref[...])
    cotangent = cotangent_ref[...].astype(F32)
    second_grad = cotangent + norm_back(unit, inverse, vector_ref[2:3, :], incoming)
    second_grad_ref[...] = second_grad
    branch = second_grad.astype(LOW)
    branch_ref[...] = branch
    mixed = dot(branch, output[...], NT).astype(LOW)
    wide = mixed_ref.shape[2]
    for j in range(PLANE):
        mixed_ref[j] = mixed[:, wide * j : wide * j + wide]
    sums_ref[...] = jnp.concatenate(
        [
            jnp.sum(incoming * unit, axis=0, keepdims=True),
            jnp.sum(incoming, axis=0, keepdims=True),
            jnp.sum(cotangent, axis=0, keepdims=True),
        ],
        axis=0,
    )


def output_grad_kernel(place_ref, mixed_ref, *refs):
    branch_refs, outs, (whole, left, right) = refs[:2], refs[2:-3], refs[-3:]
    join(branch_refs, right)
    number = right.shape[0] // PLANE
    for r in range(PLANE):
        left[pl.ds(r * number, number), :] = mixed_ref[block_rows(place_ref[0] ^ relative(r), number), :]
    whole[...] = dot(left[...], right[...], TN)
    if len(outs) == 1:
        outs[0][...] = whole[...].astype(LOW)
    else:
        for q, out in enumerate(outs):
            pair = block_rows((place_ref[1] >> 1) ^ q, whole.shape[0] // len(outs))
            out[...] = whole[pair, :].astype(LOW)


def first_back_kernel(
    planes, place_ref, own_ref, from_after_ref, from_before_ref, query_ref, first_ref, unit_ref,
    weight, two_sums_ref, up_sums_ref, active_ref, *refs
):
    shrink_refs, (grad_ref, near_ref, far_ref, corner_ref, sums_ref, joined, vectors, shrink) = refs[:planes], refs[planes:]
    gather_planes(place_ref[1], shrink_refs, shrink)
    spot = place_ref[0]
    number, columns = near_ref.shape[1] // 2, near_ref.shape[2]
    wide = query_ref.shape[1]
    pairs = (own_ref[...] + from_after_ref[...].astype(F32) + from_before_ref[...].astype(F32)).astype(LOW)
    joined[:, :wide] = query_ref[...]
    joined[:, wide:] = pairs
    grad = dot(first_ref[...], joined[...], TN).astype(LOW)
    gain = jnp.zeros((1, columns), F32)
    shift = jnp.zeros((1, columns), F32)
    for k, m in ((1, 2), (1, 0), (0, 2), (0, 0)):
        part = jnp.concatenate(
            [joined[block_rows(spot ^ (2 * (m + i) + k), number), :] for i in range(2)], axis=0
        )
        down = dot(part, weight[...], NT)
        unit = unit_ref[pl.ds((4 * k + m) * number, 2 * number), :].astype(F32)
        gain += jnp.sum(down * unit, axis=0, keepdims=True)
        shift += jnp.sum(down, axis=0, keepdims=True)
        lower = dot(active_ref[pl.ds((4 * k + m) * number, 2 * number), :], shrink[...])
        outs = (near_ref, far_ref, corner_ref)
        put_block(outs, k, m, jnp.concatenate([down[:number], lower[:number]], axis=0))
        put_block(outs, k, m + 1, jnp.concatenate([down[number:], lower[number:]], axis=0))
    sums_ref[...] = jnp.concatenate([gain, shift], axis=0)
    if len(grad_ref.shape) == 2:
        grad_ref[...] = grad
        return
    devices, tall, _ = grad_ref.shape
    rows = (tall - EXTRA) // 3
    vectors[...] = jnp.zeros_like(vectors)
    vectors[0:2, :] = sums_ref[...]
    vectors[2:5, :] = two_sums_ref[...]
    for g in range(up_sums_ref.shape[1] // LANES):
        lanes = pl.ds(pl.multiple_of(spot * LANES, LANES), LANES)
        vectors[5 + g : 6 + g, lanes] = up_sums_ref[:, g * LANES : (g + 1) * LANES]
    in_lot = LANES // rows
    part = lax.broadcasted_iota(jnp.int32, (EXTRA, LANES), 1) // rows
    top = lax.broadcasted_iota(jnp.int32, (EXTRA, LANES), 0) == 0
    for lot in range(devices // in_lot):
        values = vectors[:EXTRA, lot * LANES : (lot + 1) * LANES]
        last = vectors[EXTRA : EXTRA + 1, lot * LANES : (lot + 1) * LANES]
        last = jnp.concatenate([last[:, LANES - rows :], last[:, : LANES - rows]], axis=1)
        for i in range(in_lot):
            d = lot * in_lot + i
            sums = jnp.where(part == i, values, jnp.where((part == (i + 1) % in_lot) & top, last, 0.0))
            grad_ref[d, 3 * rows :, :] = sums.astype(LOW)
            for c in range(3):
                grad_ref[d, c * rows : (c + 1) * rows, :] = grad[
                    d * rows : (d + 1) * rows, c * wide : (c + 1) * wide
                ]


def last_kernel(one_ref, two_ref, three_ref, tokens_ref, second_grad_ref, second_ref, vector_ref, out_ref, block_ref):
    number = tokens_ref.shape[0]
    both = one_ref[...] + two_ref[...].astype(F32) + three_ref[...].astype(F32)
    unit, inverse = norm_parts(tokens_ref[...].astype(F32))
    back = norm_back(unit, inverse, vector_ref[0:1, :], both[:number])
    out_ref[...] = (second_grad_ref[...] + back).astype(LOW)
    block_ref[...] = (second_ref[...] + both[number:] + vector_ref[4:5, :]).astype(LOW)


def sum_kernel(wide, with_vectors, whole_count, parts_count, place_ref, square_ref, *refs):
    others, parts, refs = refs[:whole_count], refs[whole_count : whole_count + parts_count], refs[whole_count + parts_count :]
    part_ref, grad_ref, total_ref = refs[:3]
    stacked = with_vectors
    devices = part_ref.shape[0]
    rows = grad_ref.shape[0]
    square = jnp.zeros((rows, wide), F32)
    start = 0
    for c in range(part_ref.shape[2] // wide if not stacked else part_ref.shape[1] // rows):
        here = (slice(c * rows, (c + 1) * rows), slice(None)) if stacked else (slice(rows), slice(c * wide, (c + 1) * wide))
        for j in range(PLANE):
            sources = range(j, devices, PLANE)
            whole = sum(part_ref[(d, *here)].astype(F32) for d in sources)
            grad_ref[:, start : start + wide] = whole
            square += whole * whole
            start += wide
    found = jnp.sum(square, keepdims=True) + square_ref[...]
    for ref in others:
        found += jnp.sum(ref[...] * ref[...], keepdims=True)
    if parts:
        whole = sum(ref[...].astype(F32) for ref in parts)
        refs[-1][...] = whole
        found += jnp.sum(whole * whole, keepdims=True)
    if with_vectors:
        vectors = sum(part_ref[d, 3 * rows :, :].astype(F32) for d in range(devices))
        refs[3][...] = jnp.zeros_like(refs[3])
        refs[3][:EXTRA, :] = vectors
        refs[3][EXTRA : EXTRA + 1, :] = jnp.concatenate([vectors[:1, rows:], vectors[:1, :rows]], axis=1)
        lanes = lax.broadcasted_iota(jnp.int32, (2 * EXTRA, LANES), 1)
        mine = lanes // rows == lax.rem(place_ref[1] * PLANE + place_ref[0], LANES // rows)
        found += jnp.sum(jnp.where(mine, refs[3][...] * refs[3][...], 0.0), keepdims=True)
    total_ref[...] = jnp.broadcast_to(found.reshape((1,) * len(total_ref.shape)), total_ref.shape)


def sum_parts(wide, rows, part, square, place, lot=None, others=(), parts=()):
    vectors = lot is not None
    n, _, columns = part.shape
    columns = 3 * columns if vectors else columns
    if wide % LANES == 0 and rows % 16 == 0:
        outs = [like((rows, PLANE * columns), F32), like((n, 1, LANES) if vectors else (1, 1), F32)]
        found = kernel_call(
            functools.partial(sum_kernel, wide, vectors, len(others), len(parts)),
            outs + [like((2 * EXTRA, LANES), F32)] * vectors + [like(p.shape, F32) for p in parts[:1]],
            square,
            *others,
            *parts,
            part,
            scalars=(place,),
        )
        return found
    whole = part.astype(F32)
    if vectors:
        whole = whole[:, : 3 * rows].reshape(n, 3, rows, wide).transpose(0, 2, 1, 3)
    whole = whole.reshape(-1, PLANE, rows, columns // wide, wide).sum(0)
    whole = whole.transpose(1, 2, 0, 3).reshape(rows, -1)
    square = square[0, 0] + jnp.sum(whole * whole) + sum(jnp.sum(g * g) for g in others)
    if not vectors:
        return whole, square.reshape(1, 1)
    joined = sum(p.astype(F32) for p in parts)
    found = part[:, 3 * rows :].astype(F32).sum(0)
    found = jnp.concatenate([found, jnp.roll(found[:1], -rows, axis=1)], axis=0)
    mine = lax.dynamic_slice_in_dim(found, rows * lot, rows, axis=1)
    square = square + jnp.sum(mine * mine) + jnp.sum(joined * joined)
    return whole, jnp.full((n, 1, LANES), square), found, joined


def update_kernel(square_ref, *refs):
    norm = jnp.sqrt(jnp.sum(square_ref[...], axis=0)[:, :1])
    refs[-1][...] = norm
    refs = refs[:-1]
    factor = jnp.minimum(1.0, CLIP_NORM / (norm + 1e-06))
    smooth_rate = min(0.999, (1.0 + STEP) / (10.0 + STEP))
    count = len(LEARNING_RATES)
    states, grads, outs = refs[: 3 * count], refs[3 * count : 4 * count], refs[4 * count :]
    for place, rate in enumerate(LEARNING_RATES):
        weight, moment, average = (ref[...] for ref in states[3 * place : 3 * place + 3])
        clipped = factor * grads[place][...] + WEIGHT_DECAY * weight
        velocity = MOMENTUM * moment + clipped
        updated = weight - rate * (clipped + MOMENTUM * velocity)
        outs[3 * place][...] = velocity
        outs[3 * place + 1][...] = updated
        outs[3 * place + 2][...] = smooth_rate * average + (1.0 - smooth_rate) * updated


def with_vectors(attend_grad, one_sums, two_sums, up_sums, spot, n, rows, hidden):
    columns = attend_grad.shape[0]
    planes, lots, in_lot = n // PLANE, columns // LANES, LANES // rows
    up_sums = lax.dynamic_update_slice_in_dim(
        jnp.zeros((planes, PLANE, hidden), F32), up_sums.reshape(planes, 1, hidden), spot, axis=1
    )
    sums = jnp.concatenate([one_sums, two_sums, up_sums.reshape(-1, columns)], axis=0)
    sums = jnp.moveaxis(sums.reshape(-1, lots, LANES), 1, 0)
    last = jnp.roll(sums[:, EXTRA:], rows, axis=2)
    each, part = jnp.arange(in_lot)[:, None, None], jnp.arange(LANES) // rows
    top = jnp.arange(EXTRA)[:, None] == 0
    sums = jnp.where(
        part == each, sums[:, None, :EXTRA], jnp.where((part == (each + 1) % in_lot) & top, last[:, None], 0.0)
    )
    grad = attend_grad.reshape(n, rows, 3, -1).transpose(0, 2, 1, 3).reshape(n, 3 * rows, -1)
    return jnp.concatenate([grad, sums.astype(LOW).reshape(n, EXTRA, LANES)], axis=1)


def on_device(
    tokens,
    scene_lengths,
    cotangent,
    attend_weight,
    output_weight,
    expand_weight,
    reduce_weight,
    vector_params,
    attend_momentum,
    output_momentum,
    expand_momentum,
    reduce_momentum,
    vector_momentum,
    attend_average,
    output_average,
    expand_average,
    reduce_average,
    vector_average,
):
    n = lax.axis_size("seq")
    planes = n // PLANE
    device = lax.axis_index("seq")
    plane, spot = device // PLANE, device % PLANE
    place = jnp.stack([spot, plane]).astype(jnp.int32)
    number, columns = tokens.shape
    shared = number * PLANE
    rows = columns // n
    hidden = reduce_weight.shape[0]
    wide = columns // PLANE
    lots = columns // LANES
    in_lot = LANES // rows
    inner = planes * hidden
    near_like, far_like = like((4, number, columns), F32), like((3, number, columns), LOW)
    block_like, block_exact = like((number, columns), LOW), like((number, columns), F32)
    shared_scratch = pltpu.VMEM((shared, columns), LOW)
    square_scratch = pltpu.VMEM((columns, columns), LOW)

    vector_low = vector_params.astype(LOW)
    sides = spread_sides(tokens)
    attend = attend_weight.astype(LOW).reshape(rows, 3, PLANE, wide).transpose(2, 1, 0, 3).reshape(PLANE, 3 * rows, wide)
    part, following = device % in_lot, (device + 1) % in_lot
    vector_part = lax.dynamic_update_slice(jnp.zeros((EXTRA, LANES), LOW), vector_low[:EXTRA], (0, rows * part))
    vector_part = lax.dynamic_update_slice(vector_part, vector_low[EXTRA:], (0, rows * following))
    attend = jnp.concatenate(
        [
            jnp.broadcast_to(attend[None], (planes,) + attend.shape).reshape(n, 3 * rows, wide),
            jnp.broadcast_to(vector_part[None], (n,) + vector_part.shape),
        ],
        axis=1,
    )
    attend = exchange(after(attend, *sides))
    pieces = attend[:, 3 * rows :].reshape(lots, in_lot, EXTRA, LANES).astype(F32)
    lane_part = jnp.arange(LANES) // rows
    each = jnp.arange(in_lot)[:, None, None]
    main = jnp.sum(jnp.where(lane_part == each, pieces, 0.0), axis=1)
    last = jnp.sum(jnp.where(lane_part == (each + 1) % in_lot, pieces[:, :, :1], 0.0), axis=1)
    last = jnp.concatenate([last[:, :, rows:], last[:, :, :rows]], axis=2)
    lot_vectors = jnp.concatenate([main, jnp.broadcast_to(last, main.shape)], axis=2)
    if rows % 16:
        attend = attend[:, : 3 * rows].reshape(n, 3, rows, wide).transpose(0, 2, 1, 3).reshape(columns, 3 * wide)
    corner = spread_corner(*sides)
    output = after(output_weight.astype(LOW), *sides)
    for bit in output_steps(planes)[:-3]:
        output = grow(output, bit)
    expand = (
        expand_weight.astype(LOW)
        .reshape(rows, planes, PLANE, hidden)
        .transpose(2, 0, 1, 3)
        .reshape(PLANE, rows, inner)
    )
    expand = jnp.broadcast_to(expand[None], (planes,) + expand.shape).reshape(n, rows, inner)
    expand = [expand[:, :, : inner // 2], expand[:, :, inner // 2 :]]
    shrink = reduce_weight.astype(LOW)
    corner, expand, shrink = tie(corner, expand, shrink)
    gathered = spread_far(tokens, sides, corner)
    gathered, output = tie(gathered, output)

    units, first_low, queries, pairs, attend, vectors = kernel_call(
        project_kernel,
        [
            like((shared, columns), LOW),
            like((shared, columns), LOW),
            like((shared, wide), LOW),
            like((shared, 2 * wide), LOW),
            like((columns, 3 * wide), LOW),
            like((2 * EXTRA, columns), F32),
        ],
        *gathered,
        attend,
        lot_vectors,
        scalars=(place,),
        scratch=[shared_scratch],
        flops=6 * shared * columns * wide,
    )
    bias_up = lax.dynamic_index_in_dim(
        vectors[5 : vector_params.shape[0]].reshape(planes, PLANE, hidden), spot, axis=1, keepdims=False
    ).reshape(1, inner)

    before, behind = move(pairs, PLANE), move(pairs, -PLANE)
    expand[0] = exchange(after(expand[0], pairs)).reshape(columns, inner // 2)
    output = grow(after(output, pairs), 4)
    cotangents = grow(after(cotangent, pairs), 2)
    queries, output, cotangents = tie(queries, output, cotangents)

    finish = jnp.cumsum(scene_lengths)
    begin = finish - scene_lengths
    base = (plane - 1) * shared
    position = plane * shared + jnp.arange(shared, dtype=jnp.int32)
    past = begin[None, :] <= position[:, None]
    span_begin = jnp.max(jnp.where(past, begin[None, :], 0), axis=1) - base
    span_end = jnp.min(jnp.where(finish[None, :] > position[:, None], finish[None, :], 1 << 30), axis=1) - base
    spans = jnp.stack([span_begin, span_end])
    bounds = jnp.stack([begin, finish]) - base
    bounds = jnp.pad(bounds, ((0, 0), (0, LANES - bounds.shape[1])))
    output = grow(output, 2)
    cotangents = grow(cotangents, 4)
    shrink_turns = {1: turn(after(shrink, queries), 1)}
    mixed_exact, mixed_low, logs = attention(spans, bounds, queries, before, pairs, behind)
    mixed_low, output, cotangents, expand[0], shrink_turns = tie(
        mixed_low, output, cotangents, expand[0], shrink_turns
    )

    mixed = exchange(mixed_low.reshape(PLANE, number, wide), plane_groups())
    output = [output, swap(output, 1)]
    cotangents = [cotangents, swap(cotangents, 1)]
    shrink_turns.update({s: turn(after(shrink, mixed_low), s) for s in range(2, planes)})
    output = ordered_output(device, planes, output)
    second, normed = kernel_call(
        functools.partial(mix_out_kernel, planes),
        [block_exact, block_like],
        mixed,
        tokens,
        vectors,
        *output,
        scalars=(place,),
        scratch=[square_scratch],
        flops=2 * number * columns * columns,
    )

    expand[1] = exchange(after(expand[1], mixed)).reshape(columns, inner // 2)
    sides = spread_sides(normed)
    sides, shrink_turns, cotangents = tie(sides, shrink_turns, cotangents)
    corner = spread_corner(*sides)
    shrink = [shrink] + [shrink_turns[s] for s in range(1, planes)]
    normed_all = spread_far(normed, sides, corner)

    inner_low = like((shared, inner), LOW)
    grad_near, grad_far, grad_corner, active, upper_grad, up_sums = kernel_call(
        functools.partial(feed_kernel, planes),
        [near_like, far_like, block_like, inner_low, inner_low, like((1, inner), F32)],
        *normed_all,
        *cotangents,
        *shrink,
        *expand,
        bias_up,
        scalars=(place,),
        scratch=[pltpu.VMEM((columns, inner), LOW), pltpu.VMEM((inner, columns), LOW), shared_scratch, shared_scratch],
        flops=6 * shared * columns * inner,
    )

    normed_grad = collect(grad_near, grad_far, grad_corner)
    shrink_grad = kernel_call(
        shrink_grad_kernel,
        [like((hidden, columns), LOW)] * planes,
        active,
        *cotangents,
        scalars=(place,),
        scratch=[pltpu.VMEM((inner, columns), F32), shared_scratch],
        flops=2 * shared * columns * inner,
    )
    shrink_turns = [turn(shrink_grad[s], s) for s in range(1, planes)]
    normed_grad, shrink_turns[:1] = tie(normed_grad, shrink_turns[:1])
    second_grad, branch_grad, mixed_grad, two_sums = kernel_call(
        functools.partial(norm_two_back_kernel, planes),
        [block_exact, block_like, like((PLANE, number, wide), LOW), like((3, columns), F32)],
        *normed_grad,
        second,
        cotangent,
        vectors,
        *output,
        scalars=(place,),
        scratch=[square_scratch],
        flops=2 * number * columns * columns,
    )

    mixed_grad = exchange(mixed_grad, plane_groups()).reshape(shared, wide)
    (expand_grad,) = kernel_call(
        expand_grad_kernel,
        [like((columns, inner), LOW)],
        after(upper_grad, branch_grad),
        *normed_all,
        scratch=[shared_scratch],
        flops=2 * shared * columns * inner,
    )
    branch_sides = spread_sides(branch_grad)
    mixed_grad, expand_grad, branch_sides, shrink_turns = tie(mixed_grad, expand_grad, branch_sides, shrink_turns)
    shrink_grad = sum(g.astype(F32) for g in [shrink_grad[0], *shrink_turns])

    expand_part = exchange(after(expand_grad, mixed_grad).reshape(n, rows, inner))
    branch_corner = spread_corner(*branch_sides)
    query_grad, before_grad, own_grad, behind_grad = attention_back(
        spans, bounds, queries, before, pairs, behind, mixed_exact, logs, mixed_grad
    )
    before_grad, behind_grad, branch_corner = tie(before_grad, behind_grad, branch_corner)

    from_after, from_before = move(before_grad, -PLANE), move(behind_grad, PLANE)
    branch = jnp.concatenate([branch_grad, *branch_sides, *branch_corner], axis=0)
    output_grad = kernel_call(
        output_grad_kernel,
        [like((2 * rows, columns), LOW)] * (planes // 2) if rows % 16 == 0 else [like((wide, columns), LOW)],
        mixed_low,
        branch,
        swap(branch, 1),
        scalars=(place,),
        scratch=[pltpu.VMEM((wide, columns), F32), pltpu.VMEM((shared, wide), LOW), shared_scratch],
        flops=2 * shared * columns * wide,
    )
    if len(output_grad) == 1:
        pairs_of = (plane >> 1) ^ jnp.arange(planes // 2)
        output_grad = jnp.take(output_grad[0].reshape(-1, 2 * rows, columns), pairs_of, axis=0, mode="clip")
    expand_grad, squares = sum_parts(hidden, rows, expand_part, jnp.zeros((1, 1), F32), place, others=[shrink_grad])
    from_after, from_before, output_grad, expand_grad, squares = tie(
        from_after, from_before, output_grad, expand_grad, squares
    )
    output_pairs = [
        lax.ppermute(
            output_grad[q],
            "seq",
            [(g * PLANE + j, j * planes + 2 * ((g >> 1) ^ q) + (g & 1)) for g in range(planes) for j in range(PLANE)],
        )
        for q in range(planes // 2)
    ]

    fused = rows % 16 == 0 and hidden == LANES
    attend_grad, first_near, first_far, first_corner, one_sums = kernel_call(
        functools.partial(first_back_kernel, planes),
        [
            like((n, 3 * rows + EXTRA, wide) if fused else (columns, 3 * wide), LOW),
            like((4, 2 * number, columns), F32),
            like((3, 2 * number, columns), LOW),
            like((2 * number, columns), LOW),
            like((2, columns), F32),
        ],
        own_grad,
        from_after,
        from_before,
        query_grad,
        first_low,
        units,
        attend,
        two_sums,
        up_sums,
        active,
        *shrink,
        scalars=(place,),
        scratch=[
            pltpu.VMEM((shared, 3 * wide), LOW),
            pltpu.VMEM((2 * EXTRA, columns), F32),
            pltpu.VMEM((inner, columns), LOW),
        ],
        flops=2 * shared * columns * 6 * wide,
    )
    more = vector_params.shape[0] - EXTRA
    attend_part = attend_grad
    if not fused:
        attend_part = with_vectors(attend_grad, one_sums, two_sums, up_sums, spot, n, rows, hidden)
    attend_part, first_near, first_far, first_corner, output_pairs = tie(
        attend_part, first_near, first_far, first_corner, output_pairs
    )
    both_cores = sum(g.astype(F32) for g in output_pairs)
    output_parts = [
        lax.dynamic_slice_in_dim(both_cores, rows * (device & 1), rows, axis=0),
        swap(lax.dynamic_slice_in_dim(both_cores, rows * (1 - (device & 1)), rows, axis=0).astype(LOW), 1),
    ]
    attend_part = exchange(attend_part)
    both = collect(first_near, first_far, first_corner)
    input_gradient, block_output = kernel_call(
        last_kernel, [block_like, block_like], *both, tokens, second_grad, second, vectors
    )
    attend_grad, squares, vector_grad, output_grad = sum_parts(
        wide, rows, attend_part, squares, place, device % in_lot, parts=output_parts
    )
    vector_grad = lax.dynamic_slice_in_dim(vector_grad, rows * (device % in_lot), rows, axis=1)
    vector_grad = vector_grad[: vector_params.shape[0]]
    squares, input_gradient, block_output = tie(exchange(squares), input_gradient, block_output)
    states = (
        (attend_weight, attend_momentum, attend_average),
        (output_weight, output_momentum, output_average),
        (expand_weight, expand_momentum, expand_average),
        (reduce_weight, reduce_momentum, reduce_average),
        (vector_params, vector_momentum, vector_average),
    )
    *updates, gradient_norm = kernel_call(
        update_kernel,
        [like(g[0].shape, F32) for g in states for _ in range(3)] + [like((1, 1), F32)],
        squares,
        *[a for g in states for a in g],
        attend_grad,
        output_grad,
        expand_grad,
        shrink_grad,
        vector_grad,
    )
    return (block_output, input_gradient, gradient_norm.reshape(()), *updates)


def solution(mesh):
    split, turned = P("seq", None), P(None, "seq")
    return jax.shard_map(
        on_device,
        mesh=mesh,
        in_specs=(split, P()) + (split,) * 5 + (turned,) + ((split,) * 4 + (turned,)) * 2,
        out_specs=(split, split, P()) + (split,) * 12 + (turned,) * 3,
        check_vma=False,
    )
```
